32 devices in a mesh: fsdp: 16 (over z, y, core), seq: 2 (over x).
Axes of the slice: x: 2, y: 2, z: 4, core: 2. Of those that a mesh axis runs over, the one named last changes fastest.
Arguments:
- tokens: bfloat16 [16, 1600, 1024], P('fsdp', 'seq'), may hold values from -6 to 6
- keep_mask: int32 [80, 256], P('fsdp'), may hold values from 0 to 1, as said below
- ln1_gain: bfloat16 [1024], P(('fsdp', 'seq')), may hold values from 0.5 to 1.5
- ln1_bias: bfloat16 [1024], P(('fsdp', 'seq')), may hold values from -2 to 2
- qkv_weight: bfloat16 [1024, 3072], P(('fsdp', 'seq')), may hold values from -0.1875 to 0.1875
- qv_bias: bfloat16 [2048], P(('fsdp', 'seq')), may hold values from -2 to 2
- proj_weight: bfloat16 [1024, 1024], P(('fsdp', 'seq')), may hold values from -0.75 to 0.75
- proj_bias: bfloat16 [1024], P(('fsdp', 'seq')), may hold values from -2 to 2
- ln2_gain: bfloat16 [1024], P(('fsdp', 'seq')), may hold values from 0.5 to 1.5
- ln2_bias: bfloat16 [1024], P(('fsdp', 'seq')), may hold values from -2 to 2
- fc1_weight: bfloat16 [1024, 4096], P(('fsdp', 'seq')), may hold values from -0.1875 to 0.1875
- fc1_bias: bfloat16 [4096], P(('fsdp', 'seq')), may hold values from -2 to 2
- fc2_weight: bfloat16 [4096, 1024], P(('fsdp', 'seq')), may hold values from -0.125 to 0.125
- fc2_bias: bfloat16 [1024], P(('fsdp', 'seq')), may hold values from -2 to 2
- cotangent: bfloat16 [16, 1600, 1024], P('fsdp', 'seq'), may hold values from -6 to 6
Outputs:
- layer_out: bfloat16 [16, 1600, 1024], P('fsdp', 'seq')
- tokens_grad: bfloat16 [16, 1600, 1024], P('fsdp', 'seq')
- ln1_gain_grad: float32 [1024], P(('fsdp', 'seq'))
- ln1_bias_grad: float32 [1024], P(('fsdp', 'seq'))
- qkv_weight_grad: float32 [1024, 3072], P(('fsdp', 'seq'))
- qv_bias_grad: float32 [2048], P(('fsdp', 'seq'))
- proj_weight_grad: float32 [1024, 1024], P(('fsdp', 'seq'))
- proj_bias_grad: float32 [1024], P(('fsdp', 'seq'))
- ln2_gain_grad: float32 [1024], P(('fsdp', 'seq'))
- ln2_bias_grad: float32 [1024], P(('fsdp', 'seq'))
- fc1_weight_grad: float32 [1024, 4096], P(('fsdp', 'seq'))
- fc1_bias_grad: float32 [4096], P(('fsdp', 'seq'))
- fc2_weight_grad: float32 [4096, 1024], P(('fsdp', 'seq'))
- fc2_bias_grad: float32 [1024], P(('fsdp', 'seq'))
The draws below stay inside these ranges and needn't reach their ends.
Inputs may be any that keep to these rules, and one draw needn't show every extreme that they name: `keep_mask`: 1 keeps a patch and 0 drops it; every image keeps at least 60 percent of its 256 patches; buffer tokens are always kept.
All inputs are finite; a program needn't handle non-finite values.
Results may differ from the reference program's by a relative error of at most 0.012.
Values may be sent and summed in bfloat16 or wider, within the bound.
A program may use at most 256 MiB of HBM per device.

```python
import jax
import jax.numpy as jnp
from jax import lax

D = 1024
HEADS = 16
HEAD_DIM = 64
FF = 4096
PATCHES = 256
BUF = 64
L = 320
SEQ_LEN = 1600
IMAGES = 80
SEQS = 16


def draw_keep_mask(key, part):
    count_key, order_key = jax.random.split(jax.random.fold_in(key, 7))
    least = (3 * PATCHES + 4) // 5
    counts = jax.random.randint(count_key, (IMAGES, 1), least, PATCHES + 1)
    order_keys = jax.random.split(order_key, IMAGES)
    ranks = jax.vmap(lambda single: jax.random.permutation(single, PATCHES))(order_keys)
    return (ranks < counts).astype(jnp.int32)


def spiked(result, stream_key, source, target, parts, factor):
    def block_of(dim):
        return (jnp.arange(result.shape[dim]) // (result.shape[dim] // parts)).reshape((-1,) + (1,) * (result.ndim - 1 - dim))

    one_side = jax.random.permutation(stream_key, parts)[block_of(target)]
    second = (block_of(target) + parts // 2) % parts
    return jnp.where((block_of(source) == one_side) | (block_of(source) == second), factor * result, result)


def shard_levels(own_key, extent, shards, low, largest):
    level, own = 1.0, jax.random.fold_in(own_key, 6)
    for axis_at, blocks in shards:
        steps = jnp.exp(jax.random.uniform(jax.random.fold_in(own, axis_at), (blocks,), jnp.float32, low / len(shards), largest / len(shards)))
        level = level * jnp.repeat(steps, extent[axis_at] // blocks).reshape([-1 if axis == axis_at else 1 for axis in range(len(extent))])
    return level


def gaussian(own_key, dims, spread, reach, cuts=(), held_as=jnp.bfloat16):
    level = shard_levels(own_key, dims, cuts, -0.22, 0.18) if cuts else 1.0
    result = jax.random.normal(own_key, dims, jnp.float32) * spread * level
    return jnp.minimum(jnp.maximum(result, -reach), reach).astype(held_as)


def heavy_noise(key, shape, scale, bound, cuts, heavy, kind=jnp.bfloat16):
    result = scale * jax.random.normal(key, shape, jnp.float32)
    if cuts:
        result = result * shard_levels(key, shape, cuts, -0.22, 0.18)
    return jnp.clip(spiked(result, jax.random.fold_in(key, 3), *heavy), -bound, bound).astype(kind)


def setup_inputs(seed: int = 0) -> dict:
    keys = jax.random.split(jax.random.key(seed), 16)
    return {
        "tokens": gaussian(keys[0], (SEQS, SEQ_LEN, D), 1.0, 6.0, ((0, 16), (1, 2))),
        "keep_mask": draw_keep_mask(jax.random.fold_in(keys[15], 71), 0),
        "ln1_gain": jnp.clip(1.0 + 0.1 * jax.random.normal(keys[2], (D,), jnp.float32), 0.5, 1.5).astype(jnp.bfloat16),
        "ln1_bias": gaussian(keys[3], (D,), 0.3, 2.0, ((0, 32),)),
        "qkv_weight": gaussian(keys[4], (D, 3 * D), D ** -0.5, 0.1875, ((0, 32),)),
        "qv_bias": gaussian(keys[5], (2 * D,), 0.3, 2.0, ((0, 32),)),
        "proj_weight": gaussian(keys[6], (D, D), (D // 16) ** -0.5, 0.75, ((0, 32),)),
        "proj_bias": gaussian(keys[7], (D,), 0.3, 2.0, ((0, 32),)),
        "ln2_gain": jnp.clip(1.0 + 0.1 * jax.random.normal(keys[8], (D,), jnp.float32), 0.5, 1.5).astype(jnp.bfloat16),
        "ln2_bias": gaussian(keys[9], (D,), 0.3, 2.0, ((0, 32),)),
        "fc1_weight": gaussian(keys[10], (D, FF), D ** -0.5, 0.1875, ((0, 32),)),
        "fc1_bias": gaussian(keys[11], (FF,), 0.3, 2.0, ((0, 32),)),
        "fc2_weight": gaussian(keys[12], (FF, D), (FF // 2) ** -0.5, 0.125, ((0, 32),)),
        "fc2_bias": gaussian(keys[13], (D,), 0.3, 2.0, ((0, 32),)),
        "cotangent": heavy_noise(keys[14], (SEQS, SEQ_LEN, D), 1.0, 6.0, ((0, 16), (1, 2)), (0, 2, 16, 2.0)),
    }


@jax.custom_vjp
def low(v):
    return lax.optimization_barrier(v.astype(jnp.bfloat16)).astype(jnp.float32)

@jax.custom_vjp
def low_back(v):
    return v

def low_keep(v):
    return (low(v), None)

def low_pass(kept, grad):
    return (grad,)

def back_keep(v):
    return (v, None)

def back_low(kept, grad):
    return (low(grad),)
low.defvjp(low_keep, low_pass)
low_back.defvjp(back_keep, back_low)

def layer_norm(value, gain, shift):
    mean = lax.optimization_barrier(jnp.mean(value, axis=-1, keepdims=True))
    centred = value - mean
    inverse = lax.rsqrt(lax.optimization_barrier(jnp.mean(centred * centred, axis=-1, keepdims=True)) + 1e-06)
    return centred * inverse * gain + shift

def layer(images, valid, params):
    ln1_gain, ln1_bias, qkv_weight, qv_bias, proj_weight, proj_bias, ln2_gain, ln2_bias, fc1_weight, fc1_bias, fc2_weight, fc2_bias = params
    highest = lax.Precision.HIGHEST
    count, length, width = images.shape
    normed = low(layer_norm(images, ln1_gain, ln1_bias))
    full_bias = jnp.concatenate([qv_bias[:width], jnp.zeros((width,), images.dtype), qv_bias[width:]])
    qkv = low(low_back(jnp.einsum('gtd,de->gte', normed, qkv_weight, precision=highest) + full_bias))
    qkv = qkv.reshape(count, length, 3, HEADS, HEAD_DIM)
    query, keyed, values = (qkv[:, :, 0], qkv[:, :, 1], qkv[:, :, 2])
    scores = low_back(jnp.einsum('gqhd,gkhd->ghqk', query, keyed, precision=highest) * HEAD_DIM ** (-0.5))
    scores = jnp.where(valid[:, None, None, :] > 0, scores, -1e+30)
    probs = low(jax.nn.softmax(scores, axis=-1))
    attn = jnp.einsum('ghqk,gkhd->gqhd', probs, values, precision=highest).reshape(count, length, width)
    attn = low(low_back(attn))
    resid = images + low_back(jnp.einsum('gtd,de->gte', attn, proj_weight, precision=highest)) + proj_bias
    normed2 = low(layer_norm(resid, ln2_gain, ln2_bias))
    hidden = low_back(jnp.einsum('gtd,df->gtf', normed2, fc1_weight, precision=highest)) + fc1_bias
    act = low(jax.nn.gelu(hidden, approximate=False))
    branch = low_back(jnp.einsum('gtf,fd->gtd', act, fc2_weight, precision=highest)) + fc2_bias
    return valid[:, :, None] * (resid + branch)

def reference(tokens, keep_mask, ln1_gain, ln1_bias, qkv_weight, qv_bias, proj_weight, proj_bias, ln2_gain, ln2_bias, fc1_weight, fc1_bias, fc2_weight, fc2_bias, cotangent):
    group = 8
    blocks = IMAGES // group
    valid = jnp.concatenate([jnp.ones((IMAGES, BUF), jnp.float32), keep_mask.astype(jnp.float32)], axis=1)
    params = tuple((p.astype(jnp.float32) for p in (ln1_gain, ln1_bias, qkv_weight, qv_bias, proj_weight, proj_bias, ln2_gain, ln2_bias, fc1_weight, fc1_bias, fc2_weight, fc2_bias)))
    images = tokens.astype(jnp.float32).reshape(IMAGES, L, D)
    valid_blocks = valid.reshape(blocks, group, L)
    checked = jax.checkpoint(layer)

    def whole(inputs, weights):

        def one(pair):
            return checked(pair[0], pair[1], weights)
        outputs = lax.map(one, (inputs.reshape(blocks, group, L, D), valid_blocks))
        return outputs.reshape(IMAGES, L, D)
    output, pull = jax.vjp(whole, images, params)
    grad_in, grads = pull(cotangent.astype(jnp.float32).reshape(IMAGES, L, D))
    layer_out = output.reshape(SEQS, SEQ_LEN, D).astype(jnp.bfloat16)
    tokens_grad = grad_in.reshape(SEQS, SEQ_LEN, D).astype(jnp.bfloat16)
    return (layer_out, tokens_grad, grads[0], grads[1], grads[2], grads[3], grads[4], grads[5], grads[6], grads[7], grads[8], grads[9], grads[10], grads[11])
```

```python
import functools
import math

import jax
import jax.numpy as jnp
from jax import lax
from jax.experimental import pallas as pl
from jax.experimental.pallas import tpu as pltpu
from jax.sharding import PartitionSpec as P

HEADS = 16
HEAD_DIM = 64
BUF = 64
L = 320
MESH = pl.DeviceIdType.MESH
BF = jnp.bfloat16
F32 = jnp.float32
LANES = 128
MIB = 2**20


def nn(a, b):
    return lax.dot_general(a, b, (((1,), (0,)), ((), ())), preferred_element_type=F32)


def nt(a, b):
    return lax.dot_general(a, b, (((1,), (1,)), ((), ())), preferred_element_type=F32)


def tn(a, b):
    return lax.dot_general(a, b, (((0,), (0,)), ((), ())), preferred_element_type=F32)


class Place:
    def __init__(self, nz, nx):
        f = lax.axis_index("fsdp")
        self.x = lax.axis_index("seq")
        self.nz, self.nx = nz, nx
        self.z = lax.div(f, 4)
        self.y = lax.rem(lax.div(f, 2), 2)
        self.c = lax.rem(f, 2)
        self.odd = lax.rem(self.x, 2)

    def at(self, z=None, y=None, c=None, x=None):
        z = self.z if z is None else z
        y = self.y if y is None else y
        c = self.c if c is None else c
        x = self.x if x is None else x
        return {"fsdp": (z * 2 + y) * 2 + c, "seq": x}

    def zs(self):
        return [lax.rem(self.z + d, self.nz) for d in range(1, self.nz)]

    def xs(self):
        return [lax.rem(self.x + d, self.nx) for d in range(1, self.nx)]

    def partner(self):
        return self.at(x=self.x + 1 - 2 * self.odd)

    def greet(self):
        peers = [self.at(z=z) for z in self.zs()] + [self.at(x=x) for x in self.xs()]
        peers += [self.at(y=1 - self.y), self.at(c=1 - self.c)]
        barrier = pltpu.get_barrier_semaphore()
        for peer in peers:
            pl.semaphore_signal(barrier, inc=1, device_id=peer, device_id_type=MESH)
        pl.semaphore_wait(barrier, len(peers))


class Sems:
    def __init__(self, send, recv):
        self.send, self.recv, self.used = send, recv, 0

    def copy(self, src, dst, device):
        slot = self.used
        self.used += 1
        return pltpu.make_async_remote_copy(
            src_ref=src,
            dst_ref=dst,
            send_sem=self.send.at[slot],
            recv_sem=self.recv.at[slot],
            device_id=device,
            device_id_type=MESH,
        )


def gather_copies(here, sems, src, buf, cols, early):
    lo, width = cols
    every = pl.ds(lo, width)
    a, b = pl.ds(lo, width // 2), pl.ds(lo + width // 2, width // 2)
    z, y, c, x = here.z, here.y, here.c, here.x
    if early:
        first = [sems.copy(src.at[:, every], buf.at[z, y, c, x, :, every], here.at(z=t)) for t in here.zs()]
        second = [sems.copy(buf.at[:, y, c, x, :, a], buf.at[:, y, c, x, :, a], here.at(x=t)) for t in here.xs()]
        second += [sems.copy(buf.at[:, y, c, x, :, b], buf.at[:, y, c, x, :, b], here.at(y=1 - y))]
    else:
        first = [sems.copy(src.at[:, a], buf.at[z, y, c, x, :, a], here.at(x=t)) for t in here.xs()]
        first += [sems.copy(src.at[:, b], buf.at[z, y, c, x, :, b], here.at(y=1 - y))]
        second = [sems.copy(buf.at[z, y, c, :, :, a], buf.at[z, y, c, :, :, a], here.at(z=t)) for t in here.zs()]
        second += [sems.copy(buf.at[z, :, c, x, :, b], buf.at[z, :, c, x, :, b], here.at(z=t)) for t in here.zs()]
    third = [sems.copy(buf.at[:, y, c, :, :, a], buf.at[:, y, c, :, :, a], here.at(y=1 - y))]
    third += [sems.copy(buf.at[:, :, c, x, :, b], buf.at[:, :, c, x, :, b], here.at(x=t)) for t in here.xs()]
    last = [sems.copy(buf.at[:, :, c, :, :, every], buf.at[:, :, c, :, :, every], here.at(c=1 - c))]
    return [first, second, third, last]


def small_copies(here, sems, src, buf):
    z, y, c, x = here.z, here.y, here.c, here.x
    first = [sems.copy(src, buf.at[z, y, c, x], here.at(z=t)) for t in here.zs()]
    second = [sems.copy(buf.at[:, y, c, x], buf.at[:, y, c, x], here.at(x=t)) for t in here.xs()]
    third = [sems.copy(buf.at[:, y, c], buf.at[:, y, c], here.at(y=1 - y))]
    last = [sems.copy(buf.at[:, :, c], buf.at[:, :, c], here.at(c=1 - c))]
    return [first, second, third, last]


def gather_count(nz, nx, early):
    if early:
        return (nz - 1) + (nx - 1) + 1 + 1 + (nx - 1) + 1
    return (nx - 1) + 1 + 2 * (nz - 1) + 1 + (nx - 1) + 1


def columns(buf, lo, width):
    part = buf[:, :, :, :, :, pl.ds(lo, width)]
    return part.reshape(-1, width)


def norm_stats(value):
    mean = jnp.mean(value, axis=-1, keepdims=True)
    centred = value - mean
    inverse = lax.rsqrt(jnp.mean(centred * centred, axis=-1, keepdims=True) + 1e-06)
    return centred * inverse, inverse


def gelu_pair(v):
    e = jnp.exp(v * v * (-0.5))
    t = pl.reciprocal(1.0 + (0.3275911 * math.sqrt(0.5)) * jnp.abs(v), approx=False)
    poly = 0.5 * 1.061405429
    for a in (-1.453152027, 1.421413741, -0.284496736, 0.254829592):
        poly = poly * t + 0.5 * a
    tail = poly * t * e
    cdf = jnp.where(v >= 0, 1.0 - tail, tail)
    return v * cdf, cdf + v * e * (1.0 / math.sqrt(2.0 * math.pi))


VECS = (("ln1g", 0, 1), ("ln1b", 1, 1), ("projb", 2, 1), ("ln2g", 3, 1), ("ln2b", 4, 1), ("fc2b", 5, 1), ("qvb", 6, 2), ("fc1b", 8, 4))
ROW = {name: i for i, (name, _, _) in enumerate(VECS)}
PACK = 12
PACK_ROWS = 16


def expand_vectors(small_buf, vec, count, width):
    unit = width // count
    total = PACK * unit
    pieces = small_buf[...].astype(F32).reshape(count, PACK_ROWS, total)
    pieces = jnp.sum(pieces, axis=1).astype(BF)
    for row, (_, start, times) in enumerate(VECS):
        per = unit * times
        shift = per.bit_length() - 1
        for lo in range(0, width * times, width):
            index = lax.broadcasted_iota(jnp.int32, (total, width), 1) + lo
            source = lax.broadcasted_iota(jnp.int32, (total, width), 0) - start * unit
            pick = ((index & (per - 1)) == source).astype(F32).astype(BF)
            spread = nn(pieces, pick)
            owner = lax.shift_right_logical(lax.broadcasted_iota(jnp.int32, (count, width), 1) + lo, shift)
            mine = owner == lax.broadcasted_iota(jnp.int32, (count, width), 0)
            vec[row : row + 1, lo : lo + width] = jnp.sum(jnp.where(mine, spread, 0.0), axis=0, keepdims=True)


class Sizes:
    def __init__(self, nz, nx, part, width, hidden):
        self.nz, self.nx, self.part, self.width, self.hidden = nz, nx, part, width, hidden
        self.count = nz * 4 * nx
        self.half = part % L
        self.frame = part + self.half
        self.whole = part // L
        self.rows = width // self.count

    def fits(self, sequences):
        paired = self.half * 2 == L and self.half % 32 == 0 and self.part % 32 == 0 and self.nx % 2 == 0
        return sequences == 1 and paired and self.rows % 32 == 0 and self.nz > 1 and self.hidden % self.width == 0


def forward_chunks(s):
    step = s.width
    out = [(0, i * step, step, True) for i in range(3)] + [(1, 0, step, True)]
    out += [(2, i * step, step, True) for i in range(s.hidden // step)]
    narrow = s.width * s.width // s.hidden
    out += [(3, i * narrow, narrow, True) for i in range(s.width // narrow)]
    return out


def forward_copies(s):
    total = sum(gather_count(s.nz, s.nx, early) for _, _, _, early in forward_chunks(s))
    return total + (s.nz - 1) + (s.nx - 1) + 1 + 1 + 1


def attend(s, k0, q0, row0, count, image, qkv, valid, attn, p_slot, p_out, p_sem):
    width = s.width
    low = lax.broadcasted_iota(jnp.int32, (1, LANES), 1) < HEAD_DIM
    zero = jnp.zeros((), BF)
    keep = valid[pl.ds(image, 1), :] > 0

    def out_copy(step, slot):
        return pltpu.make_async_copy(
            p_slot.at[slot, :, pl.ds(0, count), :],
            p_out.at[pl.ds(step * 4, 4), pl.ds(row0, count), :],
            p_sem.at[slot],
        )

    def body(step, carry):
        slot = lax.rem(step, 2)

        @pl.when(step >= 2)
        def _():
            out_copy(step - 2, slot).wait()

        for pair in range(2):
            col = pl.multiple_of((step * 2 + pair) * LANES, LANES)
            q2 = qkv[pl.ds(q0, count), pl.ds(col, LANES)]
            k2 = qkv[pl.ds(k0, L), pl.ds(col + width, LANES)]
            v2 = qkv[pl.ds(k0, L), pl.ds(col + 2 * width, LANES)]
            mixed = None
            for head in range(2):
                sel = low if head == 0 else jnp.logical_not(low)
                scores = nt(jnp.where(sel, q2, zero) * BF(HEAD_DIM**-0.5), k2)
                scores = jnp.where(keep, scores, -1e30)
                expo = jnp.exp(scores - jnp.max(scores, axis=-1, keepdims=True))
                probs = (expo * (1.0 / jnp.sum(expo, axis=-1, keepdims=True))).astype(BF)
                p_slot[slot, pair * 2 + head, pl.ds(0, count), :] = probs
                part = nn(probs, jnp.where(sel, v2, zero))
                mixed = part if mixed is None else mixed + part
            attn[pl.ds(row0, count), pl.ds(col, LANES)] = mixed.astype(BF)
        out_copy(step, slot).start()
        return carry

    lax.fori_loop(0, HEADS // 4, body, 0)
    for step in (HEADS // 4 - 2, HEADS // 4 - 1):
        out_copy(step, step % 2).wait()


def forward_kernel(
    s,
    x_ref,
    valid,
    own_valid,
    small_ref,
    wq_ref,
    wp_ref,
    w1_ref,
    w2_ref,
    out_ref,
    n1_out,
    qkv_out,
    attn_out,
    r1_out,
    n2_out,
    act_out,
    slope_out,
    p_out,
    wq_out,
    wp_out,
    w1_out,
    w2_out,
    vec_out,
    wq_buf,
    wp_buf,
    w1_buf,
    w2_buf,
    small_buf,
    vec,
    xf,
    n1f,
    qkvf,
    attn,
    r1,
    n2,
    act,
    slope,
    hidden,
    p_slot,
    send,
    recv,
    local_sem,
    save_sem,
    slope_sem,
    p_sem,
):
    here = Place(s.nz, s.nx)
    sems = Sems(send, recv)
    odd, width, part, half = here.odd, s.width, s.part, s.half
    off = pl.multiple_of(odd * half, 32)
    z, y, c, x = here.z, here.y, here.c, here.x
    srcs = (wq_ref, wp_ref, w1_ref, w2_ref)
    bufs = (wq_buf, wp_buf, w1_buf, w2_buf)
    outs = (wq_out, wp_out, w1_out, w2_out)

    own = [pltpu.make_async_copy(src, buf.at[z, y, c, x], local_sem.at[i]) for i, (src, buf) in enumerate(zip(srcs, bufs))]
    own.append(pltpu.make_async_copy(small_ref, small_buf.at[z, y, c, x], local_sem.at[4]))
    own.append(pltpu.make_async_copy(x_ref, xf.at[pl.ds(off, part), :], local_sem.at[5]))
    for copy in own:
        copy.start()

    chunks = forward_chunks(s)
    plans = [gather_copies(here, sems, srcs[w], bufs[w], (lo, n), early) for w, lo, n, early in chunks]
    small = small_copies(here, sems, small_ref, small_buf)
    plans[0] = [extra + base for base, extra in zip(plans[0], small)]
    edge_from = pl.multiple_of((part - half) * (1 - odd), 32)
    edge_to = pl.multiple_of(part * odd, 32)
    halo = sems.copy(x_ref.at[pl.ds(edge_from, half), :], xf.at[pl.ds(edge_to, half), :], here.partner())

    saves = []
    slots = iter(range(save_sem.shape[0]))

    def save(src, dst, listed=True):
        copy = pltpu.make_async_copy(src, dst, save_sem.at[next(slots)])
        copy.start()
        if listed:
            saves.append(copy)
        return copy

    here.greet()
    halo.start()
    last = len(chunks)

    def pump(k):
        for phase in (3, 2, 1):
            j = k - phase
            if 0 <= j < last:
                for copy in plans[j][phase - 1]:
                    copy.wait_recv()
                if k == 1 and phase == 1:
                    for copy in own:
                        copy.wait()
                for copy in plans[j][phase]:
                    copy.start()
        if k < last:
            for copy in plans[k][0]:
                copy.start()
        j = k - 4
        if 0 <= j < last:
            for copy in plans[j][3]:
                copy.wait_recv()
            w, lo, n, _ = chunks[j]
            save(bufs[w].at[:, :, :, :, :, pl.ds(lo, n)], outs[w].at[:, :, :, :, :, pl.ds(lo, n)])

    def norm_one():
        expand_vectors(small_buf, vec, s.count, width)
        save(vec, vec_out)
        halo.wait_recv()

        def body(i, carry):
            rows = pl.ds(pl.multiple_of(i * 32, 32), 32)
            unit, _ = norm_stats(xf[rows, :].astype(F32))
            n1f[rows, :] = (unit * vec[ROW["ln1g"] : ROW["ln1g"] + 1, :width] + vec[ROW["ln1b"] : ROW["ln1b"] + 1, :width]).astype(BF)
            return carry

        lax.fori_loop(0, s.frame // 32, body, 0)
        return save(n1f, n1_out, listed=False)

    def project(third):
        for lo in range(0, width, 512):
            got = nn(n1f[...], columns(wq_buf, third * width + lo, 512))
            if third != 1:
                start = (third // 2) * width + lo
                got = got + vec[ROW["qvb"] : ROW["qvb"] + 1, start : start + 512]
            qkvf[:, third * width + lo : third * width + lo + 512] = got.astype(BF)

    def whole_image(i):
        k0 = pl.multiple_of((i + odd) * L, 32)
        row0 = pl.multiple_of(i * L + odd * half, 32)
        attend(s, k0, k0, row0, L, i + odd, qkvf, valid, attn, p_slot, p_out, p_sem)

    def edge_image():
        k0 = pl.multiple_of(s.whole * L * (1 - odd), 32)
        q0 = pl.multiple_of(s.whole * L * (1 - odd) + half * odd, 32)
        row0 = pl.multiple_of(s.whole * L * (1 - odd), 32)
        attend(s, k0, q0, row0, half, s.whole * (1 - odd), qkvf, valid, attn, p_slot, p_out, p_sem)

    def output_projection():
        save(attn, attn_out)
        for lo in range(0, width, 512):
            got = nn(attn[...], columns(wp_buf, lo, 512)) + vec[ROW["projb"] : ROW["projb"] + 1, lo : lo + 512]
            r1[:, lo : lo + 512] = got + xf[pl.ds(off, part), lo : lo + 512].astype(F32)
        save(r1, r1_out)

        def body(i, carry):
            rows = pl.ds(pl.multiple_of(i * 32, 32), 32)
            unit, _ = norm_stats(r1[rows, :])
            n2[rows, :] = (unit * vec[ROW["ln2g"] : ROW["ln2g"] + 1, :width] + vec[ROW["ln2b"] : ROW["ln2b"] + 1, :width]).astype(BF)
            return carry

        lax.fori_loop(0, part // 32, body, 0)
        save(n2, n2_out)

    slope_copies = []

    def up(i):
        slot = i % 2
        if i >= 2:
            slope_copies[i - 2].wait()
        for lo in range(0, width, 512):
            at = i * width + lo
            hidden[...] = nn(n2[...], columns(w1_buf, at, 512)) + vec[ROW["fc1b"] : ROW["fc1b"] + 1, at : at + 512]

            def body(j, carry):
                rows = pl.ds(pl.multiple_of(j * 32, 32), 32)
                value, grade = gelu_pair(hidden[rows, :])
                act[rows, at : at + 512] = value.astype(BF)
                slope[slot, rows, lo : lo + 512] = grade.astype(BF)
                return carry

            lax.fori_loop(0, part // 32, body, 0)
        copy = pltpu.make_async_copy(slope.at[slot], slope_out.at[:, pl.ds(i * width, width)], slope_sem.at[slot])
        copy.start()
        slope_copies.append(copy)
        save(act.at[:, pl.ds(i * width, width)], act_out.at[:, pl.ds(i * width, width)])

    narrow = width * width // s.hidden
    result = n1f

    def down(i):
        lo = i * narrow
        branch = nn(act[...], columns(w2_buf, lo, narrow)) + vec[ROW["fc2b"] : ROW["fc2b"] + 1, lo : lo + narrow]
        result[pl.ds(0, part), lo : lo + narrow] = (own_valid[...] * (r1[:, lo : lo + narrow] + branch)).astype(BF)

    ups = s.hidden // width
    downs = width // narrow
    kept = {}

    def run(task):
        kind, i = task
        if kind == "norm":
            kept["n1"] = norm_one()
        elif kind == "qkv":
            project(i)
        elif kind == "image":
            whole_image(i)
        elif kind == "edge":
            edge_image()
        elif kind == "proj":
            save(qkvf, qkv_out)
            output_projection()
        elif kind == "up":
            up(i)
        elif kind == "down":
            if i == 0:
                kept["n1"].wait()
            down(i)

    tasks = {4: [("norm", 0), ("qkv", 0)], 5: [("qkv", 1)], 6: [("qkv", 2), ("image", 0)], 7: [("image", 1)], 8: [("edge", 0), ("proj", 0), ("up", 0)]}
    for i in range(1, ups):
        tasks.setdefault(8 + i, []).append(("up", i))
    for i in range(downs):
        tasks.setdefault(8 + ups + i, []).append(("down", i))
    for k in range(last + 4):
        pump(k)
        for task in tasks.get(k, []):
            run(task)

    final = pltpu.make_async_copy(result.at[pl.ds(0, part), :], out_ref, local_sem.at[0])
    final.start()
    for copy in slope_copies[-2:]:
        copy.wait()
    for copy in saves:
        copy.wait()
    halo.wait_send()
    for plan in plans:
        for phase in plan:
            for copy in phase:
                copy.wait_send()
    final.wait()


def forward_call(s, x, valid, own_valid, small, wq, wp, w1, w2):
    anyspace = pl.BlockSpec(memory_space=pl.ANY)
    vmem = pl.BlockSpec(memory_space=pltpu.VMEM)
    lead = (s.nz, 2, 2, s.nx)
    shape = lambda dims, kind=BF: jax.ShapeDtypeStruct(dims, kind)
    part, width, hidden, rows = s.part, s.width, s.hidden, s.rows
    fat = hidden // s.count
    gathered = [lead + (rows, 3 * width), lead + (rows, width), lead + (rows, hidden), lead + (fat, width)]
    outs = [
        shape((part, width)),
        shape((s.frame, width)),
        shape((s.frame, 3 * width)),
        shape((part, width)),
        shape((part, width), F32),
        shape((part, width)),
        shape((part, hidden)),
        shape((part, hidden)),
        shape((HEADS, part, L)),
        *[shape(dims) for dims in gathered],
        shape((8, hidden), F32),
    ]
    copies = forward_copies(s)
    scratch = [pltpu.VMEM(dims, BF) for dims in gathered]
    scratch += [
        pltpu.VMEM(lead + (PACK_ROWS, PACK * rows), BF),
        pltpu.VMEM((8, hidden), F32),
        pltpu.VMEM((s.frame, width), BF),
        pltpu.VMEM((s.frame, width), BF),
        pltpu.VMEM((s.frame, 3 * width), BF),
        pltpu.VMEM((part, width), BF),
        pltpu.VMEM((part, width), F32),
        pltpu.VMEM((part, width), BF),
        pltpu.VMEM((part, hidden), BF),
        pltpu.VMEM((2, part, width), BF),
        pltpu.VMEM((part, 512), F32),
        pltpu.VMEM((2, 4, L, L), BF),
        pltpu.SemaphoreType.DMA((copies,)),
        pltpu.SemaphoreType.DMA((copies,)),
        pltpu.SemaphoreType.DMA((6,)),
        pltpu.SemaphoreType.DMA((32,)),
        pltpu.SemaphoreType.DMA((2,)),
        pltpu.SemaphoreType.DMA((2,)),
    ]
    return pl.pallas_call(
        functools.partial(forward_kernel, s),
        out_shape=outs,
        in_specs=[anyspace, vmem, vmem, anyspace, anyspace, anyspace, anyspace, anyspace],
        out_specs=[anyspace] * len(outs),
        scratch_shapes=scratch,
        name="forward",
        compiler_params=pltpu.CompilerParams(collective_id=0, has_side_effects=True, vmem_limit_bytes=63 * MIB),
    )(x, valid, own_valid, small, wq, wp, w1, w2)


def frames(s, keep_mask):
    images = keep_mask.shape[0]
    x = lax.axis_index("seq")
    odd = lax.rem(x, 2)
    valid = jnp.concatenate([jnp.ones((images, BUF), F32), keep_mask.astype(F32)], axis=1)
    first = lax.div(x * s.part - odd * s.half, L)
    framed = lax.dynamic_slice_in_dim(valid, first, s.whole + 1, 0)
    framed = jnp.pad(framed, ((0, 8 - s.whole - 1), (0, 0)))
    own = lax.dynamic_slice_in_dim(valid.reshape(-1), x * s.part, s.part, 0).reshape(s.part, 1)
    return framed, own


def pack_small(s, ln1_gain, ln1_bias, proj_bias, ln2_gain, ln2_bias, fc2_bias, qv_bias, fc1_bias):
    row = jnp.concatenate([ln1_gain, ln1_bias, proj_bias, ln2_gain, ln2_bias, fc2_bias, qv_bias, fc1_bias])
    return jnp.pad(row[None, :], ((0, PACK_ROWS - 1), (0, 0)))


class Scatter:
    SLOTS = 3

    def __init__(self, s, here, sems, g, l0, l1a, l1b, l2a, l2b, s2, l3, fin, credit, fin_sem, total):
        self.s, self.here, self.sems, self.total = s, here, sems, total
        self.g, self.l0, self.l1a, self.l1b, self.l2a, self.l2b = g, l0, l1a, l1b, l2a, l2b
        self.s2, self.l3, self.fin, self.credit, self.fin_sem = s2, l3, fin, credit, fin_sem
        nx, nz = s.nx, s.nz
        z, y, c, x = here.z, here.y, here.c, here.x
        self.fore_x, self.fore_z = here.xs(), here.zs()
        self.back_x = [lax.rem(x + nx - d, nx) for d in range(1, nx)]
        self.back_z = [lax.rem(z + nz - d, nz) for d in range(1, nz)]
        self.base = {"c": 0, "1y": 1, "1x": 2, "2x": 1 + nx, "2y": 2 * nx, "z": 2 * nx + 1}
        self.sent = {}
        self.out = {}
        self.width = g.shape[-1]
        self.a, self.b = pl.ds(0, self.width // 2), pl.ds(self.width // 2, self.width // 2)

    @staticmethod
    def copies(s):
        return 1 + 1 + (s.nx - 1) + (s.nx - 1) + 1 + (s.nz - 1)

    def take(self, j, key, d=0):
        if j >= self.SLOTS:
            pl.semaphore_wait(self.credit.at[self.base[key] + d], 1)

    def give(self, j, key, device, d=0):
        if j + self.SLOTS < self.total:
            pl.semaphore_signal(self.credit.at[self.base[key] + d], inc=1, device_id=device, device_id_type=MESH)

    def launch(self, j, stage, copies):
        for copy in copies:
            copy.start()
        self.sent[(j, stage)] = copies

    def landed(self, j, stage):
        for copy in self.sent[(j, stage)]:
            copy.wait_recv()

    def left(self, j, stage):
        for copy in self.sent.pop((j, stage)):
            copy.wait_send()

    def free_g(self, j):
        if j >= 2:
            self.left(j - 2, 0)

    def stage0(self, j):
        here, c = self.here, self.here.c
        self.take(j, "c")
        src = self.g.at[j % 2, :, :, 1 - c]
        self.launch(j, 0, [self.sems.copy(src, self.l0.at[j % self.SLOTS], here.at(c=1 - c))])

    def stage1(self, j):
        here, l0, g = self.here, self.l0, self.g
        y, c, x, t, u = here.y, here.c, here.x, j % self.SLOTS, j % 2
        self.landed(j, 0)

        def body(zz, carry):
            for yy in range(2):
                for xx in range(self.s.nx):
                    l0[t, zz, yy, xx] = l0[t, zz, yy, xx] + g[u, zz, yy, c, xx]
            return carry

        lax.fori_loop(0, self.s.nz, body, 0)
        copies = []
        self.take(j, "1y")
        copies.append(self.sems.copy(l0.at[t, :, 1 - y, :, :, self.a], self.l1a.at[t], here.at(y=1 - y)))
        for d, peer in enumerate(self.fore_x):
            self.take(j, "1x", d)
            copies.append(self.sems.copy(l0.at[t, :, :, peer, :, self.b], self.l1b.at[t, d], here.at(x=peer)))
        self.launch(j, 1, copies)

    def stage2(self, j):
        here, l0, l1a, l1b = self.here, self.l0, self.l1a, self.l1b
        y, c, x, t = here.y, here.c, here.x, j % self.SLOTS
        self.landed(j, 1)

        def body(zz, carry):
            for xx in range(self.s.nx):
                l1a[t, zz, xx] = l1a[t, zz, xx] + l0[t, zz, y, xx, :, self.a]
            for yy in range(2):
                got = l0[t, zz, yy, x, :, self.b].astype(F32)
                for d in range(self.s.nx - 1):
                    got = got + l1b[t, d, zz, yy].astype(F32)
                l1b[t, 0, zz, yy] = got.astype(BF)
            return carry

        lax.fori_loop(0, self.s.nz, body, 0)
        copies = []
        for d, peer in enumerate(self.fore_x):
            self.take(j, "2x", d)
            copies.append(self.sems.copy(l1a.at[t, :, peer], self.l2a.at[t, d], here.at(x=peer)))
        self.take(j, "2y")
        copies.append(self.sems.copy(l1b.at[t, 0, :, 1 - y], self.l2b.at[t], here.at(y=1 - y)))
        self.launch(j, 2, copies)
        self.left(j, 1)
        self.give(j, "c", here.at(c=1 - c))

    def stage3(self, j):
        here, l1a, l1b, l2a, l2b, s2 = self.here, self.l1a, self.l1b, self.l2a, self.l2b, self.s2
        y, x, t = here.y, here.x, j % self.SLOTS
        self.landed(j, 2)

        def body(zz, carry):
            got = l1a[t, zz, x].astype(F32)
            for d in range(self.s.nx - 1):
                got = got + l2a[t, d, zz].astype(F32)
            s2[t, zz, :, self.a] = got.astype(BF)
            s2[t, zz, :, self.b] = l2b[t, zz] + l1b[t, 0, zz, y]
            return carry

        lax.fori_loop(0, self.s.nz, body, 0)
        copies = []
        for d, peer in enumerate(self.fore_z):
            self.take(j, "z", d)
            copies.append(self.sems.copy(s2.at[t, peer], self.l3.at[t, d], here.at(z=peer)))
        self.launch(j, 3, copies)
        self.left(j, 2)
        self.give(j, "1y", here.at(y=1 - y))
        self.give(j, "2y", here.at(y=1 - y))
        for d, peer in enumerate(self.back_x):
            self.give(j, "1x", here.at(x=peer), d)
            self.give(j, "2x", here.at(x=peer), d)

    def stage4(self, j, targets):
        here, s2, l3, fin = self.here, self.s2, self.l3, self.fin
        t, u = j % self.SLOTS, j % 2
        self.landed(j, 3)
        for copy in self.out.pop(j - 2, []):
            copy.wait()
        got = s2[t, here.z].astype(F32)
        for d in range(self.s.nz - 1):
            got = got + l3[t, d].astype(F32)
        fin[u] = got
        self.left(j, 3)
        for d, peer in enumerate(self.back_z):
            self.give(j, "z", here.at(z=peer), d)
        copies = [pltpu.make_async_copy(src, dst, self.fin_sem.at[u, i]) for i, (src, dst) in enumerate(targets(fin.at[u]))]
        for copy in copies:
            copy.start()
        self.out[j] = copies

    def finish(self):
        for copies in self.out.values():
            for copy in copies:
                copy.wait()
        for j, stage in sorted(self.sent):
            self.left(j, stage)


def small_scatter_copies(s):
    return 1 + (s.nx - 1) + 1 + (s.nz - 1)


class SmallScatter:
    def __init__(self, s, here, sems, whole, m0, m1, m2, m3):
        self.s, self.here, self.sems = s, here, sems
        self.whole, self.m0, self.m1, self.m2, self.m3 = whole, m0, m1, m2, m3
        self.sent = {}

    def launch(self, stage, copies):
        for copy in copies:
            copy.start()
        self.sent[stage] = copies

    def landed(self, stage):
        for copy in self.sent[stage]:
            copy.wait_recv()

    def stage(self, n, out=None):
        here, s = self.here, self.s
        z, y, c, x = here.z, here.y, here.c, here.x
        whole, m0, m1, m2, m3 = self.whole, self.m0, self.m1, self.m2, self.m3
        if n == 0:
            self.launch(0, [self.sems.copy(whole.at[:, :, 1 - c], m0, here.at(c=1 - c))])
        elif n == 1:
            self.landed(0)
            for zz in range(s.nz):
                for yy in range(2):
                    for xx in range(s.nx):
                        m0[zz, yy, xx] = m0[zz, yy, xx] + whole[zz, yy, c, xx]
            self.launch(1, [self.sems.copy(m0.at[:, :, p], m1.at[d], here.at(x=p)) for d, p in enumerate(here.xs())])
        elif n == 2:
            self.landed(1)
            for zz in range(s.nz):
                for yy in range(2):
                    got = m0[zz, yy, x]
                    for d in range(s.nx - 1):
                        got = got + m1[d, zz, yy]
                    m1[0, zz, yy] = got
            self.launch(2, [self.sems.copy(m1.at[0, :, 1 - y], m2, here.at(y=1 - y))])
        elif n == 3:
            self.landed(2)
            for zz in range(s.nz):
                m2[zz] = m2[zz] + m1[0, zz, y]
            self.launch(3, [self.sems.copy(m2.at[p], m3.at[d], here.at(z=p)) for d, p in enumerate(here.zs())])
        else:
            self.landed(3)
            got = m2[z]
            for d in range(s.nz - 1):
                got = got + m3[d]
            out[...] = got

    def finish(self):
        for copies in self.sent.values():
            for copy in copies:
                copy.wait_send()


def pack_vectors(vec, packed, s):
    unit = s.width // s.count
    total = PACK * unit
    acc = jnp.zeros((s.count, total), F32)
    for row, (_, start, times) in enumerate(VECS):
        per = unit * times
        shift = per.bit_length() - 1
        for lo in range(0, s.width * times, s.width):
            index = lax.broadcasted_iota(jnp.int32, (s.width, total), 0) + lo
            target = lax.broadcasted_iota(jnp.int32, (s.width, total), 1) - start * unit
            pick = ((index & (per - 1)) == target).astype(F32)
            owner = lax.shift_right_logical(lax.broadcasted_iota(jnp.int32, (s.count, s.width), 1) + lo, shift)
            mine = owner == lax.broadcasted_iota(jnp.int32, (s.count, s.width), 0)
            spread = jnp.where(mine, vec[row : row + 1, lo : lo + s.width], 0.0)
            acc = acc + lax.dot_general(
                spread, pick, (((1,), (0,)), ((), ())), precision=lax.Precision.HIGHEST, preferred_element_type=F32
            )
    packed[...] = jnp.broadcast_to(acc[:, None, :], (s.count, 8, total)).reshape(s.nz, 2, 2, s.nx, 8, total)


def attend_back(s, k0, q0, row0, count, qkv, grad_out, dqkv, p_slot, p_in, p_sem):
    width, frame = s.width, s.frame
    low = lax.broadcasted_iota(jnp.int32, (1, LANES), 1) < HEAD_DIM
    zero = jnp.zeros((), BF)
    steps = HEADS // 4

    def in_copy(step, slot):
        return pltpu.make_async_copy(
            p_in.at[pl.ds(step * 4, 4), pl.ds(row0, count), :],
            p_slot.at[slot, :, pl.ds(0, count), :],
            p_sem.at[slot],
        )

    in_copy(0, 0).start()

    def body(step, carry):
        slot = lax.rem(step, 2)

        @pl.when(step + 1 < steps)
        def _():
            in_copy(step + 1, 1 - slot).start()

        in_copy(step, slot).wait()
        for pair in range(2):
            col = pl.multiple_of((step * 2 + pair) * LANES, LANES)
            q2 = qkv[pl.ds(q0, count), pl.ds(col, LANES)]
            k2 = qkv[pl.ds(frame + k0, L), pl.ds(col, LANES)]
            v2 = qkv[pl.ds(2 * frame + k0, L), pl.ds(col, LANES)]
            g2 = grad_out[pl.ds(row0, count), pl.ds(col, LANES)]
            dq = dk = dv = None
            for head in range(2):
                sel = low if head == 0 else jnp.logical_not(low)
                probs = p_slot[slot, pair * 2 + head, pl.ds(0, count), :]
                grad = jnp.where(sel, g2, zero)
                dprobs = nt(grad, v2)
                wide = probs.astype(F32)
                rowdot = jnp.sum(dprobs * wide, axis=-1, keepdims=True)
                dscores = (wide * (dprobs - rowdot)).astype(BF)
                more = (nn(dscores, jnp.where(sel, k2, zero)), tn(dscores, jnp.where(sel, q2, zero)), tn(probs, grad))
                dq, dk, dv = more if dq is None else (dq + more[0], dk + more[1], dv + more[2])
            scale = HEAD_DIM**-0.5
            dqkv[pl.ds(q0, count), pl.ds(col, LANES)] = (dq * scale).astype(BF)
            dqkv[pl.ds(k0, L), pl.ds(col + width, LANES)] = (dk * scale).astype(BF)
            dqkv[pl.ds(k0, L), pl.ds(col + 2 * width, LANES)] = dv.astype(BF)
        return carry

    lax.fori_loop(0, steps, body, 0)


def fold_rows(value):
    return jnp.sum(value.reshape(-1, 8, value.shape[-1]), axis=0)


CHUNK = 1024


def backward_chunks(s):
    out = [(3, i) for i in range(s.width * (s.hidden // s.width) // CHUNK)]
    out += [(2, i) for i in range(s.hidden // CHUNK)]
    out += [(1, i) for i in range(s.width // CHUNK)]
    out += [(0, i) for i in range(3 * s.width // CHUNK)]
    return out


def backward_copies(s):
    return Scatter.copies(s) * len(backward_chunks(s)) + small_scatter_copies(s) + 1


def backward_kernel(
    s,
    x_ref,
    own_valid,
    cot_ref,
    n1_ref,
    qkv_ref,
    attn_ref,
    r1_ref,
    n2_ref,
    act_ref,
    slope_ref,
    p_ref,
    wq_ref,
    wp_ref,
    w1_ref,
    w2_ref,
    vec,
    out_ref,
    dwq_out,
    dwp_out,
    dw1_out,
    dw2_out,
    small_out,
    buf_a,
    buf_b,
    tall,
    broad,
    wide_a,
    wide_b,
    grad_b,
    mid,
    attn,
    n1f,
    p_slot,
    edge_send,
    edge_in,
    sums,
    packed,
    m0,
    m1,
    m2,
    m3,
    small_fin,
    g,
    l0,
    l1a,
    l1b,
    l2a,
    l2b,
    s2,
    l3,
    fin,
    send,
    recv,
    load_sem,
    p_sem,
    fin_sem,
    credit,
):
    here = Place(s.nz, s.nx)
    sems = Sems(send, recv)
    odd, width, part, half, frame, hidden = here.odd, s.width, s.part, s.half, s.frame, s.hidden
    off = pl.multiple_of(odd * half, 32)
    slots = iter(range(load_sem.shape[0]))

    def load(src, dst):
        copy = pltpu.make_async_copy(src, dst, load_sem.at[next(slots)])
        copy.start()
        return copy

    cot_load = load(cot_ref, grad_b)
    act_load = load(act_ref, buf_a.at[pl.ds(0, part), :])
    w2_load = load(w2_ref, tall)
    slope_load = load(slope_ref, buf_b)
    n2_load = load(n2_ref, mid)
    w1_load = load(w1_ref, broad)
    r1_load = load(r1_ref, wide_a.at[pl.ds(0, part), :])
    attn_load = load(attn_ref, attn)
    pending = {}

    chunks = backward_chunks(s)
    total = len(chunks)
    scatter = Scatter(s, here, sems, g, l0, l1a, l1b, l2a, l2b, s2, l3, fin, credit, fin_sem, total)
    small = SmallScatter(s, here, sems, packed, m0, m1, m2, m3)
    here.greet()

    def name(key, value, times=1):
        sums[ROW[key] : ROW[key] + 1, : width * times] = value

    def prepare():
        cot_load.wait()

        def body(i, carry):
            rows = pl.ds(pl.multiple_of(i * 32, 32), 32)
            grad_b[rows, :] = (grad_b[rows, :].astype(F32) * own_valid[rows, :]).astype(BF)
            return carry

        lax.fori_loop(0, part // 32, body, 0)
        act_load.wait()

    ratio = hidden // width
    narrow = CHUNK // ratio
    deep = hidden // s.nz

    def down_grad(i, slot):
        def body(zz, carry):
            rows = pl.ds(pl.multiple_of(zz * deep, deep), deep)
            got = tn(buf_a[pl.ds(0, part), rows], grad_b[:, i * narrow : (i + 1) * narrow]).astype(BF)
            got = got.reshape(2, 2, s.nx, ratio, s.rows, narrow)
            for q in range(ratio):
                g[slot, zz, :, :, :, :, q * narrow : (q + 1) * narrow] = got[:, :, :, q]
            return carry

        lax.fori_loop(0, s.nz, body, 0)

    def grad_tile(lhs, rhs, slot):
        for lo in range(0, CHUNK, 512):
            got = tn(lhs, rhs(lo)).astype(BF)
            g[slot, :, :, :, :, :, lo : lo + 512] = got.reshape(s.nz, 2, 2, s.nx, s.rows, 512)

    def hidden_grad(i):
        for lo in range(i * width, (i + 1) * width, 512):
            wide_b[:, :512] = nt(grad_b[...], tall[lo : lo + 512, :])

            def body(j, carry):
                rows = pl.ds(pl.multiple_of(j * 32, 32), 32)
                got = wide_b[rows, :512] * buf_b[rows, lo : lo + 512].astype(F32)
                buf_b[rows, lo : lo + 512] = got.astype(BF)
                return carry + fold_rows(got)

            folded = lax.fori_loop(0, part // 32, body, jnp.zeros((8, 512), F32))
            sums[ROW["fc1b"] : ROW["fc1b"] + 1, lo : lo + 512] = jnp.sum(folded, axis=0, keepdims=True)

    def second_norm_product(lo):
        wide_b[:, lo : lo + 256] = nt(buf_b[...], broad[lo : lo + 256, :])

    def second_norm_back():
        ones = jnp.ones((8, part), BF)
        name("fc2b", nn(ones, grad_b[...])[0:1])
        gain = vec[ROW["ln2g"] : ROW["ln2g"] + 1, :width]

        def body(i, carry):
            rows = pl.ds(pl.multiple_of(i * 32, 32), 32)
            unit, inverse = norm_stats(wide_a[rows, :])
            got = wide_b[rows, :]
            u = got * gain
            back = u - jnp.mean(u, axis=-1, keepdims=True) - unit * jnp.mean(u * unit, axis=-1, keepdims=True)
            back = grad_b[rows, :].astype(F32) + inverse * back
            wide_b[rows, :] = back
            n1f[rows, :] = back.astype(BF)
            return carry[0] + fold_rows(got * unit), carry[1] + fold_rows(got), carry[2] + fold_rows(back)

        zeros = jnp.zeros((8, width), F32)
        gain_sum, shift_sum, bias_sum = lax.fori_loop(0, part // 32, body, (zeros, zeros, zeros))
        name("ln2g", jnp.sum(gain_sum, axis=0, keepdims=True))
        name("ln2b", jnp.sum(shift_sum, axis=0, keepdims=True))
        name("projb", jnp.sum(bias_sum, axis=0, keepdims=True))

    def attention_grad():
        for lo in range(0, width, 512):
            grad_b[:, lo : lo + 512] = nt(n1f[:part, :], tall[3 * frame + lo : 3 * frame + lo + 512, :]).astype(BF)

    def first_norm_product(lo):
        got = nt(buf_a[:, : 3 * width], broad[lo : lo + 256, : 3 * width])
        wide_a[:, lo : lo + 256] = got

    def first_norm_back():
        gain = vec[ROW["ln1g"] : ROW["ln1g"] + 1, :width]

        def body(i, carry):
            rows = pl.ds(pl.multiple_of(i * 32, 32), 32)
            framed = pl.ds(pl.multiple_of(i * 32 + off, 32), 32)
            unit, inverse = norm_stats(attn[rows, :].astype(F32))
            got = wide_a[framed, :]
            u = got * gain
            back = u - jnp.mean(u, axis=-1, keepdims=True) - unit * jnp.mean(u * unit, axis=-1, keepdims=True)
            mid[rows, :] = (wide_b[rows, :] + inverse * back).astype(BF)
            return carry[0] + fold_rows(got * unit), carry[1] + fold_rows(got)

        zeros = jnp.zeros((8, width), F32)
        gain_sum, shift_sum = lax.fori_loop(0, part // 32, body, (zeros, zeros))
        name("ln1g", jnp.sum(gain_sum, axis=0, keepdims=True))
        name("ln1b", jnp.sum(shift_sum, axis=0, keepdims=True))

    far = pl.multiple_of(part * (1 - odd), 32)
    near = pl.multiple_of((part - half) * (1 - odd) + half * odd, 32)
    edge = sems.copy(edge_send, edge_in, here.partner())

    def send_edge():
        edge_send[...] = wide_a[pl.ds(far, half), :].astype(BF)
        edge.start()

    def take_edge():
        edge.wait_recv()
        wide_a[pl.ds(near, half), :] = wide_a[pl.ds(near, half), :] + edge_in[...].astype(F32)

    def bias_grad():
        ones = jnp.ones((8, frame), BF)
        for third in (0, 2):
            got = nn(ones, buf_a[:, third * width : (third + 1) * width])[0:1]
            sums[ROW["qvb"] : ROW["qvb"] + 1, (third // 2) * width : (third // 2 + 1) * width] = got

    def run(task, slot):
        kind, i = task
        if kind == "prepare":
            prepare()
        elif kind == "down":
            down_grad(i, slot)
        elif kind == "hidden":
            if i == 0:
                w2_load.wait()
                slope_load.wait()
            hidden_grad(i)
            if i == ratio - 1:
                pending["wp"] = load(wp_ref, tall.at[pl.ds(3 * frame, width), :])
                pending["qkv"] = [load(qkv_ref.at[:, pl.ds(t * width, width)], tall.at[pl.ds(t * frame, frame), :]) for t in range(3)]
        elif kind == "up":
            if i == 0:
                n2_load.wait()
            grad_tile(mid[...], lambda lo: buf_b[:, i * CHUNK + lo : i * CHUNK + lo + 512], slot)
        elif kind == "ln2":
            if i == 0:
                w1_load.wait()
            second_norm_product(i * 512)
            second_norm_product(i * 512 + 256)
            if i == width // 512 - 1:
                pending["wq"] = load(wq_ref, broad.at[:, pl.ds(0, 3 * width)])
        elif kind == "mid":
            r1_load.wait()
            second_norm_back()
        elif kind == "proj":
            attn_load.wait()
            grad_tile(attn[...], lambda lo: n1f[:part, i * CHUNK + lo : i * CHUNK + lo + 512], slot)
            if i == width // CHUNK - 1:
                pending["x"] = load(x_ref, attn)
                pending["n1"] = load(n1_ref, n1f)
        elif kind == "gattn":
            pending["wp"].wait()
            attention_grad()
            for copy in pending["qkv"]:
                copy.wait()
            buf_a[pl.ds(far, half), :width] = jnp.zeros((half, width), BF)
        elif kind == "image":
            k0 = pl.multiple_of((i + odd) * L, 32)
            row0 = pl.multiple_of(i * L + odd * half, 32)
            attend_back(s, k0, k0, row0, L, tall, grad_b, buf_a, p_slot, p_ref, p_sem)
        elif kind == "edge":
            k0 = pl.multiple_of(s.whole * L * (1 - odd), 32)
            q0 = pl.multiple_of(s.whole * L * (1 - odd) + half * odd, 32)
            attend_back(s, k0, q0, k0, half, tall, grad_b, buf_a, p_slot, p_ref, p_sem)
        elif kind == "qkv":
            if i == 0:
                pending["n1"].wait()
            grad_tile(n1f[...], lambda lo: buf_a[:, i * CHUNK + lo : i * CHUNK + lo + 512], slot)
        elif kind == "ln1":
            pending["wq"].wait()
            for lo in range(0, width, 256):
                first_norm_product(lo)
            send_edge()
            bias_grad()
        elif kind == "first":
            take_edge()
            pending["x"].wait()
            first_norm_back()
            pending["out"] = load(mid, out_ref)
            pack_vectors(sums, packed, s)
            small.stage(0)

    before = {}
    after = {}
    for k, (w, i) in enumerate(chunks):
        before[k] = [({3: "down", 2: "up", 1: "proj", 0: "qkv"}[w], i)]
    before[0].insert(0, ("prepare", 0))
    downs = s.width * ratio // CHUNK
    for i in range(ratio):
        after.setdefault(i, []).append(("hidden", i))
    ups = hidden // CHUNK
    for i in range(width // 512):
        after.setdefault(downs + i, []).append(("ln2", i))
    after.setdefault(downs + width // 512 - 1, []).append(("mid", 0))
    after.setdefault(downs + width // 512 - 1, []).append(("gattn", 0))
    for i in range(s.whole):
        after.setdefault(downs + width // 512 + i, []).append(("image", i))
    after.setdefault(downs + ups, []).append(("edge", 0))
    done = total - 1
    after.setdefault(done, []).extend([("ln1", 0), ("first", 0)])

    outs = (dwq_out, dwp_out, dw1_out, dw2_out)

    def targets(j):
        w, i = chunks[j]

        def pairs(slot):
            if w == 3:
                return [
                    (slot.at[:, pl.ds(q * narrow, narrow)], outs[3].at[pl.ds(q * s.rows, s.rows), pl.ds(i * narrow, narrow)])
                    for q in range(ratio)
                ]
            return [(slot, outs[w].at[:, pl.ds(i * CHUNK, CHUNK)])]

        return pairs

    for k in range(total + 5):
        if k < total:
            scatter.free_g(k)
            for task in before.get(k, []):
                run(task, k % 2)
        if 0 <= k - 4 < total:
            scatter.stage4(k - 4, targets(k - 4))
        if 0 <= k - 3 < total:
            scatter.stage3(k - 3)
        if 0 <= k - 2 < total:
            scatter.stage2(k - 2)
        if 0 <= k - 1 < total:
            scatter.stage1(k - 1)
        if k < total:
            scatter.stage0(k)
        if k > done:
            small.stage(min(k - done, 4), small_fin) if k - done <= 4 else None
        for task in after.get(k, []):
            run(task, None)
    final = pltpu.make_async_copy(small_fin, small_out, p_sem.at[0])
    final.start()
    scatter.finish()
    small.finish()
    edge.wait_send()
    pending["out"].wait()
    final.wait()


def backward_call(s, x, own_valid, cot, n1f, qkvf, attn, r1, n2, act, slope, p, wq, wp, w1, w2, vec):
    anyspace = pl.BlockSpec(memory_space=pl.ANY)
    vmem = pl.BlockSpec(memory_space=pltpu.VMEM)
    shape = lambda dims, kind=F32: jax.ShapeDtypeStruct(dims, kind)
    part, width, hidden, rows, nz, nx, frame = s.part, s.width, s.hidden, s.rows, s.nz, s.nx, s.frame
    total = PACK * rows
    outs = [
        shape((part, width), BF),
        shape((rows, 3 * width)),
        shape((rows, width)),
        shape((rows, hidden)),
        shape((hidden // s.count, width)),
        shape((8, total)),
    ]
    copies = backward_copies(s)
    ring = Scatter.SLOTS
    scratch = [
        pltpu.VMEM((frame, hidden), BF),
        pltpu.VMEM((part, hidden), BF),
        pltpu.VMEM((hidden, width), BF),
        pltpu.VMEM((width, hidden), BF),
        pltpu.VMEM((frame, width), F32),
        pltpu.VMEM((part, width), F32),
        pltpu.VMEM((part, width), BF),
        pltpu.VMEM((part, width), BF),
        pltpu.VMEM((part, width), BF),
        pltpu.VMEM((frame, width), BF),
        pltpu.VMEM((2, 4, L, L), BF),
        pltpu.VMEM((s.half, width), BF),
        pltpu.VMEM((s.half, width), BF),
        pltpu.VMEM((8, hidden), F32),
        pltpu.VMEM((nz, 2, 2, nx, 8, total), F32),
        pltpu.VMEM((nz, 2, nx, 8, total), F32),
        pltpu.VMEM((nx - 1, nz, 2, 8, total), F32),
        pltpu.VMEM((nz, 8, total), F32),
        pltpu.VMEM((nz - 1, 8, total), F32),
        pltpu.VMEM((8, total), F32),
        pltpu.VMEM((2, nz, 2, 2, nx, rows, CHUNK), BF),
        pltpu.VMEM((ring, nz, 2, nx, rows, CHUNK), BF),
        pltpu.VMEM((ring, nz, nx, rows, CHUNK // 2), BF),
        pltpu.VMEM((ring, nx - 1, nz, 2, rows, CHUNK // 2), BF),
        pltpu.VMEM((ring, nx - 1, nz, rows, CHUNK // 2), BF),
        pltpu.VMEM((ring, nz, rows, CHUNK // 2), BF),
        pltpu.VMEM((ring, nz, rows, CHUNK), BF),
        pltpu.VMEM((ring, nz - 1, rows, CHUNK), BF),
        pltpu.VMEM((2, rows, CHUNK), F32),
        pltpu.SemaphoreType.DMA((copies,)),
        pltpu.SemaphoreType.DMA((copies,)),
        pltpu.SemaphoreType.DMA((24,)),
        pltpu.SemaphoreType.DMA((2,)),
        pltpu.SemaphoreType.DMA((2, hidden // width)),
        pltpu.SemaphoreType.REGULAR((2 * nx + nz,)),
    ]
    return pl.pallas_call(
        functools.partial(backward_kernel, s),
        out_shape=outs,
        in_specs=[anyspace, vmem] + [anyspace] * 13 + [vmem],
        out_specs=[anyspace] * len(outs),
        scratch_shapes=scratch,
        name="backward",
        compiler_params=pltpu.CompilerParams(collective_id=1, has_side_effects=True, vmem_limit_bytes=63 * MIB),
    )(x, own_valid, cot, n1f, qkvf, attn, r1, n2, act, slope, p, wq, wp, w1, w2, vec)


def layer_norm(value, gain, shift):
    mean = jnp.mean(value, axis=-1, keepdims=True)
    centred = value - mean
    inverse = lax.rsqrt(jnp.mean(centred * centred, axis=-1, keepdims=True) + 1e-06)
    unit = centred * inverse
    return (unit * gain + shift, unit, inverse)


def norm_back(grad_out, unit, inverse, gain):
    scaled = grad_out * gain
    grad_in = inverse * (
        scaled
        - jnp.mean(scaled, axis=-1, keepdims=True)
        - unit * jnp.mean(scaled * unit, axis=-1, keepdims=True)
    )
    return (grad_in, jnp.sum(grad_out * unit, axis=0), jnp.sum(grad_out, axis=0))


def split_heads(block, head_count):
    return block.reshape(block.shape[0], block.shape[1], head_count, -1)


def masked_scores(query, keyed, valid, scale):
    scores = jnp.einsum("gqhd,gkhd->ghqk", query, keyed, preferred_element_type=jnp.float32) * scale
    return jnp.where(valid[:, None, None, :] > 0, scores, -1e30)


def plain_shards(
    tokens,
    keep_mask,
    ln1_gain,
    ln1_bias,
    qkv_weight,
    qv_bias,
    proj_weight,
    proj_bias,
    ln2_gain,
    ln2_bias,
    fc1_weight,
    fc1_bias,
    fc2_weight,
    fc2_bias,
    cotangent,
):
    f32 = jnp.float32
    bf16 = jnp.bfloat16
    n_seq = lax.axis_size("seq")
    seq_count, part_len, width = tokens.shape
    seq_len = part_len * n_seq
    img_len = L
    head_local = HEADS // n_seq
    head_width = width // n_seq
    scale = HEAD_DIM ** (-0.5)
    rows = seq_count * part_len
    image_count = keep_mask.shape[0]
    per_group = 1
    pair_count = image_count // per_group
    valid = jnp.concatenate([jnp.ones((image_count, BUF), f32), keep_mask.astype(f32)], axis=1)
    seq_valid = valid.reshape(seq_count, seq_len)
    own_valid = lax.dynamic_slice_in_dim(
        seq_valid, lax.axis_index("seq") * part_len, part_len, 1
    ).reshape(rows, 1)
    valid_pairs = valid.reshape(pair_count, per_group, img_len)
    params = (
        lax.all_gather(ln1_gain, ("fsdp", "seq"), axis=0, tiled=True),
        lax.all_gather(ln1_bias, ("fsdp", "seq"), axis=0, tiled=True),
        lax.all_gather(qkv_weight, ("fsdp", "seq"), axis=0, tiled=True),
        lax.all_gather(qv_bias, ("fsdp", "seq"), axis=0, tiled=True),
        lax.all_gather(proj_weight, ("fsdp", "seq"), axis=0, tiled=True),
        lax.all_gather(proj_bias, ("fsdp", "seq"), axis=0, tiled=True),
        lax.all_gather(ln2_gain, ("fsdp", "seq"), axis=0, tiled=True),
        lax.all_gather(ln2_bias, ("fsdp", "seq"), axis=0, tiled=True),
        lax.all_gather(fc1_weight, ("fsdp", "seq"), axis=0, tiled=True),
        lax.all_gather(fc1_bias, ("fsdp", "seq"), axis=0, tiled=True),
        lax.all_gather(fc2_weight, ("fsdp", "seq"), axis=0, tiled=True),
        lax.all_gather(fc2_bias, ("fsdp", "seq"), axis=0, tiled=True),
    )
    (
        gain_one,
        shift_one,
        w_qkv,
        bias_qv,
        w_proj,
        bias_proj,
        gain_two,
        shift_two,
        w_up,
        bias_up,
        w_down,
        bias_down,
    ) = params
    inputs = tokens.astype(f32).reshape(rows, width)
    normed, unit_one, inv_one = layer_norm(inputs, gain_one.astype(f32), shift_one.astype(f32))
    normed_b = normed.astype(bf16)
    bias_qv = bias_qv.astype(f32)
    full_bias = jnp.concatenate([bias_qv[:width], jnp.zeros((width,), f32), bias_qv[width:]])
    qkv = (jnp.dot(normed_b, w_qkv, preferred_element_type=f32) + full_bias).astype(bf16)
    heads = lax.all_to_all(
        qkv.reshape(seq_count, part_len, 3, width), "seq", split_axis=3, concat_axis=1, tiled=True
    )
    pairs = heads.reshape(pair_count, per_group, img_len, 3, head_width)

    def attend(group):
        block, mask = group
        query = split_heads(block[:, :, 0], head_local)
        keyed = split_heads(block[:, :, 1], head_local)
        values = split_heads(block[:, :, 2], head_local)
        scores = masked_scores(query, keyed, mask, scale)
        top = jnp.max(scores, axis=-1, keepdims=True)
        expo = jnp.exp(scores - top)
        total = jnp.sum(expo, axis=-1, keepdims=True)
        probs = (expo / total).astype(bf16)
        mixed = jnp.einsum("ghqk,gkhd->gqhd", probs, values, preferred_element_type=f32)
        return (
            mixed.reshape(per_group, img_len, head_width).astype(bf16),
            (top + jnp.log(total))[..., 0],
        )

    attn_heads, log_totals = lax.map(attend, (pairs, valid_pairs))
    attn_heads = attn_heads.reshape(seq_count, seq_len, head_width)
    attn_local = lax.all_to_all(attn_heads, "seq", split_axis=1, concat_axis=2, tiled=True).reshape(
        rows, width
    )
    resid = inputs + jnp.dot(attn_local, w_proj, preferred_element_type=f32) + bias_proj.astype(f32)
    normed_two, unit_two, inv_two = layer_norm(resid, gain_two.astype(f32), shift_two.astype(f32))
    normed_two_b = normed_two.astype(bf16)
    hidden = jnp.dot(normed_two_b, w_up, preferred_element_type=f32) + bias_up.astype(f32)
    act, gelu_pull = jax.vjp(lambda value: jax.nn.gelu(value, approximate=False), hidden)
    act_b = act.astype(bf16)
    branch = jnp.dot(act_b, w_down, preferred_element_type=f32) + bias_down.astype(f32)
    layer_out = (own_valid * (resid + branch)).astype(bf16).reshape(seq_count, part_len, width)
    gain_one, w_qkv, w_proj, gain_two, w_up, w_down = (
        lax.all_gather(ln1_gain, ("fsdp", "seq"), axis=0, tiled=True),
        lax.all_gather(qkv_weight, ("fsdp", "seq"), axis=0, tiled=True),
        lax.all_gather(proj_weight, ("fsdp", "seq"), axis=0, tiled=True),
        lax.all_gather(ln2_gain, ("fsdp", "seq"), axis=0, tiled=True),
        lax.all_gather(fc1_weight, ("fsdp", "seq"), axis=0, tiled=True),
        lax.all_gather(fc2_weight, ("fsdp", "seq"), axis=0, tiled=True),
    )
    grad = own_valid * cotangent.astype(f32).reshape(rows, width)
    down_bias_grad = jnp.sum(grad, axis=0)
    grad_b = grad.astype(bf16)
    down_grad = jnp.dot(act_b.T, grad_b, preferred_element_type=f32)
    grad_act = jnp.dot(grad_b, w_down.T, preferred_element_type=f32)
    grad_hidden = gelu_pull(grad_act)[0]
    up_bias_grad = jnp.sum(grad_hidden, axis=0)
    grad_hidden_b = grad_hidden.astype(bf16)
    up_grad = jnp.dot(normed_two_b.T, grad_hidden_b, preferred_element_type=f32)
    grad_normed_two = jnp.dot(grad_hidden_b, w_up.T, preferred_element_type=f32)
    grad_resid_ln, gain_two_grad, shift_two_grad = norm_back(
        grad_normed_two, unit_two, inv_two, gain_two.astype(f32)
    )
    grad_resid = grad + grad_resid_ln
    proj_bias_grad = jnp.sum(grad_resid, axis=0)
    grad_resid_b = grad_resid.astype(bf16)
    proj_grad = jnp.dot(attn_local.T, grad_resid_b, preferred_element_type=f32)
    grad_attn = jnp.dot(grad_resid_b, w_proj.T, preferred_element_type=f32).astype(bf16)
    grad_heads = lax.all_to_all(
        grad_attn.reshape(seq_count, part_len, width),
        "seq",
        split_axis=2,
        concat_axis=1,
        tiled=True,
    )
    grad_pairs = grad_heads.reshape(pair_count, per_group, img_len, head_width)

    def attend_back(group):
        block, mask, lse, grad_mixed = group
        query = split_heads(block[:, :, 0], head_local)
        keyed = split_heads(block[:, :, 1], head_local)
        values = split_heads(block[:, :, 2], head_local)
        grad_out = split_heads(grad_mixed, head_local)
        scores = masked_scores(query, keyed, mask, scale)
        probs = jnp.exp(scores - lse[..., None])
        dprobs = jnp.einsum("gqhd,gkhd->ghqk", grad_out, values, preferred_element_type=f32)
        grad_values = jnp.einsum(
            "ghqk,gqhd->gkhd", probs.astype(bf16), grad_out, preferred_element_type=f32
        )
        rowdot = jnp.sum(dprobs * probs, axis=-1, keepdims=True)
        grad_scores = (probs * (dprobs - rowdot)).astype(bf16)
        grad_query = (
            jnp.einsum("ghqk,gkhd->gqhd", grad_scores, keyed, preferred_element_type=f32) * scale
        )
        grad_keyed = (
            jnp.einsum("ghqk,gqhd->gkhd", grad_scores, query, preferred_element_type=f32) * scale
        )
        stacked = jnp.stack(
            [
                grad_query.reshape(per_group, img_len, head_width),
                grad_keyed.reshape(per_group, img_len, head_width),
                grad_values.reshape(per_group, img_len, head_width),
            ],
            axis=2,
        )
        return stacked.astype(bf16)

    grad_qkv_heads = lax.map(attend_back, (pairs, valid_pairs, log_totals, grad_pairs))
    grad_qkv_heads = grad_qkv_heads.reshape(seq_count, seq_len, 3, head_width)
    grad_qkv = lax.all_to_all(
        grad_qkv_heads, "seq", split_axis=1, concat_axis=3, tiled=True
    ).reshape(rows, 3 * width)
    column_sums = jnp.sum(grad_qkv.astype(f32), axis=0)
    qv_grad = jnp.concatenate([column_sums[:width], column_sums[2 * width :]])
    qkv_grad = jnp.dot(normed_b.T, grad_qkv, preferred_element_type=f32)
    grad_normed = jnp.dot(grad_qkv, w_qkv.T, preferred_element_type=f32)
    grad_in_ln, gain_one_grad, shift_one_grad = norm_back(
        grad_normed, unit_one, inv_one, gain_one.astype(f32)
    )
    tokens_grad = (grad_resid + grad_in_ln).astype(bf16).reshape(seq_count, part_len, width)
    summed = (
        lax.psum_scatter(gain_one_grad, ("fsdp", "seq"), scatter_dimension=0, tiled=True),
        lax.psum_scatter(shift_one_grad, ("fsdp", "seq"), scatter_dimension=0, tiled=True),
        lax.psum_scatter(qkv_grad, ("fsdp", "seq"), scatter_dimension=0, tiled=True),
        lax.psum_scatter(qv_grad, ("fsdp", "seq"), scatter_dimension=0, tiled=True),
        lax.psum_scatter(proj_grad, ("fsdp", "seq"), scatter_dimension=0, tiled=True),
        lax.psum_scatter(proj_bias_grad, ("fsdp", "seq"), scatter_dimension=0, tiled=True),
        lax.psum_scatter(gain_two_grad, ("fsdp", "seq"), scatter_dimension=0, tiled=True),
        lax.psum_scatter(shift_two_grad, ("fsdp", "seq"), scatter_dimension=0, tiled=True),
        lax.psum_scatter(up_grad, ("fsdp", "seq"), scatter_dimension=0, tiled=True),
        lax.psum_scatter(up_bias_grad, ("fsdp", "seq"), scatter_dimension=0, tiled=True),
        lax.psum_scatter(down_grad, ("fsdp", "seq"), scatter_dimension=0, tiled=True),
        lax.psum_scatter(down_bias_grad, ("fsdp", "seq"), scatter_dimension=0, tiled=True),
    )
    return (
        layer_out,
        tokens_grad,
        summed[0],
        summed[1],
        summed[2],
        summed[3],
        summed[4],
        summed[5],
        summed[6],
        summed[7],
        summed[8],
        summed[9],
        summed[10],
        summed[11],
    )


def shards(
    tokens,
    keep_mask,
    ln1_gain,
    ln1_bias,
    qkv_weight,
    qv_bias,
    proj_weight,
    proj_bias,
    ln2_gain,
    ln2_bias,
    fc1_weight,
    fc1_bias,
    fc2_weight,
    fc2_bias,
    cotangent,
):
    n_fsdp, n_seq = lax.axis_size("fsdp"), lax.axis_size("seq")
    s = Sizes(n_fsdp // 4, n_seq, tokens.shape[1], tokens.shape[2], fc1_weight.shape[1])
    if not s.fits(tokens.shape[0]):
        return plain_shards(
            tokens,
            keep_mask,
            ln1_gain,
            ln1_bias,
            qkv_weight,
            qv_bias,
            proj_weight,
            proj_bias,
            ln2_gain,
            ln2_bias,
            fc1_weight,
            fc1_bias,
            fc2_weight,
            fc2_bias,
            cotangent,
        )
    framed, own = frames(s, keep_mask)
    small = pack_small(s, ln1_gain, ln1_bias, proj_bias, ln2_gain, ln2_bias, fc2_bias, qv_bias, fc1_bias)
    x = tokens.reshape(s.part, s.width)
    cot = cotangent.reshape(s.part, s.width)
    out, n1f, qkvf, attn, r1, n2, act, slope, p, wq, wp, w1, w2, vec = forward_call(
        s, x, framed, own, small, qkv_weight, proj_weight, fc1_weight, fc2_weight
    )
    flat = [w.reshape(-1, w.shape[-1]) for w in (wq, wp, w1, w2)]
    back, dwq, dwp, dw1, dw2, vecs = backward_call(s, x, own, cot, n1f, qkvf, attn, r1, n2, act, slope, p, *flat, vec)
    unit = s.rows
    piece = {name: vecs[0, start * unit : (start + times) * unit] for name, start, times in VECS}
    return (
        out.reshape(tokens.shape),
        back.reshape(tokens.shape),
        piece["ln1g"],
        piece["ln1b"],
        dwq,
        piece["qvb"],
        dwp,
        piece["projb"],
        piece["ln2g"],
        piece["ln2b"],
        dw1,
        piece["fc1b"],
        dw2,
        piece["fc2b"],
    )


def solution(mesh):
    rows = P(("fsdp", "seq"))
    weight = P(("fsdp", "seq"), None)
    data = P("fsdp", "seq", None)
    placed = (data, P("fsdp", None), rows, rows, weight, rows, weight, rows, rows, rows, weight, rows, weight, rows, data)
    return jax.shard_map(
        shards,
        mesh=mesh,
        in_specs=placed,
        out_specs=(data, data, rows, rows, weight, rows, weight, rows, rows, rows, weight, rows, weight, rows),
        check_vma=False,
    )
```

```python
import functools
import math

import jax
import jax.numpy as jnp
from jax import lax
from jax.experimental import pallas as pl
from jax.experimental.pallas import tpu as pltpu
from jax.sharding import PartitionSpec as P

HEADS = 16
HEAD_DIM = 64
BUF = 64
L = 320
MESH = pl.DeviceIdType.MESH
BF = jnp.bfloat16
F32 = jnp.float32
LANES = 128
MIB = 2**20


def nn(a, b):
    return lax.dot_general(a, b, (((1,), (0,)), ((), ())), preferred_element_type=F32)


def nt(a, b):
    return lax.dot_general(a, b, (((1,), (1,)), ((), ())), preferred_element_type=F32)


def tn(a, b):
    return lax.dot_general(a, b, (((0,), (0,)), ((), ())), preferred_element_type=F32)


class Place:
    def __init__(self, nz, nx):
        f = lax.axis_index("fsdp")
        self.x = lax.axis_index("seq")
        self.nz, self.nx = nz, nx
        self.z = lax.div(f, 4)
        self.y = lax.rem(lax.div(f, 2), 2)
        self.c = lax.rem(f, 2)
        self.odd = lax.rem(self.x, 2)

    def at(self, z=None, y=None, c=None, x=None):
        z = self.z if z is None else z
        y = self.y if y is None else y
        c = self.c if c is None else c
        x = self.x if x is None else x
        return {"fsdp": (z * 2 + y) * 2 + c, "seq": x}

    def zs(self):
        return [lax.rem(self.z + d, self.nz) for d in range(1, self.nz)]

    def xs(self):
        return [lax.rem(self.x + d, self.nx) for d in range(1, self.nx)]

    def partner(self):
        return self.at(x=self.x + 1 - 2 * self.odd)

    def greet(self):
        peers = [self.at(z=z) for z in self.zs()] + [self.at(x=x) for x in self.xs()]
        peers += [self.at(y=1 - self.y), self.at(c=1 - self.c)]
        barrier = pltpu.get_barrier_semaphore()
        for peer in peers:
            pl.semaphore_signal(barrier, inc=1, device_id=peer, device_id_type=MESH)
        pl.semaphore_wait(barrier, len(peers))


class Sems:
    def __init__(self, send, recv):
        self.send, self.recv, self.used = send, recv, 0

    def copy(self, src, dst, device):
        slot = self.used
        self.used += 1
        return pltpu.make_async_remote_copy(
            src_ref=src,
            dst_ref=dst,
            send_sem=self.send.at[slot],
            recv_sem=self.recv.at[slot],
            device_id=device,
            device_id_type=MESH,
        )


def gather_copies(here, sems, src, buf, rows, cols, early):
    (top, height), (lo, width) = rows, cols
    if height >= width:
        at_a, at_b = (pl.ds(top, height // 2), pl.ds(lo, width)), (pl.ds(top + height // 2, height // 2), pl.ds(lo, width))
    else:
        at_a, at_b = (pl.ds(top, height), pl.ds(lo, width // 2)), (pl.ds(top, height), pl.ds(lo + width // 2, width // 2))
    every = (pl.ds(top, height), pl.ds(lo, width))
    z, y, c, x = here.z, here.y, here.c, here.x
    full = pl.ds(0, here.nz), pl.ds(0, 2), pl.ds(0, here.nx)

    def move(place, part, device):
        ref = buf.at[(*place, *part)]
        return sems.copy(ref, ref, device)

    mine = (z, y, c, x)
    if early:
        first = [sems.copy(src.at[every], buf.at[(*mine, *every)], here.at(z=t)) for t in here.zs()]
        second = [move((full[0], y, c, x), at_a, here.at(x=t)) for t in here.xs()]
        second += [move((full[0], y, c, x), at_b, here.at(y=1 - y))]
    else:
        first = [sems.copy(src.at[at_a], buf.at[(*mine, *at_a)], here.at(x=t)) for t in here.xs()]
        first += [sems.copy(src.at[at_b], buf.at[(*mine, *at_b)], here.at(y=1 - y))]
        second = [move((z, y, c, full[2]), at_a, here.at(z=t)) for t in here.zs()]
        second += [move((z, full[1], c, x), at_b, here.at(z=t)) for t in here.zs()]
    third = [move((full[0], y, c, full[2]), at_a, here.at(y=1 - y))]
    third += [move((full[0], full[1], c, x), at_b, here.at(x=t)) for t in here.xs()]
    last = [move((full[0], full[1], c, full[2]), every, here.at(c=1 - c))]
    return [first, second, third, last]


def small_copies(here, sems, src, buf):
    z, y, c, x = here.z, here.y, here.c, here.x
    first = [sems.copy(src, buf.at[z, y, c, x], here.at(z=t)) for t in here.zs()]
    second = [sems.copy(buf.at[:, y, c, x], buf.at[:, y, c, x], here.at(x=t)) for t in here.xs()]
    third = [sems.copy(buf.at[:, y, c], buf.at[:, y, c], here.at(y=1 - y))]
    last = [sems.copy(buf.at[:, :, c], buf.at[:, :, c], here.at(c=1 - c))]
    return [first, second, third, last]


def gather_count(nz, nx, early):
    if early:
        return (nz - 1) + (nx - 1) + 1 + 1 + (nx - 1) + 1
    return (nx - 1) + 1 + 2 * (nz - 1) + 1 + (nx - 1) + 1


def columns(buf, lo, width):
    part = buf[:, :, :, :, :, pl.ds(lo, width)]
    return part.reshape(-1, width)


def norm_stats(value):
    mean = jnp.mean(value, axis=-1, keepdims=True)
    centred = value - mean
    inverse = lax.rsqrt(jnp.mean(centred * centred, axis=-1, keepdims=True) + 1e-06)
    return centred * inverse, inverse


def gelu_pair(v):
    e = jnp.exp(v * v * (-0.5))
    t = pl.reciprocal(1.0 + (0.3275911 * math.sqrt(0.5)) * jnp.abs(v), approx=False)
    poly = 0.5 * 1.061405429
    for a in (-1.453152027, 1.421413741, -0.284496736, 0.254829592):
        poly = poly * t + 0.5 * a
    tail = poly * t * e
    cdf = jnp.where(v >= 0, 1.0 - tail, tail)
    return v * cdf, cdf + v * e * (1.0 / math.sqrt(2.0 * math.pi))


VECS = (("ln1g", 0, 1), ("ln1b", 1, 1), ("projb", 2, 1), ("ln2g", 3, 1), ("ln2b", 4, 1), ("fc2b", 5, 1), ("qvb", 6, 2), ("fc1b", 8, 4))
ROW = {name: i for i, (name, _, _) in enumerate(VECS)}
PACK = 12
PACK_ROWS = 16


def expand_vectors(small_buf, vec, count, width):
    unit = width // count
    total = PACK * unit
    pieces = small_buf[...].astype(F32).reshape(count, PACK_ROWS, total)
    pieces = jnp.sum(pieces, axis=1).astype(BF)
    for row, (_, start, times) in enumerate(VECS):
        per = unit * times
        shift = per.bit_length() - 1
        for lo in range(0, width * times, width):
            index = lax.broadcasted_iota(jnp.int32, (total, width), 1) + lo
            source = lax.broadcasted_iota(jnp.int32, (total, width), 0) - start * unit
            pick = ((index & (per - 1)) == source).astype(F32).astype(BF)
            spread = nn(pieces, pick)
            owner = lax.shift_right_logical(lax.broadcasted_iota(jnp.int32, (count, width), 1) + lo, shift)
            mine = owner == lax.broadcasted_iota(jnp.int32, (count, width), 0)
            vec[row : row + 1, lo : lo + width] = jnp.sum(jnp.where(mine, spread, 0.0), axis=0, keepdims=True)


class Sizes:
    def __init__(self, nz, nx, part, width, hidden):
        self.nz, self.nx, self.part, self.width, self.hidden = nz, nx, part, width, hidden
        self.count = nz * 4 * nx
        self.half = part % L
        self.frame = part + self.half
        self.whole = part // L
        self.rows = width // self.count

    def fits(self, sequences):
        paired = self.half * 2 == L and self.half % 32 == 0 and self.part % 32 == 0 and self.nx % 2 == 0
        return sequences == 1 and paired and self.rows % 32 == 0 and self.nz > 1 and self.hidden % self.width == 0


LAG = 3
LATE = (2, 5)
BUDGET = 2.5


def forward_chunks(s):
    step = 512
    narrow = step * s.width // s.hidden
    fat = s.hidden // s.count
    cut = [(0, (0, s.rows), (lo, step)) for lo in range(0, 3 * s.width, step)]
    cut += [(1, (0, s.rows), (lo, step)) for lo in range(0, s.width, step)]
    cut += [(2, (0, s.rows), (lo, step)) for lo in range(0, s.hidden, step)]
    cut += [(3, (0, fat), (lo, narrow)) for lo in range(0, s.width, narrow)]
    return [(*item, i % LATE[1] != LATE[0]) for i, item in enumerate(cut)]


def forward_copies(s):
    total = sum(gather_count(s.nz, s.nx, early) for *_, early in forward_chunks(s))
    return total + (s.nz - 1) + (s.nx - 1) + 1 + 1 + 1


def attend(s, steps, k0, q0, row0, count, image, qkv, valid, attn, p_slot, p_out, p_sem):
    width = s.width
    low = lax.broadcasted_iota(jnp.int32, (1, LANES), 1) < HEAD_DIM
    zero = jnp.zeros((), BF)
    keep = valid[pl.ds(image, 1), :] > 0

    def out_copy(step, slot):
        return pltpu.make_async_copy(
            p_slot.at[slot, :, pl.ds(0, count), :],
            p_out.at[pl.ds(step * 4, 4), pl.ds(row0, count), :],
            p_sem.at[slot],
        )

    def body(step, carry):
        slot = lax.rem(step, 2)

        @pl.when(step >= steps[0] + 2)
        def _():
            out_copy(step - 2, slot).wait()

        for pair in range(2):
            col = pl.multiple_of((step * 2 + pair) * LANES, LANES)
            q2 = qkv[pl.ds(q0, count), pl.ds(col, LANES)]
            k2 = qkv[pl.ds(k0, L), pl.ds(col + width, LANES)]
            v2 = qkv[pl.ds(k0, L), pl.ds(col + 2 * width, LANES)]
            mixed = None
            for head in range(2):
                sel = low if head == 0 else jnp.logical_not(low)
                scores = nt(jnp.where(sel, q2, zero) * BF(HEAD_DIM**-0.5), k2)
                scores = jnp.where(keep, scores, -1e30)
                expo = jnp.exp(scores - jnp.max(scores, axis=-1, keepdims=True))
                probs = (expo * (1.0 / jnp.sum(expo, axis=-1, keepdims=True))).astype(BF)
                p_slot[slot, pair * 2 + head, pl.ds(0, count), :] = probs
                part = nn(probs, jnp.where(sel, v2, zero))
                mixed = part if mixed is None else mixed + part
            attn[pl.ds(row0, count), pl.ds(col, LANES)] = mixed.astype(BF)
        out_copy(step, slot).start()
        return carry

    first, end = steps
    lax.fori_loop(first, end, body, 0)
    for step in (end - 2, end - 1):
        out_copy(step, step % 2).wait()


def forward_kernel(
    s,
    x_ref,
    valid,
    own_valid,
    small_ref,
    wq_ref,
    wp_ref,
    w1_ref,
    w2_ref,
    out_ref,
    n1_out,
    qkv_out,
    attn_out,
    r1_out,
    n2_out,
    act_out,
    slope_out,
    p_out,
    wq_out,
    wp_out,
    w1_out,
    w2_out,
    vec_out,
    wq_buf,
    wp_buf,
    w1_buf,
    w2_buf,
    small_buf,
    vec,
    xf,
    n1f,
    qkvf,
    attn,
    r1,
    n2,
    act,
    slope,
    hidden,
    p_slot,
    send,
    recv,
    local_sem,
    save_sem,
    slope_sem,
    p_sem,
):
    here = Place(s.nz, s.nx)
    sems = Sems(send, recv)
    odd, width, part, half = here.odd, s.width, s.part, s.half
    off = pl.multiple_of(odd * half, 32)
    z, y, c, x = here.z, here.y, here.c, here.x
    srcs = (wq_ref, wp_ref, w1_ref, w2_ref)
    bufs = (wq_buf, wp_buf, w1_buf, w2_buf)
    outs = (wq_out, wp_out, w1_out, w2_out)

    own = [pltpu.make_async_copy(src, buf.at[z, y, c, x], local_sem.at[i]) for i, (src, buf) in enumerate(zip(srcs, bufs))]
    own.append(pltpu.make_async_copy(small_ref, small_buf.at[z, y, c, x], local_sem.at[4]))
    own.append(pltpu.make_async_copy(x_ref, xf.at[pl.ds(off, part), :], local_sem.at[5]))
    for copy in own:
        copy.start()

    chunks = forward_chunks(s)
    plans = [gather_copies(here, sems, srcs[w], bufs[w], rows, cols, early) for w, rows, cols, early in chunks]
    small = small_copies(here, sems, small_ref, small_buf)
    plans[0] = [extra + base for base, extra in zip(plans[0], small)]
    edge_from = pl.multiple_of((part - half) * (1 - odd), 32)
    edge_to = pl.multiple_of(part * odd, 32)
    halo = sems.copy(x_ref.at[pl.ds(edge_from, half), :], xf.at[pl.ds(edge_to, half), :], here.partner())

    saves = []
    slots = iter(range(save_sem.shape[0]))

    def save(src, dst, listed=True):
        copy = pltpu.make_async_copy(src, dst, save_sem.at[next(slots)])
        copy.start()
        if listed:
            saves.append(copy)
        return copy

    here.greet()
    halo.start()
    last = len(chunks)

    starts = [0, LAG, 2 * LAG, 3 * LAG]
    ready = 3 * LAG + 1

    def pump(k):
        j = k - ready
        if 0 <= j < last:
            for copy in plans[j][3]:
                copy.wait_recv()
            w, rows, cols, _ = chunks[j]
            part_of = (slice(None),) * 4 + (pl.ds(*rows), pl.ds(*cols))
            save(bufs[w].at[part_of], outs[w].at[part_of])
        for phase in (3, 2, 1):
            j = k - starts[phase]
            if 0 <= j < last:
                for copy in plans[j][phase - 1]:
                    copy.wait_recv()
                if j == 0 and phase == 1:
                    for copy in own:
                        copy.wait()
                for copy in plans[j][phase]:
                    copy.start()
        if k < last:
            for copy in plans[k][0]:
                copy.start()

    def norm_one():
        expand_vectors(small_buf, vec, s.count, width)
        save(vec, vec_out)
        halo.wait_recv()

        def body(i, carry):
            rows = pl.ds(pl.multiple_of(i * 32, 32), 32)
            unit, _ = norm_stats(xf[rows, :].astype(F32))
            n1f[rows, :] = (unit * vec[ROW["ln1g"] : ROW["ln1g"] + 1, :width] + vec[ROW["ln1b"] : ROW["ln1b"] + 1, :width]).astype(BF)
            return carry

        lax.fori_loop(0, s.frame // 32, body, 0)
        return save(n1f, n1_out, listed=False)

    def project(i):
        third, lo = divmod(i * 512, width)
        got = nn(n1f[...], columns(wq_buf, i * 512, 512))
        if third != 1:
            start = (third // 2) * width + lo
            got = got + vec[ROW["qvb"] : ROW["qvb"] + 1, start : start + 512]
        qkvf[:, i * 512 : i * 512 + 512] = got.astype(BF)

    def whole_image(i, heads):
        k0 = pl.multiple_of((i + odd) * L, 32)
        row0 = pl.multiple_of(i * L + odd * half, 32)
        attend(s, heads, k0, k0, row0, L, i + odd, qkvf, valid, attn, p_slot, p_out, p_sem)

    def edge_image(heads):
        k0 = pl.multiple_of(s.whole * L * (1 - odd), 32)
        q0 = pl.multiple_of(s.whole * L * (1 - odd) + half * odd, 32)
        row0 = pl.multiple_of(s.whole * L * (1 - odd), 32)
        attend(s, heads, k0, q0, row0, half, s.whole * (1 - odd), qkvf, valid, attn, p_slot, p_out, p_sem)

    def output_projection(i):
        lo = i * 512
        got = nn(attn[...], columns(wp_buf, lo, 512)) + vec[ROW["projb"] : ROW["projb"] + 1, lo : lo + 512]
        r1[:, lo : lo + 512] = got + xf[pl.ds(off, part), lo : lo + 512].astype(F32)

    def norm_two():
        save(r1, r1_out)

        def body(i, carry):
            rows = pl.ds(pl.multiple_of(i * 32, 32), 32)
            unit, _ = norm_stats(r1[rows, :])
            n2[rows, :] = (unit * vec[ROW["ln2g"] : ROW["ln2g"] + 1, :width] + vec[ROW["ln2b"] : ROW["ln2b"] + 1, :width]).astype(BF)
            return carry

        lax.fori_loop(0, part // 32, body, 0)
        save(n2, n2_out)

    slope_copies = []

    def up(i):
        slot, at = i % 2, i * 512
        if i >= 2:
            slope_copies[i - 2].wait()
        hidden[...] = nn(n2[...], columns(w1_buf, at, 512)) + vec[ROW["fc1b"] : ROW["fc1b"] + 1, at : at + 512]

        def body(j, carry):
            rows = pl.ds(pl.multiple_of(j * 32, 32), 32)
            value, grade = gelu_pair(hidden[rows, :])
            act[rows, at : at + 512] = value.astype(BF)
            slope[slot, rows, :] = grade.astype(BF)
            return carry

        lax.fori_loop(0, part // 32, body, 0)
        copy = pltpu.make_async_copy(slope.at[slot], slope_out.at[:, pl.ds(at, 512)], slope_sem.at[slot])
        copy.start()
        slope_copies.append(copy)
        save(act.at[:, pl.ds(at, 512)], act_out.at[:, pl.ds(at, 512)])

    narrow = 256
    result = n1f

    def down(i):
        lo = i * narrow
        branch = nn(act[...], columns(w2_buf, lo, narrow)) + vec[ROW["fc2b"] : ROW["fc2b"] + 1, lo : lo + narrow]
        result[pl.ds(0, part), lo : lo + narrow] = (own_valid[...] * (r1[:, lo : lo + narrow] + branch)).astype(BF)

    ends = {}
    for j, (w, _, (lo, n), _) in enumerate(chunks):
        ends[w, lo + n] = j + ready
    kept = {}

    def norm():
        kept["n1"] = norm_one()

    def first_down():
        kept["n1"].wait()
        down(0)

    tasks = [(ready, 4.0, norm)]
    tasks += [(ends[0, (i + 1) * 512], 1.6, functools.partial(project, i)) for i in range(3 * width // 512)]
    steps = HEADS // 4
    halves = ((0, steps // 2), (steps // 2, steps))
    for i in range(s.whole):
        tasks += [(0, 3.5, functools.partial(whole_image, i, heads)) for heads in halves]
    tasks += [(0, 2.9, functools.partial(edge_image, heads)) for heads in halves]
    tasks += [(0, 0.0, lambda: (save(qkvf, qkv_out), save(attn, attn_out)))]
    tasks += [(ends[1, (i + 1) * 512], 1.4, functools.partial(output_projection, i)) for i in range(width // 512)]
    tasks += [(0, 2.5, norm_two)]
    tasks += [(ends[2, (i + 1) * 512], 3.0, functools.partial(up, i)) for i in range(s.hidden // 512)]
    tasks += [(ends[3, (i + 1) * narrow], 2.2, first_down if i == 0 else functools.partial(down, i)) for i in range(width // narrow)]
    for k in range(last + ready):
        pump(k)
        budget = BUDGET
        while tasks and tasks[0][0] <= k and (budget > 0 or k + 1 == last + ready):
            _, cost, task = tasks.pop(0)
            task()
            budget -= cost

    final = pltpu.make_async_copy(result.at[pl.ds(0, part), :], out_ref, local_sem.at[0])
    final.start()
    for copy in slope_copies[-2:]:
        copy.wait()
    for copy in saves:
        copy.wait()
    halo.wait_send()
    for plan in plans:
        for phase in plan:
            for copy in phase:
                copy.wait_send()
    final.wait()


def forward_call(s, x, valid, own_valid, small, wq, wp, w1, w2):
    anyspace = pl.BlockSpec(memory_space=pl.ANY)
    vmem = pl.BlockSpec(memory_space=pltpu.VMEM)
    lead = (s.nz, 2, 2, s.nx)
    shape = lambda dims, kind=BF: jax.ShapeDtypeStruct(dims, kind)
    part, width, hidden, rows = s.part, s.width, s.hidden, s.rows
    fat = hidden // s.count
    gathered = [lead + (rows, 3 * width), lead + (rows, width), lead + (rows, hidden), lead + (fat, width)]
    outs = [
        shape((part, width)),
        shape((s.frame, width)),
        shape((s.frame, 3 * width)),
        shape((part, width)),
        shape((part, width), F32),
        shape((part, width)),
        shape((part, hidden)),
        shape((part, hidden)),
        shape((HEADS, part, L)),
        *[shape(dims) for dims in gathered],
        shape((8, hidden), F32),
    ]
    copies = forward_copies(s)
    scratch = [pltpu.VMEM(dims, BF) for dims in gathered]
    scratch += [
        pltpu.VMEM(lead + (PACK_ROWS, PACK * rows), BF),
        pltpu.VMEM((8, hidden), F32),
        pltpu.VMEM((s.frame, width), BF),
        pltpu.VMEM((s.frame, width), BF),
        pltpu.VMEM((s.frame, 3 * width), BF),
        pltpu.VMEM((part, width), BF),
        pltpu.VMEM((part, width), F32),
        pltpu.VMEM((part, width), BF),
        pltpu.VMEM((part, hidden), BF),
        pltpu.VMEM((2, part, 512), BF),
        pltpu.VMEM((part, 512), F32),
        pltpu.VMEM((2, 4, L, L), BF),
        pltpu.SemaphoreType.DMA((copies,)),
        pltpu.SemaphoreType.DMA((copies,)),
        pltpu.SemaphoreType.DMA((6,)),
        pltpu.SemaphoreType.DMA((len(forward_chunks(s)) + 6 + s.hidden // 512,)),
        pltpu.SemaphoreType.DMA((2,)),
        pltpu.SemaphoreType.DMA((2,)),
    ]
    return pl.pallas_call(
        functools.partial(forward_kernel, s),
        out_shape=outs,
        in_specs=[anyspace, vmem, vmem, anyspace, anyspace, anyspace, anyspace, anyspace],
        out_specs=[anyspace] * len(outs),
        scratch_shapes=scratch,
        name="forward",
        compiler_params=pltpu.CompilerParams(collective_id=0, has_side_effects=True, vmem_limit_bytes=63 * MIB),
    )(x, valid, own_valid, small, wq, wp, w1, w2)


def frames(s, keep_mask):
    images = keep_mask.shape[0]
    x = lax.axis_index("seq")
    odd = lax.rem(x, 2)
    valid = jnp.concatenate([jnp.ones((images, BUF), F32), keep_mask.astype(F32)], axis=1)
    first = lax.div(x * s.part - odd * s.half, L)
    framed = lax.dynamic_slice_in_dim(valid, first, s.whole + 1, 0)
    framed = jnp.pad(framed, ((0, 8 - s.whole - 1), (0, 0)))
    own = lax.dynamic_slice_in_dim(valid.reshape(-1), x * s.part, s.part, 0).reshape(s.part, 1)
    return framed, own


def pack_small(s, ln1_gain, ln1_bias, proj_bias, ln2_gain, ln2_bias, fc2_bias, qv_bias, fc1_bias):
    pieces = (ln1_gain, ln1_bias, proj_bias, ln2_gain, ln2_bias, fc2_bias, qv_bias, fc1_bias)
    total, at, row = PACK * s.rows, 0, 0
    for piece in pieces:
        row = row + jnp.pad(piece[None, :], ((0, PACK_ROWS - 1), (at, total - at - piece.shape[0])))
        at += piece.shape[0]
    return row


class Scatter:
    G_SLOTS = 4
    RING = (5, 6, 4, 4)
    OFFSET = (0, 1, 3, 5, 7)

    def __init__(self, s, here, sems, g, l0, l1a, l1b, l2a, l2b, s2, l3, fin, credit, fin_sem, total):
        self.s, self.here, self.sems, self.total = s, here, sems, total
        self.g, self.l0, self.l1a, self.l1b, self.l2a, self.l2b = g, l0, l1a, l1b, l2a, l2b
        self.s2, self.l3, self.fin, self.credit, self.fin_sem = s2, l3, fin, credit, fin_sem
        nx, nz = s.nx, s.nz
        z, y, c, x = here.z, here.y, here.c, here.x
        self.fore_x, self.fore_z = here.xs(), here.zs()
        self.back_x = [lax.rem(x + nx - d, nx) for d in range(1, nx)]
        self.back_z = [lax.rem(z + nz - d, nz) for d in range(1, nz)]
        self.stage_of = {"c": 0, "1y": 1, "1x": 1, "2x": 2, "2y": 2, "z": 3}
        self.base = {"c": 0, "1y": 1, "1x": 2, "2x": 1 + nx, "2y": 2 * nx, "z": 2 * nx + 1}
        self.sent = {}
        self.out = {}
        self.width = g.shape[-1]
        self.a, self.b = pl.ds(0, self.width // 2), pl.ds(self.width // 2, self.width // 2)

    @staticmethod
    def copies(s):
        return 1 + 1 + (s.nx - 1) + (s.nx - 1) + 1 + (s.nz - 1)

    def take(self, j, key, d=0):
        if j >= self.RING[self.stage_of[key]]:
            pl.semaphore_wait(self.credit.at[self.base[key] + d], 1)

    def give(self, j, key, device, d=0):
        if j + self.RING[self.stage_of[key]] < self.total:
            pl.semaphore_signal(self.credit.at[self.base[key] + d], inc=1, device_id=device, device_id_type=MESH)

    def launch(self, j, stage, copies):
        for copy in copies:
            copy.start()
        self.sent[(j, stage)] = copies

    def landed(self, j, stage):
        for copy in self.sent[(j, stage)]:
            copy.wait_recv()

    def left(self, j, stage):
        for copy in self.sent.pop((j, stage)):
            copy.wait_send()

    def free_g(self, j):
        if j >= self.G_SLOTS:
            self.left(j - self.G_SLOTS, 0)

    def stage0(self, j):
        here, c = self.here, self.here.c
        self.take(j, "c")
        src = self.g.at[j % self.G_SLOTS, :, :, 1 - c]
        self.launch(j, 0, [self.sems.copy(src, self.l0.at[j % self.RING[0]], here.at(c=1 - c))])

    def stage1(self, j):
        here, l0, g = self.here, self.l0, self.g
        y, c, t, t1, u = here.y, here.c, j % self.RING[0], j % self.RING[1], j % self.G_SLOTS
        self.landed(j, 0)

        def body(zz, carry):
            for yy in range(2):
                for xx in range(self.s.nx):
                    l0[t, zz, yy, xx] = l0[t, zz, yy, xx] + g[u, zz, yy, c, xx]
            return carry

        lax.fori_loop(0, self.s.nz, body, 0)
        copies = []
        self.take(j, "1y")
        copies.append(self.sems.copy(l0.at[t, :, 1 - y, :, :, self.a], self.l1a.at[t1], here.at(y=1 - y)))
        for d, peer in enumerate(self.fore_x):
            self.take(j, "1x", d)
            copies.append(self.sems.copy(l0.at[t, :, :, peer, :, self.b], self.l1b.at[t1, d], here.at(x=peer)))
        self.launch(j, 1, copies)

    def stage2(self, j):
        here, l0, l1a, l1b = self.here, self.l0, self.l1a, self.l1b
        y, c, x = here.y, here.c, here.x
        t, t1, t2 = j % self.RING[0], j % self.RING[1], j % self.RING[2]
        self.landed(j, 1)

        def body(zz, carry):
            for xx in range(self.s.nx):
                l1a[t1, zz, xx] = l1a[t1, zz, xx] + l0[t, zz, y, xx, :, self.a]
            for yy in range(2):
                got = l0[t, zz, yy, x, :, self.b].astype(F32)
                for d in range(self.s.nx - 1):
                    got = got + l1b[t1, d, zz, yy].astype(F32)
                l1b[t1, 0, zz, yy] = got.astype(BF)
            return carry

        lax.fori_loop(0, self.s.nz, body, 0)
        copies = []
        for d, peer in enumerate(self.fore_x):
            self.take(j, "2x", d)
            copies.append(self.sems.copy(l1a.at[t1, :, peer], self.l2a.at[t2, d], here.at(x=peer)))
        self.take(j, "2y")
        copies.append(self.sems.copy(l1b.at[t1, 0, :, 1 - y], self.l2b.at[t2], here.at(y=1 - y)))
        self.launch(j, 2, copies)
        self.left(j, 1)
        self.give(j, "c", here.at(c=1 - c))

    def stage3(self, j):
        here, l1a, l1b, l2a, l2b, s2 = self.here, self.l1a, self.l1b, self.l2a, self.l2b, self.s2
        y, x = here.y, here.x
        t, t1, t2 = j % self.RING[3], j % self.RING[1], j % self.RING[2]
        self.landed(j, 2)

        def body(zz, carry):
            got = l1a[t1, zz, x].astype(F32)
            for d in range(self.s.nx - 1):
                got = got + l2a[t2, d, zz].astype(F32)
            s2[t, zz, :, self.a] = got.astype(BF)
            s2[t, zz, :, self.b] = l2b[t2, zz] + l1b[t1, 0, zz, y]
            return carry

        lax.fori_loop(0, self.s.nz, body, 0)
        copies = []
        for d, peer in enumerate(self.fore_z):
            self.take(j, "z", d)
            copies.append(self.sems.copy(s2.at[t, peer], self.l3.at[t, d], here.at(z=peer)))
        self.launch(j, 3, copies)
        self.left(j, 2)
        self.give(j, "1y", here.at(y=1 - y))
        self.give(j, "2y", here.at(y=1 - y))
        for d, peer in enumerate(self.back_x):
            self.give(j, "1x", here.at(x=peer), d)
            self.give(j, "2x", here.at(x=peer), d)

    def stage4(self, j, targets):
        here, s2, l3, fin = self.here, self.s2, self.l3, self.fin
        t, u = j % self.RING[3], j % 2
        self.landed(j, 3)
        for copy in self.out.pop(j - 2, []):
            copy.wait()
        got = s2[t, here.z].astype(F32)
        for d in range(self.s.nz - 1):
            got = got + l3[t, d].astype(F32)
        fin[u] = got
        self.left(j, 3)
        for d, peer in enumerate(self.back_z):
            self.give(j, "z", here.at(z=peer), d)
        copies = [pltpu.make_async_copy(src, dst, self.fin_sem.at[u, i]) for i, (src, dst) in enumerate(targets(fin.at[u]))]
        for copy in copies:
            copy.start()
        self.out[j] = copies

    def finish(self):
        for copies in self.out.values():
            for copy in copies:
                copy.wait()
        for j, stage in sorted(self.sent):
            self.left(j, stage)


def small_scatter_copies(s):
    return 1 + (s.nx - 1) + 1 + (s.nz - 1)


class SmallScatter:
    def __init__(self, s, here, sems, whole, m0, m1, m2, m3):
        self.s, self.here, self.sems = s, here, sems
        self.whole, self.m0, self.m1, self.m2, self.m3 = whole, m0, m1, m2, m3
        self.sent = {}

    def launch(self, stage, copies):
        for copy in copies:
            copy.start()
        self.sent[stage] = copies

    def landed(self, stage):
        for copy in self.sent[stage]:
            copy.wait_recv()

    def stage(self, n, out=None):
        here, s = self.here, self.s
        z, y, c, x = here.z, here.y, here.c, here.x
        whole, m0, m1, m2, m3 = self.whole, self.m0, self.m1, self.m2, self.m3
        if n == 0:
            self.launch(0, [self.sems.copy(whole.at[:, :, 1 - c], m0, here.at(c=1 - c))])
        elif n == 1:
            self.landed(0)
            for zz in range(s.nz):
                for yy in range(2):
                    for xx in range(s.nx):
                        m0[zz, yy, xx] = m0[zz, yy, xx] + whole[zz, yy, c, xx]
            self.launch(1, [self.sems.copy(m0.at[:, :, p], m1.at[d], here.at(x=p)) for d, p in enumerate(here.xs())])
        elif n == 2:
            self.landed(1)
            for zz in range(s.nz):
                for yy in range(2):
                    got = m0[zz, yy, x]
                    for d in range(s.nx - 1):
                        got = got + m1[d, zz, yy]
                    m1[0, zz, yy] = got
            self.launch(2, [self.sems.copy(m1.at[0, :, 1 - y], m2, here.at(y=1 - y))])
        elif n == 3:
            self.landed(2)
            for zz in range(s.nz):
                m2[zz] = m2[zz] + m1[0, zz, y]
            self.launch(3, [self.sems.copy(m2.at[p], m3.at[d], here.at(z=p)) for d, p in enumerate(here.zs())])
        else:
            self.landed(3)
            got = m2[z]
            for d in range(s.nz - 1):
                got = got + m3[d]
            out[...] = got

    def finish(self):
        for copies in self.sent.values():
            for copy in copies:
                copy.wait_send()


def split_three(value):
    high = value.astype(BF)
    rest = value - high.astype(F32)
    middle = rest.astype(BF)
    return high, middle, (rest - middle.astype(F32)).astype(BF)


def pack_vectors(vec, packed, s, late):
    unit = s.width // s.count
    total = PACK * unit
    acc = packed[:, :, :, :, 0, :].reshape(s.count, total) if late else jnp.zeros((s.count, total), F32)
    for row, (name, start, times) in enumerate(VECS):
        if name.startswith("ln1") != late:
            continue
        per = unit * times
        shift = per.bit_length() - 1
        for lo in range(0, s.width * times, s.width):
            index = lax.broadcasted_iota(jnp.int32, (s.width, total), 0) + lo
            target = lax.broadcasted_iota(jnp.int32, (s.width, total), 1) - start * unit
            pick = ((index & (per - 1)) == target).astype(F32).astype(BF)
            owner = lax.shift_right_logical(lax.broadcasted_iota(jnp.int32, (s.count, s.width), 1) + lo, shift)
            mine = owner == lax.broadcasted_iota(jnp.int32, (s.count, s.width), 0)
            spread = jnp.where(mine, vec[row : row + 1, lo : lo + s.width], 0.0)
            parts = jnp.concatenate(split_three(spread), axis=0)
            moved = nn(parts, pick)
            acc = acc + (moved[: s.count] + moved[s.count : 2 * s.count] + moved[2 * s.count :])
    packed[...] = jnp.broadcast_to(acc[:, None, :], (s.count, 8, total)).reshape(s.nz, 2, 2, s.nx, 8, total)


def attend_back(s, span, k0, q0, row0, count, qkv, grad_out, dqkv, p_slot, p_in, p_sem):
    width, frame = s.width, s.frame
    low = lax.broadcasted_iota(jnp.int32, (1, LANES), 1) < HEAD_DIM
    zero = jnp.zeros((), BF)
    first, end = span

    def in_copy(step, slot):
        return pltpu.make_async_copy(
            p_in.at[pl.ds(step * 4, 4), pl.ds(row0, count), :],
            p_slot.at[slot, :, pl.ds(0, count), :],
            p_sem.at[slot],
        )

    in_copy(first, first % 2).start()

    def body(step, carry):
        slot = lax.rem(step, 2)

        @pl.when(step + 1 < end)
        def _():
            in_copy(step + 1, 1 - slot).start()

        in_copy(step, slot).wait()
        for pair in range(2):
            col = pl.multiple_of((step * 2 + pair) * LANES, LANES)
            q2 = qkv[pl.ds(q0, count), pl.ds(col, LANES)]
            k2 = qkv[pl.ds(frame + k0, L), pl.ds(col, LANES)]
            v2 = qkv[pl.ds(2 * frame + k0, L), pl.ds(col, LANES)]
            g2 = grad_out[pl.ds(row0, count), pl.ds(col, LANES)]
            dq = dk = dv = None
            for head in range(2):
                sel = low if head == 0 else jnp.logical_not(low)
                probs = p_slot[slot, pair * 2 + head, pl.ds(0, count), :]
                grad = jnp.where(sel, g2, zero)
                dprobs = nt(grad, v2)
                wide = probs.astype(F32)
                rowdot = jnp.sum(dprobs * wide, axis=-1, keepdims=True)
                dscores = (wide * (dprobs - rowdot)).astype(BF)
                more = (nn(dscores, jnp.where(sel, k2, zero)), tn(dscores, jnp.where(sel, q2, zero)), tn(probs, grad))
                dq, dk, dv = more if dq is None else (dq + more[0], dk + more[1], dv + more[2])
            scale = HEAD_DIM**-0.5
            dqkv[pl.ds(q0, count), pl.ds(col, LANES)] = (dq * scale).astype(BF)
            dqkv[pl.ds(k0, L), pl.ds(col + width, LANES)] = (dk * scale).astype(BF)
            dqkv[pl.ds(k0, L), pl.ds(col + 2 * width, LANES)] = dv.astype(BF)
        return carry

    lax.fori_loop(first, end, body, 0)


def fold_rows(value):
    return jnp.sum(value.reshape(-1, 8, value.shape[-1]), axis=0)


CHUNK = 512
BACK_BUDGET = 3.0


def backward_chunks(s):
    out = [(3, i) for i in range(s.width * (s.hidden // s.width) // CHUNK)]
    out += [(2, i) for i in range(s.hidden // CHUNK)]
    out += [(1, i) for i in range(s.width // CHUNK)]
    out += [(0, i) for i in range(3 * s.width // CHUNK)]
    return out


def backward_copies(s):
    return Scatter.copies(s) * len(backward_chunks(s)) + small_scatter_copies(s) + 1


def backward_kernel(
    s,
    x_ref,
    own_valid,
    cot_ref,
    n1_ref,
    qkv_ref,
    attn_ref,
    r1_ref,
    n2_ref,
    act_ref,
    slope_ref,
    p_ref,
    wq_ref,
    wp_ref,
    w1_ref,
    w2_ref,
    vec,
    out_ref,
    dwq_out,
    dwp_out,
    dw1_out,
    dw2_out,
    small_out,
    buf_a,
    buf_b,
    tall,
    broad,
    wide_a,
    wide_b,
    grad_b,
    mid,
    attn,
    n1f,
    p_slot,
    edge_send,
    edge_in,
    sums,
    packed,
    m0,
    m1,
    m2,
    m3,
    small_fin,
    g,
    l0,
    l1a,
    l1b,
    l2a,
    l2b,
    s2,
    l3,
    fin,
    send,
    recv,
    load_sem,
    p_sem,
    fin_sem,
    credit,
):
    here = Place(s.nz, s.nx)
    sems = Sems(send, recv)
    odd, width, part, half, frame, hidden = here.odd, s.width, s.part, s.half, s.frame, s.hidden
    off = pl.multiple_of(odd * half, 32)
    slots = iter(range(load_sem.shape[0]))

    def load(src, dst):
        copy = pltpu.make_async_copy(src, dst, load_sem.at[next(slots)])
        copy.start()
        return copy

    cot_load = load(cot_ref, grad_b)
    act_load = load(act_ref, buf_a.at[pl.ds(0, part), :])
    pending = {}

    def load_piece(i):
        if i < hidden // 512:
            at = pl.ds(i * 512, 512)
            pending["piece", i] = [load(w2_ref.at[at, :], tall.at[at, :]), load(slope_ref.at[:, at], buf_b.at[:, at])]

    def load_later(i):
        if i == 0:
            pending["n2"] = load(n2_ref, mid)
        elif i <= width // 256:
            at = pl.ds((i - 1) * 256, 256)
            pending["w1", i - 1] = load(w1_ref.at[at, :], broad.at[at, :])
        elif i == width // 256 + 1:
            pending["r1"] = load(r1_ref, wide_a.at[pl.ds(0, part), :])
            pending["attn"] = load(attn_ref, attn)

    for i in range(3):
        load_piece(i)

    chunks = backward_chunks(s)
    total = len(chunks)
    scatter = Scatter(s, here, sems, g, l0, l1a, l1b, l2a, l2b, s2, l3, fin, credit, fin_sem, total)
    small = SmallScatter(s, here, sems, packed, m0, m1, m2, m3)
    here.greet()

    def name(key, value, times=1):
        sums[ROW[key] : ROW[key] + 1, : width * times] = value

    def prepare():
        cot_load.wait()

        def body(i, carry):
            rows = pl.ds(pl.multiple_of(i * 32, 32), 32)
            grad_b[rows, :] = (grad_b[rows, :].astype(F32) * own_valid[rows, :]).astype(BF)
            return carry

        lax.fori_loop(0, part // 32, body, 0)
        act_load.wait()

    ratio = hidden // width
    narrow = CHUNK // ratio
    deep = hidden // s.nz

    def down_grad(i):
        lo = i * narrow

        def body(zz, carry):
            rows = pl.ds(pl.multiple_of(zz * deep, deep), deep)
            got = tn(buf_a[pl.ds(0, part), rows], grad_b[:, lo : lo + 2 * narrow]).astype(BF)
            got = got.reshape(2, 2, s.nx, ratio, s.rows, 2 * narrow)
            for half_of in range(2):
                slot = (i + half_of) % scatter.G_SLOTS
                for q in range(ratio):
                    cut = got[:, :, :, q, :, half_of * narrow : (half_of + 1) * narrow]
                    g[slot, zz, :, :, :, :, q * narrow : (q + 1) * narrow] = cut
            return carry

        lax.fori_loop(0, s.nz, body, 0)

    def grad_tile(lhs, rhs, k):
        got = tn(lhs, rhs).astype(BF)
        g[k % scatter.G_SLOTS] = got.reshape(s.nz, 2, 2, s.nx, s.rows, CHUNK)

    def hidden_grad(i):
        lo = i * 512
        wide_b[:, :512] = nt(grad_b[...], tall[lo : lo + 512, :])

        def body(j, carry):
            rows = pl.ds(pl.multiple_of(j * 32, 32), 32)
            got = wide_b[rows, :512] * buf_b[rows, lo : lo + 512].astype(F32)
            buf_b[rows, lo : lo + 512] = got.astype(BF)
            return carry + fold_rows(got)

        folded = lax.fori_loop(0, part // 32, body, jnp.zeros((8, 512), F32))
        sums[ROW["fc1b"] : ROW["fc1b"] + 1, lo : lo + 512] = jnp.sum(folded, axis=0, keepdims=True)

    def second_norm_product(lo):
        wide_b[:, lo : lo + 256] = nt(buf_b[...], broad[lo : lo + 256, :])

    def second_norm_back():
        ones = jnp.ones((8, part), BF)
        name("fc2b", nn(ones, grad_b[...])[0:1])
        gain = vec[ROW["ln2g"] : ROW["ln2g"] + 1, :width]

        def body(i, carry):
            rows = pl.ds(pl.multiple_of(i * 32, 32), 32)
            unit, inverse = norm_stats(wide_a[rows, :])
            got = wide_b[rows, :]
            u = got * gain
            back = u - jnp.mean(u, axis=-1, keepdims=True) - unit * jnp.mean(u * unit, axis=-1, keepdims=True)
            back = grad_b[rows, :].astype(F32) + inverse * back
            wide_b[rows, :] = back
            n1f[rows, :] = back.astype(BF)
            return carry[0] + fold_rows(got * unit), carry[1] + fold_rows(got), carry[2] + fold_rows(back)

        zeros = jnp.zeros((8, width), F32)
        gain_sum, shift_sum, bias_sum = lax.fori_loop(0, part // 32, body, (zeros, zeros, zeros))
        name("ln2g", jnp.sum(gain_sum, axis=0, keepdims=True))
        name("ln2b", jnp.sum(shift_sum, axis=0, keepdims=True))
        name("projb", jnp.sum(bias_sum, axis=0, keepdims=True))

    def attention_grad():
        for lo in range(0, width, 512):
            grad_b[:, lo : lo + 512] = nt(n1f[:part, :], tall[3 * frame + lo : 3 * frame + lo + 512, :]).astype(BF)

    def first_norm_product(lo):
        got = nt(buf_a[:, : 3 * width], broad[lo : lo + 256, : 3 * width])
        wide_a[:, lo : lo + 256] = got

    def first_norm_back():
        gain = vec[ROW["ln1g"] : ROW["ln1g"] + 1, :width]

        def body(i, carry):
            rows = pl.ds(pl.multiple_of(i * 32, 32), 32)
            framed = pl.ds(pl.multiple_of(i * 32 + off, 32), 32)
            unit, inverse = norm_stats(attn[rows, :].astype(F32))
            got = wide_a[framed, :]
            u = got * gain
            back = u - jnp.mean(u, axis=-1, keepdims=True) - unit * jnp.mean(u * unit, axis=-1, keepdims=True)
            mid[rows, :] = (wide_b[rows, :] + inverse * back).astype(BF)
            return carry[0] + fold_rows(got * unit), carry[1] + fold_rows(got)

        zeros = jnp.zeros((8, width), F32)
        gain_sum, shift_sum = lax.fori_loop(0, part // 32, body, (zeros, zeros))
        name("ln1g", jnp.sum(gain_sum, axis=0, keepdims=True))
        name("ln1b", jnp.sum(shift_sum, axis=0, keepdims=True))

    far = pl.multiple_of(part * (1 - odd), 32)
    near = pl.multiple_of((part - half) * (1 - odd) + half * odd, 32)
    edge = sems.copy(edge_send, edge_in, here.partner())

    def send_edge():
        edge_send[...] = wide_a[pl.ds(far, half), :].astype(BF)
        edge.start()

    def take_edge():
        edge.wait_recv()
        wide_a[pl.ds(near, half), :] = wide_a[pl.ds(near, half), :] + edge_in[...].astype(F32)

    def bias_grad():
        ones = jnp.ones((8, frame), BF)
        for third in (0, 2):
            got = nn(ones, buf_a[:, third * width : (third + 1) * width])[0:1]
            sums[ROW["qvb"] : ROW["qvb"] + 1, (third // 2) * width : (third // 2 + 1) * width] = got

    marks = {"hidden": 0, "mid": False, "attention": False, "out": False}

    def chunk(k):
        w, i = chunks[k]
        if w == 3:
            if i % 2 == 0:
                scatter.free_g(k)
                scatter.free_g(k + 1)
                down_grad(i)
            return
        scatter.free_g(k)
        cols = pl.ds(i * CHUNK, CHUNK)
        if w == 2:
            if i == 0:
                pending["n2"].wait()
            grad_tile(mid[...], buf_b[:, cols], k)
        elif w == 1:
            if i == 0:
                pending["attn"].wait()
            grad_tile(attn[...], n1f[:part, cols], k)
            if i == width // CHUNK - 1:
                pending["x"] = load(x_ref, attn)
                pending["n1"] = load(n1_ref, n1f)
        else:
            if i == 0:
                pending["n1"].wait()
            grad_tile(n1f[...], buf_a[:, cols], k)

    def hidden_task(i):
        for copy in pending["piece", i]:
            copy.wait()
        load_piece(i + 3)
        load_later(i)
        hidden_grad(i)
        marks["hidden"] = i + 1
        if i == hidden // 512 - 1:
            pending["wp"] = load(wp_ref, tall.at[pl.ds(3 * frame, width), :])
            pending["qkv"] = [load(qkv_ref.at[:, pl.ds(t * width, width)], tall.at[pl.ds(t * frame, frame), :]) for t in range(3)]

    def product_task(i):
        pending["w1", i].wait()
        second_norm_product(i * 256)
        if i == width // 256 - 1:
            pending["wq"] = load(wq_ref, broad.at[:, pl.ds(0, 3 * width)])

    def mid_task():
        pending["r1"].wait()
        second_norm_back()
        marks["mid"] = True

    def attention_grad_task():
        pending["wp"].wait()
        attention_grad()
        for copy in pending["qkv"]:
            copy.wait()
        buf_a[pl.ds(far, half), :width] = jnp.zeros((half, width), BF)

    def image_task(i, span):
        k0 = pl.multiple_of((i + odd) * L, 32)
        row0 = pl.multiple_of(i * L + odd * half, 32)
        attend_back(s, span, k0, k0, row0, L, tall, grad_b, buf_a, p_slot, p_ref, p_sem)

    def edge_task(span):
        k0 = pl.multiple_of(s.whole * L * (1 - odd), 32)
        q0 = pl.multiple_of(s.whole * L * (1 - odd) + half * odd, 32)
        attend_back(s, span, k0, q0, k0, half, tall, grad_b, buf_a, p_slot, p_ref, p_sem)
        marks["attention"] = span[1] == HEADS // 4

    def first_product_task(i):
        if i == 0:
            pending["wq"].wait()
        first_norm_product(i * 256)

    def edge_rows_task():
        send_edge()
        bias_grad()
        pack_vectors(sums, packed, s, False)

    def first_task():
        take_edge()
        pending["x"].wait()
        first_norm_back()
        pending["out"] = load(mid, out_ref)

    def pack_task():
        pack_vectors(sums, packed, s, True)
        small.stage(0)
        marks["out"] = True

    downs = sum(w == 3 for w, _ in chunks)
    ups = sum(w == 2 for w, _ in chunks)
    tasks = [(0, 1.8, functools.partial(hidden_task, i)) for i in range(hidden // 512)]
    tasks += [(0, 2.1, functools.partial(product_task, i)) for i in range(width // 256)]
    tasks += [(0, 4.0, mid_task), (downs - 1, 2.5, attention_grad_task)]
    spans = ((0, HEADS // 8), (HEADS // 8, HEADS // 4))
    for i in range(s.whole):
        tasks += [(downs - 1, 4.3, functools.partial(image_task, i, span)) for span in spans]
    tasks += [(downs - 1, 3.7, functools.partial(edge_task, span)) for span in spans]
    tasks += [(0, 1.9, functools.partial(first_product_task, i)) for i in range(width // 256)]
    tasks += [(0, 1.0, edge_rows_task), (downs + ups + width // CHUNK, 3.5, first_task), (0, 1.0, pack_task)]

    def needs(k):
        w, i = chunks[k]
        if w == 3:
            return False
        if w == 2:
            return marks["hidden"] * 512 < (i + 1) * CHUNK
        if w == 1:
            return not marks["mid"]
        return not marks["attention"]

    outs = (dwq_out, dwp_out, dw1_out, dw2_out)

    def targets(j):
        w, i = chunks[j]

        def pairs(slot):
            if w == 3:
                return [
                    (slot.at[:, pl.ds(q * narrow, narrow)], outs[3].at[pl.ds(q * s.rows, s.rows), pl.ds(i * narrow, narrow)])
                    for q in range(ratio)
                ]
            return [(slot, outs[w].at[:, pl.ds(i * CHUNK, CHUNK)])]

        return pairs

    prepare()
    k, small_stage = 0, 0
    stages = (scatter.stage0, scatter.stage1, scatter.stage2, scatter.stage3)
    while k < total + scatter.OFFSET[4] or small_stage < 4:
        if k < total:
            while needs(k):
                tasks.pop(0)[2]()
            chunk(k)
            scatter.stage0(k)
        j = k - scatter.OFFSET[4]
        if 0 <= j < total:
            scatter.stage4(j, targets(j))
        for n in (3, 2, 1):
            j = k - scatter.OFFSET[n]
            if 0 <= j < total:
                stages[n](j)
        if marks["out"] and small_stage < 4:
            small_stage += 1
            small.stage(small_stage, small_fin)
        budget = BACK_BUDGET
        while tasks and budget > 0 and tasks[0][0] <= k:
            _, cost, task = tasks.pop(0)
            task()
            budget -= cost
        k += 1
    final = pltpu.make_async_copy(small_fin, small_out, p_sem.at[0])
    final.start()
    scatter.finish()
    small.finish()
    edge.wait_send()
    pending["out"].wait()
    final.wait()


def backward_call(s, x, own_valid, cot, n1f, qkvf, attn, r1, n2, act, slope, p, wq, wp, w1, w2, vec):
    anyspace = pl.BlockSpec(memory_space=pl.ANY)
    vmem = pl.BlockSpec(memory_space=pltpu.VMEM)
    shape = lambda dims, kind=F32: jax.ShapeDtypeStruct(dims, kind)
    part, width, hidden, rows, nz, nx, frame = s.part, s.width, s.hidden, s.rows, s.nz, s.nx, s.frame
    total = PACK * rows
    outs = [
        shape((part, width), BF),
        shape((rows, 3 * width)),
        shape((rows, width)),
        shape((rows, hidden)),
        shape((hidden // s.count, width)),
        shape((8, total)),
    ]
    copies = backward_copies(s)
    ring = Scatter.RING
    scratch = [
        pltpu.VMEM((frame, hidden), BF),
        pltpu.VMEM((part, hidden), BF),
        pltpu.VMEM((hidden, width), BF),
        pltpu.VMEM((width, hidden), BF),
        pltpu.VMEM((frame, width), F32),
        pltpu.VMEM((part, width), F32),
        pltpu.VMEM((part, width), BF),
        pltpu.VMEM((part, width), BF),
        pltpu.VMEM((part, width), BF),
        pltpu.VMEM((frame, width), BF),
        pltpu.VMEM((2, 4, L, L), BF),
        pltpu.VMEM((s.half, width), BF),
        pltpu.VMEM((s.half, width), BF),
        pltpu.VMEM((8, hidden), F32),
        pltpu.VMEM((nz, 2, 2, nx, 8, total), F32),
        pltpu.VMEM((nz, 2, nx, 8, total), F32),
        pltpu.VMEM((nx - 1, nz, 2, 8, total), F32),
        pltpu.VMEM((nz, 8, total), F32),
        pltpu.VMEM((nz - 1, 8, total), F32),
        pltpu.VMEM((8, total), F32),
        pltpu.VMEM((Scatter.G_SLOTS, nz, 2, 2, nx, rows, CHUNK), BF),
        pltpu.VMEM((ring[0], nz, 2, nx, rows, CHUNK), BF),
        pltpu.VMEM((ring[1], nz, nx, rows, CHUNK // 2), BF),
        pltpu.VMEM((ring[1], nx - 1, nz, 2, rows, CHUNK // 2), BF),
        pltpu.VMEM((ring[2], nx - 1, nz, rows, CHUNK // 2), BF),
        pltpu.VMEM((ring[2], nz, rows, CHUNK // 2), BF),
        pltpu.VMEM((ring[3], nz, rows, CHUNK), BF),
        pltpu.VMEM((ring[3], nz - 1, rows, CHUNK), BF),
        pltpu.VMEM((2, rows, CHUNK), F32),
        pltpu.SemaphoreType.DMA((copies,)),
        pltpu.SemaphoreType.DMA((copies,)),
        pltpu.SemaphoreType.DMA((16 + 2 * (hidden // 512) + width // 256,)),
        pltpu.SemaphoreType.DMA((2,)),
        pltpu.SemaphoreType.DMA((2, hidden // width)),
        pltpu.SemaphoreType.REGULAR((2 * nx + nz,)),
    ]
    return pl.pallas_call(
        functools.partial(backward_kernel, s),
        out_shape=outs,
        in_specs=[anyspace, vmem] + [anyspace] * 13 + [vmem],
        out_specs=[anyspace] * len(outs),
        scratch_shapes=scratch,
        name="backward",
        compiler_params=pltpu.CompilerParams(collective_id=1, has_side_effects=True, vmem_limit_bytes=63 * MIB),
    )(x, own_valid, cot, n1f, qkvf, attn, r1, n2, act, slope, p, wq, wp, w1, w2, vec)


def layer_norm(value, gain, shift):
    mean = jnp.mean(value, axis=-1, keepdims=True)
    centred = value - mean
    inverse = lax.rsqrt(jnp.mean(centred * centred, axis=-1, keepdims=True) + 1e-06)
    unit = centred * inverse
    return (unit * gain + shift, unit, inverse)


def norm_back(grad_out, unit, inverse, gain):
    scaled = grad_out * gain
    grad_in = inverse * (
        scaled
        - jnp.mean(scaled, axis=-1, keepdims=True)
        - unit * jnp.mean(scaled * unit, axis=-1, keepdims=True)
    )
    return (grad_in, jnp.sum(grad_out * unit, axis=0), jnp.sum(grad_out, axis=0))


def split_heads(block, head_count):
    return block.reshape(block.shape[0], block.shape[1], head_count, -1)


def masked_scores(query, keyed, valid, scale):
    scores = jnp.einsum("gqhd,gkhd->ghqk", query, keyed, preferred_element_type=jnp.float32) * scale
    return jnp.where(valid[:, None, None, :] > 0, scores, -1e30)


def plain_shards(
    tokens,
    keep_mask,
    ln1_gain,
    ln1_bias,
    qkv_weight,
    qv_bias,
    proj_weight,
    proj_bias,
    ln2_gain,
    ln2_bias,
    fc1_weight,
    fc1_bias,
    fc2_weight,
    fc2_bias,
    cotangent,
):
    f32 = jnp.float32
    bf16 = jnp.bfloat16
    n_seq = lax.axis_size("seq")
    seq_count, part_len, width = tokens.shape
    seq_len = part_len * n_seq
    img_len = L
    head_local = HEADS // n_seq
    head_width = width // n_seq
    scale = HEAD_DIM ** (-0.5)
    rows = seq_count * part_len
    image_count = keep_mask.shape[0]
    per_group = 1
    pair_count = image_count // per_group
    valid = jnp.concatenate([jnp.ones((image_count, BUF), f32), keep_mask.astype(f32)], axis=1)
    seq_valid = valid.reshape(seq_count, seq_len)
    own_valid = lax.dynamic_slice_in_dim(
        seq_valid, lax.axis_index("seq") * part_len, part_len, 1
    ).reshape(rows, 1)
    valid_pairs = valid.reshape(pair_count, per_group, img_len)
    params = (
        lax.all_gather(ln1_gain, ("fsdp", "seq"), axis=0, tiled=True),
        lax.all_gather(ln1_bias, ("fsdp", "seq"), axis=0, tiled=True),
        lax.all_gather(qkv_weight, ("fsdp", "seq"), axis=0, tiled=True),
        lax.all_gather(qv_bias, ("fsdp", "seq"), axis=0, tiled=True),
        lax.all_gather(proj_weight, ("fsdp", "seq"), axis=0, tiled=True),
        lax.all_gather(proj_bias, ("fsdp", "seq"), axis=0, tiled=True),
        lax.all_gather(ln2_gain, ("fsdp", "seq"), axis=0, tiled=True),
        lax.all_gather(ln2_bias, ("fsdp", "seq"), axis=0, tiled=True),
        lax.all_gather(fc1_weight, ("fsdp", "seq"), axis=0, tiled=True),
        lax.all_gather(fc1_bias, ("fsdp", "seq"), axis=0, tiled=True),
        lax.all_gather(fc2_weight, ("fsdp", "seq"), axis=0, tiled=True),
        lax.all_gather(fc2_bias, ("fsdp", "seq"), axis=0, tiled=True),
    )
    (
        gain_one,
        shift_one,
        w_qkv,
        bias_qv,
        w_proj,
        bias_proj,
        gain_two,
        shift_two,
        w_up,
        bias_up,
        w_down,
        bias_down,
    ) = params
    inputs = tokens.astype(f32).reshape(rows, width)
    normed, unit_one, inv_one = layer_norm(inputs, gain_one.astype(f32), shift_one.astype(f32))
    normed_b = normed.astype(bf16)
    bias_qv = bias_qv.astype(f32)
    full_bias = jnp.concatenate([bias_qv[:width], jnp.zeros((width,), f32), bias_qv[width:]])
    qkv = (jnp.dot(normed_b, w_qkv, preferred_element_type=f32) + full_bias).astype(bf16)
    heads = lax.all_to_all(
        qkv.reshape(seq_count, part_len, 3, width), "seq", split_axis=3, concat_axis=1, tiled=True
    )
    pairs = heads.reshape(pair_count, per_group, img_len, 3, head_width)

    def attend(group):
        block, mask = group
        query = split_heads(block[:, :, 0], head_local)
        keyed = split_heads(block[:, :, 1], head_local)
        values = split_heads(block[:, :, 2], head_local)
        scores = masked_scores(query, keyed, mask, scale)
        top = jnp.max(scores, axis=-1, keepdims=True)
        expo = jnp.exp(scores - top)
        total = jnp.sum(expo, axis=-1, keepdims=True)
        probs = (expo / total).astype(bf16)
        mixed = jnp.einsum("ghqk,gkhd->gqhd", probs, values, preferred_element_type=f32)
        return (
            mixed.reshape(per_group, img_len, head_width).astype(bf16),
            (top + jnp.log(total))[..., 0],
        )

    attn_heads, log_totals = lax.map(attend, (pairs, valid_pairs))
    attn_heads = attn_heads.reshape(seq_count, seq_len, head_width)
    attn_local = lax.all_to_all(attn_heads, "seq", split_axis=1, concat_axis=2, tiled=True).reshape(
        rows, width
    )
    resid = inputs + jnp.dot(attn_local, w_proj, preferred_element_type=f32) + bias_proj.astype(f32)
    normed_two, unit_two, inv_two = layer_norm(resid, gain_two.astype(f32), shift_two.astype(f32))
    normed_two_b = normed_two.astype(bf16)
    hidden = jnp.dot(normed_two_b, w_up, preferred_element_type=f32) + bias_up.astype(f32)
    act, gelu_pull = jax.vjp(lambda value: jax.nn.gelu(value, approximate=False), hidden)
    act_b = act.astype(bf16)
    branch = jnp.dot(act_b, w_down, preferred_element_type=f32) + bias_down.astype(f32)
    layer_out = (own_valid * (resid + branch)).astype(bf16).reshape(seq_count, part_len, width)
    gain_one, w_qkv, w_proj, gain_two, w_up, w_down = (
        lax.all_gather(ln1_gain, ("fsdp", "seq"), axis=0, tiled=True),
        lax.all_gather(qkv_weight, ("fsdp", "seq"), axis=0, tiled=True),
        lax.all_gather(proj_weight, ("fsdp", "seq"), axis=0, tiled=True),
        lax.all_gather(ln2_gain, ("fsdp", "seq"), axis=0, tiled=True),
        lax.all_gather(fc1_weight, ("fsdp", "seq"), axis=0, tiled=True),
        lax.all_gather(fc2_weight, ("fsdp", "seq"), axis=0, tiled=True),
    )
    grad = own_valid * cotangent.astype(f32).reshape(rows, width)
    down_bias_grad = jnp.sum(grad, axis=0)
    grad_b = grad.astype(bf16)
    down_grad = jnp.dot(act_b.T, grad_b, preferred_element_type=f32)
    grad_act = jnp.dot(grad_b, w_down.T, preferred_element_type=f32)
    grad_hidden = gelu_pull(grad_act)[0]
    up_bias_grad = jnp.sum(grad_hidden, axis=0)
    grad_hidden_b = grad_hidden.astype(bf16)
    up_grad = jnp.dot(normed_two_b.T, grad_hidden_b, preferred_element_type=f32)
    grad_normed_two = jnp.dot(grad_hidden_b, w_up.T, preferred_element_type=f32)
    grad_resid_ln, gain_two_grad, shift_two_grad = norm_back(
        grad_normed_two, unit_two, inv_two, gain_two.astype(f32)
    )
    grad_resid = grad + grad_resid_ln
    proj_bias_grad = jnp.sum(grad_resid, axis=0)
    grad_resid_b = grad_resid.astype(bf16)
    proj_grad = jnp.dot(attn_local.T, grad_resid_b, preferred_element_type=f32)
    grad_attn = jnp.dot(grad_resid_b, w_proj.T, preferred_element_type=f32).astype(bf16)
    grad_heads = lax.all_to_all(
        grad_attn.reshape(seq_count, part_len, width),
        "seq",
        split_axis=2,
        concat_axis=1,
        tiled=True,
    )
    grad_pairs = grad_heads.reshape(pair_count, per_group, img_len, head_width)

    def attend_back(group):
        block, mask, lse, grad_mixed = group
        query = split_heads(block[:, :, 0], head_local)
        keyed = split_heads(block[:, :, 1], head_local)
        values = split_heads(block[:, :, 2], head_local)
        grad_out = split_heads(grad_mixed, head_local)
        scores = masked_scores(query, keyed, mask, scale)
        probs = jnp.exp(scores - lse[..., None])
        dprobs = jnp.einsum("gqhd,gkhd->ghqk", grad_out, values, preferred_element_type=f32)
        grad_values = jnp.einsum(
            "ghqk,gqhd->gkhd", probs.astype(bf16), grad_out, preferred_element_type=f32
        )
        rowdot = jnp.sum(dprobs * probs, axis=-1, keepdims=True)
        grad_scores = (probs * (dprobs - rowdot)).astype(bf16)
        grad_query = (
            jnp.einsum("ghqk,gkhd->gqhd", grad_scores, keyed, preferred_element_type=f32) * scale
        )
        grad_keyed = (
            jnp.einsum("ghqk,gqhd->gkhd", grad_scores, query, preferred_element_type=f32) * scale
        )
        stacked = jnp.stack(
            [
                grad_query.reshape(per_group, img_len, head_width),
                grad_keyed.reshape(per_group, img_len, head_width),
                grad_values.reshape(per_group, img_len, head_width),
            ],
            axis=2,
        )
        return stacked.astype(bf16)

    grad_qkv_heads = lax.map(attend_back, (pairs, valid_pairs, log_totals, grad_pairs))
    grad_qkv_heads = grad_qkv_heads.reshape(seq_count, seq_len, 3, head_width)
    grad_qkv = lax.all_to_all(
        grad_qkv_heads, "seq", split_axis=1, concat_axis=3, tiled=True
    ).reshape(rows, 3 * width)
    column_sums = jnp.sum(grad_qkv.astype(f32), axis=0)
    qv_grad = jnp.concatenate([column_sums[:width], column_sums[2 * width :]])
    qkv_grad = jnp.dot(normed_b.T, grad_qkv, preferred_element_type=f32)
    grad_normed = jnp.dot(grad_qkv, w_qkv.T, preferred_element_type=f32)
    grad_in_ln, gain_one_grad, shift_one_grad = norm_back(
        grad_normed, unit_one, inv_one, gain_one.astype(f32)
    )
    tokens_grad = (grad_resid + grad_in_ln).astype(bf16).reshape(seq_count, part_len, width)
    summed = (
        lax.psum_scatter(gain_one_grad, ("fsdp", "seq"), scatter_dimension=0, tiled=True),
        lax.psum_scatter(shift_one_grad, ("fsdp", "seq"), scatter_dimension=0, tiled=True),
        lax.psum_scatter(qkv_grad, ("fsdp", "seq"), scatter_dimension=0, tiled=True),
        lax.psum_scatter(qv_grad, ("fsdp", "seq"), scatter_dimension=0, tiled=True),
        lax.psum_scatter(proj_grad, ("fsdp", "seq"), scatter_dimension=0, tiled=True),
        lax.psum_scatter(proj_bias_grad, ("fsdp", "seq"), scatter_dimension=0, tiled=True),
        lax.psum_scatter(gain_two_grad, ("fsdp", "seq"), scatter_dimension=0, tiled=True),
        lax.psum_scatter(shift_two_grad, ("fsdp", "seq"), scatter_dimension=0, tiled=True),
        lax.psum_scatter(up_grad, ("fsdp", "seq"), scatter_dimension=0, tiled=True),
        lax.psum_scatter(up_bias_grad, ("fsdp", "seq"), scatter_dimension=0, tiled=True),
        lax.psum_scatter(down_grad, ("fsdp", "seq"), scatter_dimension=0, tiled=True),
        lax.psum_scatter(down_bias_grad, ("fsdp", "seq"), scatter_dimension=0, tiled=True),
    )
    return (
        layer_out,
        tokens_grad,
        summed[0],
        summed[1],
        summed[2],
        summed[3],
        summed[4],
        summed[5],
        summed[6],
        summed[7],
        summed[8],
        summed[9],
        summed[10],
        summed[11],
    )


def shards(
    tokens,
    keep_mask,
    ln1_gain,
    ln1_bias,
    qkv_weight,
    qv_bias,
    proj_weight,
    proj_bias,
    ln2_gain,
    ln2_bias,
    fc1_weight,
    fc1_bias,
    fc2_weight,
    fc2_bias,
    cotangent,
):
    n_fsdp, n_seq = lax.axis_size("fsdp"), lax.axis_size("seq")
    s = Sizes(n_fsdp // 4, n_seq, tokens.shape[1], tokens.shape[2], fc1_weight.shape[1])
    if not s.fits(tokens.shape[0]):
        return plain_shards(
            tokens,
            keep_mask,
            ln1_gain,
            ln1_bias,
            qkv_weight,
            qv_bias,
            proj_weight,
            proj_bias,
            ln2_gain,
            ln2_bias,
            fc1_weight,
            fc1_bias,
            fc2_weight,
            fc2_bias,
            cotangent,
        )
    framed, own = frames(s, keep_mask)
    small = pack_small(s, ln1_gain, ln1_bias, proj_bias, ln2_gain, ln2_bias, fc2_bias, qv_bias, fc1_bias)
    x = tokens.reshape(s.part, s.width)
    cot = cotangent.reshape(s.part, s.width)
    out, n1f, qkvf, attn, r1, n2, act, slope, p, wq, wp, w1, w2, vec = forward_call(
        s, x, framed, own, small, qkv_weight, proj_weight, fc1_weight, fc2_weight
    )
    flat = [w.reshape(-1, w.shape[-1]) for w in (wq, wp, w1, w2)]
    back, dwq, dwp, dw1, dw2, vecs = backward_call(s, x, own, cot, n1f, qkvf, attn, r1, n2, act, slope, p, *flat, vec)
    unit = s.rows
    piece = {name: vecs[0, start * unit : (start + times) * unit] for name, start, times in VECS}
    return (
        out.reshape(tokens.shape),
        back.reshape(tokens.shape),
        piece["ln1g"],
        piece["ln1b"],
        dwq,
        piece["qvb"],
        dwp,
        piece["projb"],
        piece["ln2g"],
        piece["ln2b"],
        dw1,
        piece["fc1b"],
        dw2,
        piece["fc2b"],
    )


def solution(mesh):
    rows = P(("fsdp", "seq"))
    weight = P(("fsdp", "seq"), None)
    data = P("fsdp", "seq", None)
    placed = (data, P("fsdp", None), rows, rows, weight, rows, weight, rows, rows, rows, weight, rows, weight, rows, data)
    return jax.shard_map(
        shards,
        mesh=mesh,
        in_specs=placed,
        out_specs=(data, data, rows, rows, weight, rows, weight, rows, rows, rows, weight, rows, weight, rows),
        check_vma=False,
    )
```

```python
import functools
import math

import jax
import jax.numpy as jnp
from jax import lax
from jax.experimental import pallas as pl
from jax.experimental.pallas import tpu as pltpu
from jax.sharding import PartitionSpec as P

HEADS = 16
HEAD_DIM = 64
BUF = 64
L = 320
MESH = pl.DeviceIdType.MESH
BF = jnp.bfloat16
F32 = jnp.float32
LANES = 128
MIB = 2**20


def nn(a, b):
    return lax.dot_general(a, b, (((1,), (0,)), ((), ())), preferred_element_type=F32)


def nt(a, b):
    return lax.dot_general(a, b, (((1,), (1,)), ((), ())), preferred_element_type=F32)


def tn(a, b):
    return lax.dot_general(a, b, (((0,), (0,)), ((), ())), preferred_element_type=F32)


class Place:
    def __init__(self, nz, nx):
        f = lax.axis_index("fsdp")
        self.x = lax.axis_index("seq")
        self.nz, self.nx = nz, nx
        self.z = lax.div(f, 4)
        self.y = lax.rem(lax.div(f, 2), 2)
        self.c = lax.rem(f, 2)
        self.odd = lax.rem(self.x, 2)

    def at(self, z=None, y=None, c=None, x=None):
        z = self.z if z is None else z
        y = self.y if y is None else y
        c = self.c if c is None else c
        x = self.x if x is None else x
        return {"fsdp": (z * 2 + y) * 2 + c, "seq": x}

    def zs(self):
        return [lax.rem(self.z + d, self.nz) for d in range(1, self.nz)]

    def xs(self):
        return [lax.rem(self.x + d, self.nx) for d in range(1, self.nx)]

    def partner(self):
        return self.at(x=self.x + 1 - 2 * self.odd)

    def greet(self):
        peers = [self.at(z=z) for z in self.zs()] + [self.at(x=x) for x in self.xs()]
        peers += [self.at(y=1 - self.y), self.at(c=1 - self.c)]
        barrier = pltpu.get_barrier_semaphore()
        for peer in peers:
            pl.semaphore_signal(barrier, inc=1, device_id=peer, device_id_type=MESH)
        pl.semaphore_wait(barrier, len(peers))


class Sems:
    def __init__(self, send, recv):
        self.send, self.recv, self.used = send, recv, 0

    def copy(self, src, dst, device):
        slot = self.used
        self.used += 1
        return pltpu.make_async_remote_copy(
            src_ref=src,
            dst_ref=dst,
            send_sem=self.send.at[slot],
            recv_sem=self.recv.at[slot],
            device_id=device,
            device_id_type=MESH,
        )


def gather_copies(here, sems, src, buf, rows, cols, early):
    (top, height), (lo, width) = rows, cols
    if height >= width:
        at_a, at_b = (pl.ds(top, height // 2), pl.ds(lo, width)), (pl.ds(top + height // 2, height // 2), pl.ds(lo, width))
    else:
        at_a, at_b = (pl.ds(top, height), pl.ds(lo, width // 2)), (pl.ds(top, height), pl.ds(lo + width // 2, width // 2))
    every = (pl.ds(top, height), pl.ds(lo, width))
    z, y, c, x = here.z, here.y, here.c, here.x
    full = pl.ds(0, here.nz), pl.ds(0, 2), pl.ds(0, here.nx)

    def move(place, part, device):
        ref = buf.at[(*place, *part)]
        return sems.copy(ref, ref, device)

    mine = (z, y, c, x)
    if early:
        first = [sems.copy(src.at[every], buf.at[(*mine, *every)], here.at(z=t)) for t in here.zs()]
        second = [move((full[0], y, c, x), at_a, here.at(x=t)) for t in here.xs()]
        second += [move((full[0], y, c, x), at_b, here.at(y=1 - y))]
    else:
        first = [sems.copy(src.at[at_a], buf.at[(*mine, *at_a)], here.at(x=t)) for t in here.xs()]
        first += [sems.copy(src.at[at_b], buf.at[(*mine, *at_b)], here.at(y=1 - y))]
        second = [move((z, y, c, full[2]), at_a, here.at(z=t)) for t in here.zs()]
        second += [move((z, full[1], c, x), at_b, here.at(z=t)) for t in here.zs()]
    third = [move((full[0], y, c, full[2]), at_a, here.at(y=1 - y))]
    third += [move((full[0], full[1], c, x), at_b, here.at(x=t)) for t in here.xs()]
    last = [move((full[0], full[1], c, full[2]), every, here.at(c=1 - c))]
    return [first, second, third, last]


def small_copies(here, sems, src, buf):
    z, y, c, x = here.z, here.y, here.c, here.x
    first = [sems.copy(src, buf.at[z, y, c, x], here.at(z=t)) for t in here.zs()]
    second = [sems.copy(buf.at[:, y, c, x], buf.at[:, y, c, x], here.at(x=t)) for t in here.xs()]
    third = [sems.copy(buf.at[:, y, c], buf.at[:, y, c], here.at(y=1 - y))]
    last = [sems.copy(buf.at[:, :, c], buf.at[:, :, c], here.at(c=1 - c))]
    return [first, second, third, last]


def gather_count(nz, nx, early):
    if early:
        return (nz - 1) + (nx - 1) + 1 + 1 + (nx - 1) + 1
    return (nx - 1) + 1 + 2 * (nz - 1) + 1 + (nx - 1) + 1


def columns(buf, lo, width):
    part = buf[:, :, :, :, :, pl.ds(lo, width)]
    return part.reshape(-1, width)


def norm_stats(value):
    mean = jnp.mean(value, axis=-1, keepdims=True)
    centred = value - mean
    inverse = lax.rsqrt(jnp.mean(centred * centred, axis=-1, keepdims=True) + 1e-06)
    return centred * inverse, inverse


def gelu_pair(v):
    e = jnp.exp(v * v * (-0.5))
    t = pl.reciprocal(1.0 + (0.3275911 * math.sqrt(0.5)) * jnp.abs(v), approx=False)
    poly = 0.5 * 1.061405429
    for a in (-1.453152027, 1.421413741, -0.284496736, 0.254829592):
        poly = poly * t + 0.5 * a
    tail = poly * t * e
    cdf = jnp.where(v >= 0, 1.0 - tail, tail)
    return v * cdf, cdf + v * e * (1.0 / math.sqrt(2.0 * math.pi))


VECS = (("ln1g", 0, 1), ("ln1b", 1, 1), ("projb", 2, 1), ("ln2g", 3, 1), ("ln2b", 4, 1), ("fc2b", 5, 1), ("qvb", 6, 2), ("fc1b", 8, 4))
ROW = {name: i for i, (name, _, _) in enumerate(VECS)}
PACK = 12
PACK_ROWS = 16


def expand_vectors(small_buf, vec, count, width):
    unit = width // count
    total = PACK * unit
    pieces = small_buf[...].astype(F32).reshape(count, PACK_ROWS, total)
    pieces = jnp.sum(pieces, axis=1).astype(BF)
    for row, (_, start, times) in enumerate(VECS):
        per = unit * times
        shift = per.bit_length() - 1
        for lo in range(0, width * times, width):
            index = lax.broadcasted_iota(jnp.int32, (total, width), 1) + lo
            source = lax.broadcasted_iota(jnp.int32, (total, width), 0) - start * unit
            pick = ((index & (per - 1)) == source).astype(F32).astype(BF)
            spread = nn(pieces, pick)
            owner = lax.shift_right_logical(lax.broadcasted_iota(jnp.int32, (count, width), 1) + lo, shift)
            mine = owner == lax.broadcasted_iota(jnp.int32, (count, width), 0)
            vec[row : row + 1, lo : lo + width] = jnp.sum(jnp.where(mine, spread, 0.0), axis=0, keepdims=True)


class Sizes:
    def __init__(self, nz, nx, part, width, hidden):
        self.nz, self.nx, self.part, self.width, self.hidden = nz, nx, part, width, hidden
        self.count = nz * 4 * nx
        self.half = part % L
        self.frame = part + self.half
        self.whole = part // L
        self.rows = width // self.count

    def fits(self, sequences):
        paired = self.half * 2 == L and self.half % 32 == 0 and self.part % 32 == 0 and self.nx % 2 == 0
        return sequences == 1 and paired and self.rows % 32 == 0 and self.nz > 1 and self.hidden % self.width == 0


LAG = 3
LATE = (2, 5)
BUDGET = 2.5


def forward_chunks(s):
    step = 512
    narrow = step * s.width // s.hidden
    fat = s.hidden // s.count
    cut = [(0, (0, s.rows), (lo, step)) for lo in range(0, 3 * s.width, step)]
    cut += [(1, (0, s.rows), (lo, step)) for lo in range(0, s.width, step)]
    cut += [(2, (0, s.rows), (lo, step)) for lo in range(0, s.hidden, step)]
    cut += [(3, (0, fat), (lo, narrow)) for lo in range(0, s.width, narrow)]
    return [(*item, i % LATE[1] != LATE[0]) for i, item in enumerate(cut)]


def forward_copies(s):
    total = sum(gather_count(s.nz, s.nx, early) for *_, early in forward_chunks(s))
    return total + (s.nz - 1) + (s.nx - 1) + 1 + 1 + 1


def attend(s, steps, k0, q0, row0, count, image, qkv, valid, attn, p_slot, p_out, p_sem):
    width = s.width
    low = lax.broadcasted_iota(jnp.int32, (1, LANES), 1) < HEAD_DIM
    zero = jnp.zeros((), BF)
    keep = valid[pl.ds(image, 1), :] > 0

    def out_copy(step, slot):
        return pltpu.make_async_copy(
            p_slot.at[slot, :, pl.ds(0, count), :],
            p_out.at[pl.ds(step * 4, 4), pl.ds(row0, count), :],
            p_sem.at[slot],
        )

    def body(step, carry):
        slot = lax.rem(step, 2)

        @pl.when(step >= steps[0] + 2)
        def _():
            out_copy(step - 2, slot).wait()

        for pair in range(2):
            col = pl.multiple_of((step * 2 + pair) * LANES, LANES)
            q2 = qkv[pl.ds(q0, count), pl.ds(col, LANES)]
            k2 = qkv[pl.ds(k0, L), pl.ds(col + width, LANES)]
            v2 = qkv[pl.ds(k0, L), pl.ds(col + 2 * width, LANES)]
            mixed = None
            for head in range(2):
                sel = low if head == 0 else jnp.logical_not(low)
                scores = nt(jnp.where(sel, q2, zero) * BF(HEAD_DIM**-0.5), k2)
                scores = jnp.where(keep, scores, -1e30)
                expo = jnp.exp(scores - jnp.max(scores, axis=-1, keepdims=True))
                probs = (expo * (1.0 / jnp.sum(expo, axis=-1, keepdims=True))).astype(BF)
                p_slot[slot, pair * 2 + head, pl.ds(0, count), :] = probs
                part = nn(probs, jnp.where(sel, v2, zero))
                mixed = part if mixed is None else mixed + part
            attn[pl.ds(row0, count), pl.ds(col, LANES)] = mixed.astype(BF)
        out_copy(step, slot).start()
        return carry

    first, end = steps
    lax.fori_loop(first, end, body, 0)
    for step in (end - 2, end - 1):
        out_copy(step, step % 2).wait()


def forward_kernel(
    s,
    x_ref,
    valid,
    own_valid,
    small_ref,
    wq_ref,
    wp_ref,
    w1_ref,
    w2_ref,
    out_ref,
    n1_out,
    qkv_out,
    attn_out,
    r1_out,
    n2_out,
    act_out,
    slope_out,
    p_out,
    wq_out,
    wp_out,
    w1_out,
    w2_out,
    vec_out,
    wq_buf,
    wp_buf,
    w1_buf,
    w2_buf,
    small_buf,
    vec,
    xf,
    n1f,
    qkvf,
    attn,
    r1,
    n2,
    act,
    slope,
    hidden,
    p_slot,
    send,
    recv,
    local_sem,
    save_sem,
    slope_sem,
    p_sem,
):
    here = Place(s.nz, s.nx)
    sems = Sems(send, recv)
    odd, width, part, half = here.odd, s.width, s.part, s.half
    off = pl.multiple_of(odd * half, 32)
    z, y, c, x = here.z, here.y, here.c, here.x
    srcs = (wq_ref, wp_ref, w1_ref, w2_ref)
    bufs = (wq_buf, wp_buf, w1_buf, w2_buf)
    outs = (wq_out, wp_out, w1_out, w2_out)

    own = [pltpu.make_async_copy(src, buf.at[z, y, c, x], local_sem.at[i]) for i, (src, buf) in enumerate(zip(srcs, bufs))]
    own.append(pltpu.make_async_copy(small_ref, small_buf.at[z, y, c, x], local_sem.at[4]))
    own.append(pltpu.make_async_copy(x_ref, xf.at[pl.ds(off, part), :], local_sem.at[5]))
    for copy in own:
        copy.start()

    chunks = forward_chunks(s)
    plans = [gather_copies(here, sems, srcs[w], bufs[w], rows, cols, early) for w, rows, cols, early in chunks]
    small = small_copies(here, sems, small_ref, small_buf)
    plans[0] = [extra + base for base, extra in zip(plans[0], small)]
    edge_from = pl.multiple_of((part - half) * (1 - odd), 32)
    edge_to = pl.multiple_of(part * odd, 32)
    halo = sems.copy(x_ref.at[pl.ds(edge_from, half), :], xf.at[pl.ds(edge_to, half), :], here.partner())

    saves = []
    slots = iter(range(save_sem.shape[0]))

    def save(src, dst, listed=True):
        copy = pltpu.make_async_copy(src, dst, save_sem.at[next(slots)])
        copy.start()
        if listed:
            saves.append(copy)
        return copy

    here.greet()
    halo.start()
    last = len(chunks)

    starts = [0, LAG, 2 * LAG, 3 * LAG]
    ready = 3 * LAG + 1

    def pump(k):
        j = k - ready
        if 0 <= j < last:
            for copy in plans[j][3]:
                copy.wait_recv()
            w, rows, cols, _ = chunks[j]
            part_of = (slice(None),) * 4 + (pl.ds(*rows), pl.ds(*cols))
            save(bufs[w].at[part_of], outs[w].at[part_of])
        for phase in (3, 2, 1):
            j = k - starts[phase]
            if 0 <= j < last:
                for copy in plans[j][phase - 1]:
                    copy.wait_recv()
                if j == 0 and phase == 1:
                    for copy in own:
                        copy.wait()
                for copy in plans[j][phase]:
                    copy.start()
        if k < last:
            for copy in plans[k][0]:
                copy.start()

    def norm_one():
        expand_vectors(small_buf, vec, s.count, width)
        save(vec, vec_out)
        halo.wait_recv()

        def body(i, carry):
            rows = pl.ds(pl.multiple_of(i * 32, 32), 32)
            unit, _ = norm_stats(xf[rows, :].astype(F32))
            n1f[rows, :] = (unit * vec[ROW["ln1g"] : ROW["ln1g"] + 1, :width] + vec[ROW["ln1b"] : ROW["ln1b"] + 1, :width]).astype(BF)
            return carry

        lax.fori_loop(0, s.frame // 32, body, 0)
        return save(n1f, n1_out, listed=False)

    def project(i):
        third, lo = divmod(i * 512, width)
        got = nn(n1f[...], columns(wq_buf, i * 512, 512))
        if third != 1:
            start = (third // 2) * width + lo
            got = got + vec[ROW["qvb"] : ROW["qvb"] + 1, start : start + 512]
        qkvf[:, i * 512 : i * 512 + 512] = got.astype(BF)

    def whole_image(i, heads):
        k0 = pl.multiple_of((i + odd) * L, 32)
        row0 = pl.multiple_of(i * L + odd * half, 32)
        attend(s, heads, k0, k0, row0, L, i + odd, qkvf, valid, attn, p_slot, p_out, p_sem)

    def edge_image(heads):
        k0 = pl.multiple_of(s.whole * L * (1 - odd), 32)
        q0 = pl.multiple_of(s.whole * L * (1 - odd) + half * odd, 32)
        row0 = pl.multiple_of(s.whole * L * (1 - odd), 32)
        attend(s, heads, k0, q0, row0, half, s.whole * (1 - odd), qkvf, valid, attn, p_slot, p_out, p_sem)

    def output_projection(i):
        lo = i * 512
        got = nn(attn[...], columns(wp_buf, lo, 512)) + vec[ROW["projb"] : ROW["projb"] + 1, lo : lo + 512]
        r1[:, lo : lo + 512] = got + xf[pl.ds(off, part), lo : lo + 512].astype(F32)

    def norm_two():
        save(r1, r1_out)

        def body(i, carry):
            rows = pl.ds(pl.multiple_of(i * 32, 32), 32)
            unit, _ = norm_stats(r1[rows, :])
            n2[rows, :] = (unit * vec[ROW["ln2g"] : ROW["ln2g"] + 1, :width] + vec[ROW["ln2b"] : ROW["ln2b"] + 1, :width]).astype(BF)
            return carry

        lax.fori_loop(0, part // 32, body, 0)
        save(n2, n2_out)

    slope_copies = []

    def up(i):
        slot, at = i % 2, i * 512
        if i >= 2:
            slope_copies[i - 2].wait()
        hidden[...] = nn(n2[...], columns(w1_buf, at, 512)) + vec[ROW["fc1b"] : ROW["fc1b"] + 1, at : at + 512]

        def body(j, carry):
            rows = pl.ds(pl.multiple_of(j * 32, 32), 32)
            value, grade = gelu_pair(hidden[rows, :])
            act[rows, at : at + 512] = value.astype(BF)
            slope[slot, rows, :] = grade.astype(BF)
            return carry

        lax.fori_loop(0, part // 32, body, 0)
        copy = pltpu.make_async_copy(slope.at[slot], slope_out.at[:, pl.ds(at, 512)], slope_sem.at[slot])
        copy.start()
        slope_copies.append(copy)
        save(act.at[:, pl.ds(at, 512)], act_out.at[:, pl.ds(at, 512)])

    narrow = 256
    result = n1f

    def down(i):
        lo = i * narrow
        branch = nn(act[...], columns(w2_buf, lo, narrow)) + vec[ROW["fc2b"] : ROW["fc2b"] + 1, lo : lo + narrow]
        result[pl.ds(0, part), lo : lo + narrow] = (own_valid[...] * (r1[:, lo : lo + narrow] + branch)).astype(BF)

    ends = {}
    for j, (w, _, (lo, n), _) in enumerate(chunks):
        ends[w, lo + n] = j + ready
    kept = {}

    def norm():
        kept["n1"] = norm_one()

    def first_down():
        kept["n1"].wait()
        down(0)

    tasks = [(ready, 4.0, norm)]
    tasks += [(ends[0, (i + 1) * 512], 1.6, functools.partial(project, i)) for i in range(3 * width // 512)]
    steps = HEADS // 4
    halves = ((0, steps // 2), (steps // 2, steps))
    for i in range(s.whole):
        tasks += [(0, 3.5, functools.partial(whole_image, i, heads)) for heads in halves]
    tasks += [(0, 2.9, functools.partial(edge_image, heads)) for heads in halves]
    tasks += [(0, 0.0, lambda: (save(qkvf, qkv_out), save(attn, attn_out)))]
    tasks += [(ends[1, (i + 1) * 512], 1.4, functools.partial(output_projection, i)) for i in range(width // 512)]
    tasks += [(0, 2.5, norm_two)]
    tasks += [(ends[2, (i + 1) * 512], 3.0, functools.partial(up, i)) for i in range(s.hidden // 512)]
    tasks += [(ends[3, (i + 1) * narrow], 2.2, first_down if i == 0 else functools.partial(down, i)) for i in range(width // narrow)]
    for k in range(last + ready):
        pump(k)
        budget = BUDGET
        while tasks and tasks[0][0] <= k and (budget > 0 or k + 1 == last + ready):
            _, cost, task = tasks.pop(0)
            task()
            budget -= cost

    final = pltpu.make_async_copy(result.at[pl.ds(0, part), :], out_ref, local_sem.at[0])
    final.start()
    for copy in slope_copies[-2:]:
        copy.wait()
    for copy in saves:
        copy.wait()
    halo.wait_send()
    for plan in plans:
        for phase in plan:
            for copy in phase:
                copy.wait_send()
    final.wait()


def forward_call(s, x, valid, own_valid, small, wq, wp, w1, w2):
    anyspace = pl.BlockSpec(memory_space=pl.ANY)
    vmem = pl.BlockSpec(memory_space=pltpu.VMEM)
    lead = (s.nz, 2, 2, s.nx)
    shape = lambda dims, kind=BF: jax.ShapeDtypeStruct(dims, kind)
    part, width, hidden, rows = s.part, s.width, s.hidden, s.rows
    fat = hidden // s.count
    gathered = [lead + (rows, 3 * width), lead + (rows, width), lead + (rows, hidden), lead + (fat, width)]
    outs = [
        shape((part, width)),
        shape((s.frame, width)),
        shape((s.frame, 3 * width)),
        shape((part, width)),
        shape((part, width), F32),
        shape((part, width)),
        shape((part, hidden)),
        shape((part, hidden)),
        shape((HEADS, part, L)),
        *[shape(dims) for dims in gathered],
        shape((8, hidden), F32),
    ]
    copies = forward_copies(s)
    scratch = [pltpu.VMEM(dims, BF) for dims in gathered]
    scratch += [
        pltpu.VMEM(lead + (PACK_ROWS, PACK * rows), BF),
        pltpu.VMEM((8, hidden), F32),
        pltpu.VMEM((s.frame, width), BF),
        pltpu.VMEM((s.frame, width), BF),
        pltpu.VMEM((s.frame, 3 * width), BF),
        pltpu.VMEM((part, width), BF),
        pltpu.VMEM((part, width), F32),
        pltpu.VMEM((part, width), BF),
        pltpu.VMEM((part, hidden), BF),
        pltpu.VMEM((2, part, 512), BF),
        pltpu.VMEM((part, 512), F32),
        pltpu.VMEM((2, 4, L, L), BF),
        pltpu.SemaphoreType.DMA((copies,)),
        pltpu.SemaphoreType.DMA((copies,)),
        pltpu.SemaphoreType.DMA((6,)),
        pltpu.SemaphoreType.DMA((len(forward_chunks(s)) + 6 + s.hidden // 512,)),
        pltpu.SemaphoreType.DMA((2,)),
        pltpu.SemaphoreType.DMA((2,)),
    ]
    return pl.pallas_call(
        functools.partial(forward_kernel, s),
        out_shape=outs,
        in_specs=[anyspace, vmem, vmem, anyspace, anyspace, anyspace, anyspace, anyspace],
        out_specs=[anyspace] * len(outs),
        scratch_shapes=scratch,
        name="forward",
        compiler_params=pltpu.CompilerParams(collective_id=0, has_side_effects=True, vmem_limit_bytes=63 * MIB),
    )(x, valid, own_valid, small, wq, wp, w1, w2)


def frames(s, keep_mask):
    images = keep_mask.shape[0]
    x = lax.axis_index("seq")
    odd = lax.rem(x, 2)
    valid = jnp.concatenate([jnp.ones((images, BUF), F32), keep_mask.astype(F32)], axis=1)
    first = lax.div(x * s.part - odd * s.half, L)
    framed = lax.dynamic_slice_in_dim(valid, first, s.whole + 1, 0)
    framed = jnp.pad(framed, ((0, 8 - s.whole - 1), (0, 0)))
    own = lax.dynamic_slice_in_dim(valid.reshape(-1), x * s.part, s.part, 0).reshape(s.part, 1)
    return framed, own


def pack_small(s, ln1_gain, ln1_bias, proj_bias, ln2_gain, ln2_bias, fc2_bias, qv_bias, fc1_bias):
    pieces = (ln1_gain, ln1_bias, proj_bias, ln2_gain, ln2_bias, fc2_bias, qv_bias, fc1_bias)
    total, at, row = PACK * s.rows, 0, 0
    for piece in pieces:
        row = row + jnp.pad(piece[None, :], ((0, PACK_ROWS - 1), (at, total - at - piece.shape[0])))
        at += piece.shape[0]
    return row


class Scatter:
    G_SLOTS = 4
    RING = (5, 6, 4, 4)
    OFFSET = (0, 1, 3, 5, 7)

    def __init__(self, s, here, sems, g, l0, l1a, l1b, l2a, l2b, s2, l3, fin, credit, fin_sem, total):
        self.s, self.here, self.sems, self.total = s, here, sems, total
        self.g, self.l0, self.l1a, self.l1b, self.l2a, self.l2b = g, l0, l1a, l1b, l2a, l2b
        self.s2, self.l3, self.fin, self.credit, self.fin_sem = s2, l3, fin, credit, fin_sem
        nx, nz = s.nx, s.nz
        z, y, c, x = here.z, here.y, here.c, here.x
        self.fore_x, self.fore_z = here.xs(), here.zs()
        self.back_x = [lax.rem(x + nx - d, nx) for d in range(1, nx)]
        self.back_z = [lax.rem(z + nz - d, nz) for d in range(1, nz)]
        self.stage_of = {"c": 0, "1y": 1, "1x": 1, "2x": 2, "2y": 2, "z": 3}
        self.base = {"c": 0, "1y": 1, "1x": 2, "2x": 1 + nx, "2y": 2 * nx, "z": 2 * nx + 1}
        self.sent = {}
        self.out = {}
        self.width = g.shape[-1]
        self.a, self.b = pl.ds(0, self.width // 2), pl.ds(self.width // 2, self.width // 2)

    @staticmethod
    def copies(s):
        return 1 + 1 + (s.nx - 1) + (s.nx - 1) + 1 + (s.nz - 1)

    def take(self, j, key, d=0):
        if j >= self.RING[self.stage_of[key]]:
            pl.semaphore_wait(self.credit.at[self.base[key] + d], 1)

    def give(self, j, key, device, d=0):
        if j + self.RING[self.stage_of[key]] < self.total:
            pl.semaphore_signal(self.credit.at[self.base[key] + d], inc=1, device_id=device, device_id_type=MESH)

    def launch(self, j, stage, copies):
        for copy in copies:
            copy.start()
        self.sent[(j, stage)] = copies

    def landed(self, j, stage):
        for copy in self.sent[(j, stage)]:
            copy.wait_recv()

    def left(self, j, stage):
        for copy in self.sent.pop((j, stage)):
            copy.wait_send()

    def free_g(self, j):
        if j >= self.G_SLOTS:
            self.left(j - self.G_SLOTS, 0)

    def stage0(self, j):
        here, c = self.here, self.here.c
        self.take(j, "c")
        src = self.g.at[j % self.G_SLOTS, :, :, 1 - c]
        self.launch(j, 0, [self.sems.copy(src, self.l0.at[j % self.RING[0]], here.at(c=1 - c))])

    def stage1(self, j):
        here, l0, g = self.here, self.l0, self.g
        y, c, t, t1, u = here.y, here.c, j % self.RING[0], j % self.RING[1], j % self.G_SLOTS
        self.landed(j, 0)

        def body(zz, carry):
            for yy in range(2):
                for xx in range(self.s.nx):
                    l0[t, zz, yy, xx] = l0[t, zz, yy, xx] + g[u, zz, yy, c, xx]
            return carry

        lax.fori_loop(0, self.s.nz, body, 0)
        copies = []
        self.take(j, "1y")
        copies.append(self.sems.copy(l0.at[t, :, 1 - y, :, :, self.a], self.l1a.at[t1], here.at(y=1 - y)))
        for d, peer in enumerate(self.fore_x):
            self.take(j, "1x", d)
            copies.append(self.sems.copy(l0.at[t, :, :, peer, :, self.b], self.l1b.at[t1, d], here.at(x=peer)))
        self.launch(j, 1, copies)

    def stage2(self, j):
        here, l0, l1a, l1b = self.here, self.l0, self.l1a, self.l1b
        y, c, x = here.y, here.c, here.x
        t, t1, t2 = j % self.RING[0], j % self.RING[1], j % self.RING[2]
        self.landed(j, 1)

        def body(zz, carry):
            for xx in range(self.s.nx):
                l1a[t1, zz, xx] = l1a[t1, zz, xx] + l0[t, zz, y, xx, :, self.a]
            for yy in range(2):
                got = l0[t, zz, yy, x, :, self.b].astype(F32)
                for d in range(self.s.nx - 1):
                    got = got + l1b[t1, d, zz, yy].astype(F32)
                l1b[t1, 0, zz, yy] = got.astype(BF)
            return carry

        lax.fori_loop(0, self.s.nz, body, 0)
        copies = []
        for d, peer in enumerate(self.fore_x):
            self.take(j, "2x", d)
            copies.append(self.sems.copy(l1a.at[t1, :, peer], self.l2a.at[t2, d], here.at(x=peer)))
        self.take(j, "2y")
        copies.append(self.sems.copy(l1b.at[t1, 0, :, 1 - y], self.l2b.at[t2], here.at(y=1 - y)))
        self.launch(j, 2, copies)
        self.left(j, 1)
        self.give(j, "c", here.at(c=1 - c))

    def stage3(self, j):
        here, l1a, l1b, l2a, l2b, s2 = self.here, self.l1a, self.l1b, self.l2a, self.l2b, self.s2
        y, x = here.y, here.x
        t, t1, t2 = j % self.RING[3], j % self.RING[1], j % self.RING[2]
        self.landed(j, 2)

        def body(zz, carry):
            got = l1a[t1, zz, x].astype(F32)
            for d in range(self.s.nx - 1):
                got = got + l2a[t2, d, zz].astype(F32)
            s2[t, zz, :, self.a] = got.astype(BF)
            s2[t, zz, :, self.b] = l2b[t2, zz] + l1b[t1, 0, zz, y]
            return carry

        lax.fori_loop(0, self.s.nz, body, 0)
        copies = []
        for d, peer in enumerate(self.fore_z):
            self.take(j, "z", d)
            copies.append(self.sems.copy(s2.at[t, peer], self.l3.at[t, d], here.at(z=peer)))
        self.launch(j, 3, copies)
        self.left(j, 2)
        self.give(j, "1y", here.at(y=1 - y))
        self.give(j, "2y", here.at(y=1 - y))
        for d, peer in enumerate(self.back_x):
            self.give(j, "1x", here.at(x=peer), d)
            self.give(j, "2x", here.at(x=peer), d)

    def stage4(self, j, targets):
        here, s2, l3, fin = self.here, self.s2, self.l3, self.fin
        t, u = j % self.RING[3], j % 2
        self.landed(j, 3)
        for copy in self.out.pop(j - 2, []):
            copy.wait()
        got = s2[t, here.z].astype(F32)
        for d in range(self.s.nz - 1):
            got = got + l3[t, d].astype(F32)
        fin[u] = got
        self.left(j, 3)
        for d, peer in enumerate(self.back_z):
            self.give(j, "z", here.at(z=peer), d)
        copies = [pltpu.make_async_copy(src, dst, self.fin_sem.at[u, i]) for i, (src, dst) in enumerate(targets(fin.at[u]))]
        for copy in copies:
            copy.start()
        self.out[j] = copies

    def finish(self):
        for copies in self.out.values():
            for copy in copies:
                copy.wait()
        for j, stage in sorted(self.sent):
            self.left(j, stage)


def small_scatter_copies(s):
    return 1 + (s.nx - 1) + 1 + (s.nz - 1)


class SmallScatter:
    def __init__(self, s, here, sems, whole, m0, m1, m2, m3):
        self.s, self.here, self.sems = s, here, sems
        self.whole, self.m0, self.m1, self.m2, self.m3 = whole, m0, m1, m2, m3
        self.sent = {}

    def launch(self, stage, copies):
        for copy in copies:
            copy.start()
        self.sent[stage] = copies

    def landed(self, stage):
        for copy in self.sent[stage]:
            copy.wait_recv()

    def stage(self, n, out=None):
        here, s = self.here, self.s
        z, y, c, x = here.z, here.y, here.c, here.x
        whole, m0, m1, m2, m3 = self.whole, self.m0, self.m1, self.m2, self.m3
        if n == 0:
            self.launch(0, [self.sems.copy(whole.at[:, :, 1 - c], m0, here.at(c=1 - c))])
        elif n == 1:
            self.landed(0)
            for zz in range(s.nz):
                for yy in range(2):
                    for xx in range(s.nx):
                        m0[zz, yy, xx] = m0[zz, yy, xx] + whole[zz, yy, c, xx]
            self.launch(1, [self.sems.copy(m0.at[:, :, p], m1.at[d], here.at(x=p)) for d, p in enumerate(here.xs())])
        elif n == 2:
            self.landed(1)
            for zz in range(s.nz):
                for yy in range(2):
                    got = m0[zz, yy, x]
                    for d in range(s.nx - 1):
                        got = got + m1[d, zz, yy]
                    m1[0, zz, yy] = got
            self.launch(2, [self.sems.copy(m1.at[0, :, 1 - y], m2, here.at(y=1 - y))])
        elif n == 3:
            self.landed(2)
            for zz in range(s.nz):
                m2[zz] = m2[zz] + m1[0, zz, y]
            self.launch(3, [self.sems.copy(m2.at[p], m3.at[d], here.at(z=p)) for d, p in enumerate(here.zs())])
        else:
            self.landed(3)
            got = m2[z]
            for d in range(s.nz - 1):
                got = got + m3[d]
            out[...] = got

    def finish(self):
        for copies in self.sent.values():
            for copy in copies:
                copy.wait_send()


def split_three(value):
    high = value.astype(BF)
    rest = value - high.astype(F32)
    middle = rest.astype(BF)
    return high, middle, (rest - middle.astype(F32)).astype(BF)


def pack_vectors(vec, packed, s, late):
    unit = s.width // s.count
    total = PACK * unit
    acc = packed[:, :, :, :, 0, :].reshape(s.count, total) if late else jnp.zeros((s.count, total), F32)
    for row, (name, start, times) in enumerate(VECS):
        if name.startswith("ln1") != late:
            continue
        per = unit * times
        shift = per.bit_length() - 1
        for lo in range(0, s.width * times, s.width):
            index = lax.broadcasted_iota(jnp.int32, (s.width, total), 0) + lo
            target = lax.broadcasted_iota(jnp.int32, (s.width, total), 1) - start * unit
            pick = ((index & (per - 1)) == target).astype(F32).astype(BF)
            owner = lax.shift_right_logical(lax.broadcasted_iota(jnp.int32, (s.count, s.width), 1) + lo, shift)
            mine = owner == lax.broadcasted_iota(jnp.int32, (s.count, s.width), 0)
            spread = jnp.where(mine, vec[row : row + 1, lo : lo + s.width], 0.0)
            parts = jnp.concatenate(split_three(spread), axis=0)
            moved = nn(parts, pick)
            acc = acc + (moved[: s.count] + moved[s.count : 2 * s.count] + moved[2 * s.count :])
    packed[...] = jnp.broadcast_to(acc[:, None, :], (s.count, 8, total)).reshape(s.nz, 2, 2, s.nx, 8, total)


def attend_back(s, span, k0, q0, row0, count, qkv, grad_out, dqkv, p_slot, p_in, p_sem):
    width, frame = s.width, s.frame
    low = lax.broadcasted_iota(jnp.int32, (1, LANES), 1) < HEAD_DIM
    zero = jnp.zeros((), BF)
    first, end = span

    def in_copy(step, slot):
        return pltpu.make_async_copy(
            p_in.at[pl.ds(step * 4, 4), pl.ds(row0, count), :],
            p_slot.at[slot, :, pl.ds(0, count), :],
            p_sem.at[slot],
        )

    in_copy(first, first % 2).start()

    def body(step, carry):
        slot = lax.rem(step, 2)

        @pl.when(step + 1 < end)
        def _():
            in_copy(step + 1, 1 - slot).start()

        in_copy(step, slot).wait()
        for pair in range(2):
            col = pl.multiple_of((step * 2 + pair) * LANES, LANES)
            q2 = qkv[pl.ds(q0, count), pl.ds(col, LANES)]
            k2 = qkv[pl.ds(frame + k0, L), pl.ds(col, LANES)]
            v2 = qkv[pl.ds(2 * frame + k0, L), pl.ds(col, LANES)]
            g2 = grad_out[pl.ds(row0, count), pl.ds(col, LANES)]
            dq = dk = dv = None
            for head in range(2):
                sel = low if head == 0 else jnp.logical_not(low)
                probs = p_slot[slot, pair * 2 + head, pl.ds(0, count), :]
                grad = jnp.where(sel, g2, zero)
                dprobs = nt(grad, v2)
                wide = probs.astype(F32)
                rowdot = jnp.sum(dprobs * wide, axis=-1, keepdims=True)
                dscores = (wide * (dprobs - rowdot)).astype(BF)
                more = (nn(dscores, jnp.where(sel, k2, zero)), tn(dscores, jnp.where(sel, q2, zero)), tn(probs, grad))
                dq, dk, dv = more if dq is None else (dq + more[0], dk + more[1], dv + more[2])
            scale = HEAD_DIM**-0.5
            dqkv[pl.ds(q0, count), pl.ds(col, LANES)] = (dq * scale).astype(BF)
            dqkv[pl.ds(k0, L), pl.ds(col + width, LANES)] = (dk * scale).astype(BF)
            dqkv[pl.ds(k0, L), pl.ds(col + 2 * width, LANES)] = dv.astype(BF)
        return carry

    lax.fori_loop(first, end, body, 0)


def fold_rows(value):
    return jnp.sum(value.reshape(-1, 8, value.shape[-1]), axis=0)


CHUNK = 512
BACK_BUDGET = 3.0


def backward_chunks(s):
    out = [(3, i) for i in range(s.width * (s.hidden // s.width) // CHUNK)]
    out += [(2, i) for i in range(s.hidden // CHUNK)]
    out += [(1, i) for i in range(s.width // CHUNK)]
    out += [(0, i) for i in range(3 * s.width // CHUNK)]
    return out


def backward_copies(s):
    return Scatter.copies(s) * len(backward_chunks(s)) + small_scatter_copies(s) + 1


def backward_kernel(
    s,
    x_ref,
    own_valid,
    cot_ref,
    n1_ref,
    qkv_ref,
    attn_ref,
    r1_ref,
    n2_ref,
    act_ref,
    slope_ref,
    p_ref,
    wq_ref,
    wp_ref,
    w1_ref,
    w2_ref,
    vec,
    out_ref,
    dwq_out,
    dwp_out,
    dw1_out,
    dw2_out,
    small_out,
    buf_a,
    buf_b,
    tall,
    broad,
    wide_a,
    wide_b,
    grad_b,
    mid,
    attn,
    n1f,
    p_slot,
    edge_send,
    edge_in,
    sums,
    packed,
    m0,
    m1,
    m2,
    m3,
    small_fin,
    g,
    l0,
    l1a,
    l1b,
    l2a,
    l2b,
    s2,
    l3,
    fin,
    send,
    recv,
    load_sem,
    p_sem,
    fin_sem,
    credit,
):
    here = Place(s.nz, s.nx)
    sems = Sems(send, recv)
    odd, width, part, half, frame, hidden = here.odd, s.width, s.part, s.half, s.frame, s.hidden
    off = pl.multiple_of(odd * half, 32)
    slots = iter(range(load_sem.shape[0]))

    def load(src, dst):
        copy = pltpu.make_async_copy(src, dst, load_sem.at[next(slots)])
        copy.start()
        return copy

    cot_load = load(cot_ref, grad_b)
    act_load = load(act_ref, buf_a.at[pl.ds(0, part), :])
    pending = {}

    def load_piece(i):
        if i < hidden // 512:
            at = pl.ds(i * 512, 512)
            pending["piece", i] = [load(w2_ref.at[at, :], tall.at[at, :]), load(slope_ref.at[:, at], buf_b.at[:, at])]

    def load_later(i):
        if i == 0:
            pending["n2"] = load(n2_ref, mid)
        elif i <= width // 256:
            at = pl.ds((i - 1) * 256, 256)
            pending["w1", i - 1] = load(w1_ref.at[at, :], broad.at[at, :])
        elif i == width // 256 + 1:
            pending["r1"] = load(r1_ref, wide_a.at[pl.ds(0, part), :])
            pending["attn"] = load(attn_ref, attn)

    for i in range(3):
        load_piece(i)

    chunks = backward_chunks(s)
    total = len(chunks)
    scatter = Scatter(s, here, sems, g, l0, l1a, l1b, l2a, l2b, s2, l3, fin, credit, fin_sem, total)
    small = SmallScatter(s, here, sems, packed, m0, m1, m2, m3)
    here.greet()

    def name(key, value, times=1):
        sums[ROW[key] : ROW[key] + 1, : width * times] = value

    def prepare():
        cot_load.wait()

        def body(i, carry):
            rows = pl.ds(pl.multiple_of(i * 32, 32), 32)
            grad_b[rows, :] = (grad_b[rows, :].astype(F32) * own_valid[rows, :]).astype(BF)
            return carry

        lax.fori_loop(0, part // 32, body, 0)
        act_load.wait()

    ratio = hidden // width
    narrow = CHUNK // ratio
    deep = hidden // s.nz

    def down_grad(i):
        lo = i * narrow

        def body(zz, carry):
            rows = pl.ds(pl.multiple_of(zz * deep, deep), deep)
            got = tn(buf_a[pl.ds(0, part), rows], grad_b[:, lo : lo + 2 * narrow]).astype(BF)
            got = got.reshape(2, 2, s.nx, ratio, s.rows, 2 * narrow)
            for half_of in range(2):
                slot = (i + half_of) % scatter.G_SLOTS
                for q in range(ratio):
                    cut = got[:, :, :, q, :, half_of * narrow : (half_of + 1) * narrow]
                    g[slot, zz, :, :, :, :, q * narrow : (q + 1) * narrow] = cut
            return carry

        lax.fori_loop(0, s.nz, body, 0)

    def grad_tile(lhs, rhs, k):
        got = tn(lhs, rhs).astype(BF)
        g[k % scatter.G_SLOTS] = got.reshape(s.nz, 2, 2, s.nx, s.rows, CHUNK)

    def hidden_grad(i):
        lo = i * 512
        wide_b[:, :512] = nt(grad_b[...], tall[lo : lo + 512, :])

        def body(j, carry):
            rows = pl.ds(pl.multiple_of(j * 32, 32), 32)
            got = wide_b[rows, :512] * buf_b[rows, lo : lo + 512].astype(F32)
            buf_b[rows, lo : lo + 512] = got.astype(BF)
            return carry + fold_rows(got)

        folded = lax.fori_loop(0, part // 32, body, jnp.zeros((8, 512), F32))
        sums[ROW["fc1b"] : ROW["fc1b"] + 1, lo : lo + 512] = jnp.sum(folded, axis=0, keepdims=True)

    def second_norm_product(lo):
        wide_b[:, lo : lo + 256] = nt(buf_b[...], broad[lo : lo + 256, :])

    def second_norm_back():
        ones = jnp.ones((8, part), BF)
        name("fc2b", nn(ones, grad_b[...])[0:1])
        gain = vec[ROW["ln2g"] : ROW["ln2g"] + 1, :width]

        def body(i, carry):
            rows = pl.ds(pl.multiple_of(i * 32, 32), 32)
            unit, inverse = norm_stats(wide_a[rows, :])
            got = wide_b[rows, :]
            u = got * gain
            back = u - jnp.mean(u, axis=-1, keepdims=True) - unit * jnp.mean(u * unit, axis=-1, keepdims=True)
            back = grad_b[rows, :].astype(F32) + inverse * back
            wide_b[rows, :] = back
            n1f[rows, :] = back.astype(BF)
            return carry[0] + fold_rows(got * unit), carry[1] + fold_rows(got), carry[2] + fold_rows(back)

        zeros = jnp.zeros((8, width), F32)
        gain_sum, shift_sum, bias_sum = lax.fori_loop(0, part // 32, body, (zeros, zeros, zeros))
        name("ln2g", jnp.sum(gain_sum, axis=0, keepdims=True))
        name("ln2b", jnp.sum(shift_sum, axis=0, keepdims=True))
        name("projb", jnp.sum(bias_sum, axis=0, keepdims=True))

    def attention_grad():
        for lo in range(0, width, 512):
            grad_b[:, lo : lo + 512] = nt(n1f[:part, :], tall[3 * frame + lo : 3 * frame + lo + 512, :]).astype(BF)

    def first_norm_product(lo):
        got = nt(buf_a[:, : 3 * width], broad[lo : lo + 256, : 3 * width])
        wide_a[:, lo : lo + 256] = got

    def first_norm_back():
        gain = vec[ROW["ln1g"] : ROW["ln1g"] + 1, :width]

        def body(i, carry):
            rows = pl.ds(pl.multiple_of(i * 32, 32), 32)
            framed = pl.ds(pl.multiple_of(i * 32 + off, 32), 32)
            unit, inverse = norm_stats(attn[rows, :].astype(F32))
            got = wide_a[framed, :]
            u = got * gain
            back = u - jnp.mean(u, axis=-1, keepdims=True) - unit * jnp.mean(u * unit, axis=-1, keepdims=True)
            mid[rows, :] = (wide_b[rows, :] + inverse * back).astype(BF)
            return carry[0] + fold_rows(got * unit), carry[1] + fold_rows(got)

        zeros = jnp.zeros((8, width), F32)
        gain_sum, shift_sum = lax.fori_loop(0, part // 32, body, (zeros, zeros))
        name("ln1g", jnp.sum(gain_sum, axis=0, keepdims=True))
        name("ln1b", jnp.sum(shift_sum, axis=0, keepdims=True))

    far = pl.multiple_of(part * (1 - odd), 32)
    near = pl.multiple_of((part - half) * (1 - odd) + half * odd, 32)
    edge = sems.copy(edge_send, edge_in, here.partner())

    def send_edge():
        edge_send[...] = wide_a[pl.ds(far, half), :].astype(BF)
        edge.start()

    def take_edge():
        edge.wait_recv()
        wide_a[pl.ds(near, half), :] = wide_a[pl.ds(near, half), :] + edge_in[...].astype(F32)

    def bias_grad():
        ones = jnp.ones((8, frame), BF)
        for third in (0, 2):
            got = nn(ones, buf_a[:, third * width : (third + 1) * width])[0:1]
            sums[ROW["qvb"] : ROW["qvb"] + 1, (third // 2) * width : (third // 2 + 1) * width] = got

    marks = {"hidden": 0, "mid": False, "attention": False, "out": False}

    def chunk(k):
        w, i = chunks[k]
        if w == 3:
            if i % 2 == 0:
                scatter.free_g(k)
                scatter.free_g(k + 1)
                down_grad(i)
            return
        scatter.free_g(k)
        cols = pl.ds(i * CHUNK, CHUNK)
        if w == 2:
            if i == 0:
                pending["n2"].wait()
            grad_tile(mid[...], buf_b[:, cols], k)
        elif w == 1:
            if i == 0:
                pending["attn"].wait()
            grad_tile(attn[...], n1f[:part, cols], k)
            if i == width // CHUNK - 1:
                pending["x"] = load(x_ref, attn)
                pending["n1"] = load(n1_ref, n1f)
        else:
            if i == 0:
                pending["n1"].wait()
            grad_tile(n1f[...], buf_a[:, cols], k)

    def hidden_task(i):
        for copy in pending["piece", i]:
            copy.wait()
        load_piece(i + 3)
        load_later(i)
        hidden_grad(i)
        marks["hidden"] = i + 1
        if i == hidden // 512 - 1:
            pending["wp"] = load(wp_ref, tall.at[pl.ds(3 * frame, width), :])
            pending["qkv"] = [load(qkv_ref.at[:, pl.ds(t * width, width)], tall.at[pl.ds(t * frame, frame), :]) for t in range(3)]

    def product_task(i):
        pending["w1", i].wait()
        second_norm_product(i * 256)
        if i == width // 256 - 1:
            pending["wq"] = load(wq_ref, broad.at[:, pl.ds(0, 3 * width)])

    def mid_task():
        pending["r1"].wait()
        second_norm_back()
        marks["mid"] = True

    def attention_grad_task():
        pending["wp"].wait()
        attention_grad()
        for copy in pending["qkv"]:
            copy.wait()
        buf_a[pl.ds(far, half), :width] = jnp.zeros((half, width), BF)

    def image_task(i, span):
        k0 = pl.multiple_of((i + odd) * L, 32)
        row0 = pl.multiple_of(i * L + odd * half, 32)
        attend_back(s, span, k0, k0, row0, L, tall, grad_b, buf_a, p_slot, p_ref, p_sem)

    def edge_task(span):
        k0 = pl.multiple_of(s.whole * L * (1 - odd), 32)
        q0 = pl.multiple_of(s.whole * L * (1 - odd) + half * odd, 32)
        attend_back(s, span, k0, q0, k0, half, tall, grad_b, buf_a, p_slot, p_ref, p_sem)
        marks["attention"] = span[1] == HEADS // 4

    def first_product_task(i):
        if i == 0:
            pending["wq"].wait()
        first_norm_product(i * 256)

    def edge_rows_task():
        send_edge()
        bias_grad()
        pack_vectors(sums, packed, s, False)

    def first_task():
        take_edge()
        pending["x"].wait()
        first_norm_back()
        pending["out"] = load(mid, out_ref)

    def pack_task():
        pack_vectors(sums, packed, s, True)
        small.stage(0)
        marks["out"] = True

    downs = sum(w == 3 for w, _ in chunks)
    ups = sum(w == 2 for w, _ in chunks)
    tasks = [(0, 1.8, functools.partial(hidden_task, i)) for i in range(hidden // 512)]
    tasks += [(0, 2.1, functools.partial(product_task, i)) for i in range(width // 256)]
    tasks += [(0, 4.0, mid_task), (downs - 1, 2.5, attention_grad_task)]
    spans = ((0, HEADS // 8), (HEADS // 8, HEADS // 4))
    for i in range(s.whole):
        tasks += [(downs - 1, 4.3, functools.partial(image_task, i, span)) for span in spans]
    tasks += [(downs - 1, 3.7, functools.partial(edge_task, span)) for span in spans]
    tasks += [(0, 1.9, functools.partial(first_product_task, i)) for i in range(width // 256)]
    tasks += [(0, 1.0, edge_rows_task), (downs + ups + width // CHUNK, 3.5, first_task), (0, 1.0, pack_task)]

    def needs(k):
        w, i = chunks[k]
        if w == 3:
            return False
        if w == 2:
            return marks["hidden"] * 512 < (i + 1) * CHUNK
        if w == 1:
            return not marks["mid"]
        return not marks["attention"]

    outs = (dwq_out, dwp_out, dw1_out, dw2_out)

    def targets(j):
        w, i = chunks[j]

        def pairs(slot):
            if w == 3:
                return [
                    (slot.at[:, pl.ds(q * narrow, narrow)], outs[3].at[pl.ds(q * s.rows, s.rows), pl.ds(i * narrow, narrow)])
                    for q in range(ratio)
                ]
            return [(slot, outs[w].at[:, pl.ds(i * CHUNK, CHUNK)])]

        return pairs

    prepare()
    k, small_stage = 0, 0
    stages = (scatter.stage0, scatter.stage1, scatter.stage2, scatter.stage3)
    while k < total + scatter.OFFSET[4] or small_stage < 4:
        j = k - scatter.OFFSET[4]
        if 0 <= j < total:
            scatter.stage4(j, targets(j))
        for n in (3, 2, 1):
            j = k - scatter.OFFSET[n]
            if 0 <= j < total:
                stages[n](j)
        if k < total:
            while needs(k):
                tasks.pop(0)[2]()
            chunk(k)
            scatter.stage0(k)
        if marks["out"] and small_stage < 4:
            small_stage += 1
            small.stage(small_stage, small_fin)
        budget = BACK_BUDGET
        while tasks and budget > 0 and tasks[0][0] <= k:
            _, cost, task = tasks.pop(0)
            task()
            budget -= cost
        k += 1
    final = pltpu.make_async_copy(small_fin, small_out, p_sem.at[0])
    final.start()
    scatter.finish()
    small.finish()
    edge.wait_send()
    pending["out"].wait()
    final.wait()


def backward_call(s, x, own_valid, cot, n1f, qkvf, attn, r1, n2, act, slope, p, wq, wp, w1, w2, vec):
    anyspace = pl.BlockSpec(memory_space=pl.ANY)
    vmem = pl.BlockSpec(memory_space=pltpu.VMEM)
    shape = lambda dims, kind=F32: jax.ShapeDtypeStruct(dims, kind)
    part, width, hidden, rows, nz, nx, frame = s.part, s.width, s.hidden, s.rows, s.nz, s.nx, s.frame
    total = PACK * rows
    outs = [
        shape((part, width), BF),
        shape((rows, 3 * width)),
        shape((rows, width)),
        shape((rows, hidden)),
        shape((hidden // s.count, width)),
        shape((8, total)),
    ]
    copies = backward_copies(s)
    ring = Scatter.RING
    scratch = [
        pltpu.VMEM((frame, hidden), BF),
        pltpu.VMEM((part, hidden), BF),
        pltpu.VMEM((hidden, width), BF),
        pltpu.VMEM((width, hidden), BF),
        pltpu.VMEM((frame, width), F32),
        pltpu.VMEM((part, width), F32),
        pltpu.VMEM((part, width), BF),
        pltpu.VMEM((part, width), BF),
        pltpu.VMEM((part, width), BF),
        pltpu.VMEM((frame, width), BF),
        pltpu.VMEM((2, 4, L, L), BF),
        pltpu.VMEM((s.half, width), BF),
        pltpu.VMEM((s.half, width), BF),
        pltpu.VMEM((8, hidden), F32),
        pltpu.VMEM((nz, 2, 2, nx, 8, total), F32),
        pltpu.VMEM((nz, 2, nx, 8, total), F32),
        pltpu.VMEM((nx - 1, nz, 2, 8, total), F32),
        pltpu.VMEM((nz, 8, total), F32),
        pltpu.VMEM((nz - 1, 8, total), F32),
        pltpu.VMEM((8, total), F32),
        pltpu.VMEM((Scatter.G_SLOTS, nz, 2, 2, nx, rows, CHUNK), BF),
        pltpu.VMEM((ring[0], nz, 2, nx, rows, CHUNK), BF),
        pltpu.VMEM((ring[1], nz, nx, rows, CHUNK // 2), BF),
        pltpu.VMEM((ring[1], nx - 1, nz, 2, rows, CHUNK // 2), BF),
        pltpu.VMEM((ring[2], nx - 1, nz, rows, CHUNK // 2), BF),
        pltpu.VMEM((ring[2], nz, rows, CHUNK // 2), BF),
        pltpu.VMEM((ring[3], nz, rows, CHUNK), BF),
        pltpu.VMEM((ring[3], nz - 1, rows, CHUNK), BF),
        pltpu.VMEM((2, rows, CHUNK), F32),
        pltpu.SemaphoreType.DMA((copies,)),
        pltpu.SemaphoreType.DMA((copies,)),
        pltpu.SemaphoreType.DMA((16 + 2 * (hidden // 512) + width // 256,)),
        pltpu.SemaphoreType.DMA((2,)),
        pltpu.SemaphoreType.DMA((2, hidden // width)),
        pltpu.SemaphoreType.REGULAR((2 * nx + nz,)),
    ]
    return pl.pallas_call(
        functools.partial(backward_kernel, s),
        out_shape=outs,
        in_specs=[anyspace, vmem] + [anyspace] * 13 + [vmem],
        out_specs=[anyspace] * len(outs),
        scratch_shapes=scratch,
        name="backward",
        compiler_params=pltpu.CompilerParams(collective_id=1, has_side_effects=True, vmem_limit_bytes=63 * MIB),
    )(x, own_valid, cot, n1f, qkvf, attn, r1, n2, act, slope, p, wq, wp, w1, w2, vec)


def layer_norm(value, gain, shift):
    mean = jnp.mean(value, axis=-1, keepdims=True)
    centred = value - mean
    inverse = lax.rsqrt(jnp.mean(centred * centred, axis=-1, keepdims=True) + 1e-06)
    unit = centred * inverse
    return (unit * gain + shift, unit, inverse)


def norm_back(grad_out, unit, inverse, gain):
    scaled = grad_out * gain
    grad_in = inverse * (
        scaled
        - jnp.mean(scaled, axis=-1, keepdims=True)
        - unit * jnp.mean(scaled * unit, axis=-1, keepdims=True)
    )
    return (grad_in, jnp.sum(grad_out * unit, axis=0), jnp.sum(grad_out, axis=0))


def split_heads(block, head_count):
    return block.reshape(block.shape[0], block.shape[1], head_count, -1)


def masked_scores(query, keyed, valid, scale):
    scores = jnp.einsum("gqhd,gkhd->ghqk", query, keyed, preferred_element_type=jnp.float32) * scale
    return jnp.where(valid[:, None, None, :] > 0, scores, -1e30)


def plain_shards(
    tokens,
    keep_mask,
    ln1_gain,
    ln1_bias,
    qkv_weight,
    qv_bias,
    proj_weight,
    proj_bias,
    ln2_gain,
    ln2_bias,
    fc1_weight,
    fc1_bias,
    fc2_weight,
    fc2_bias,
    cotangent,
):
    f32 = jnp.float32
    bf16 = jnp.bfloat16
    n_seq = lax.axis_size("seq")
    seq_count, part_len, width = tokens.shape
    seq_len = part_len * n_seq
    img_len = L
    head_local = HEADS // n_seq
    head_width = width // n_seq
    scale = HEAD_DIM ** (-0.5)
    rows = seq_count * part_len
    image_count = keep_mask.shape[0]
    per_group = 1
    pair_count = image_count // per_group
    valid = jnp.concatenate([jnp.ones((image_count, BUF), f32), keep_mask.astype(f32)], axis=1)
    seq_valid = valid.reshape(seq_count, seq_len)
    own_valid = lax.dynamic_slice_in_dim(
        seq_valid, lax.axis_index("seq") * part_len, part_len, 1
    ).reshape(rows, 1)
    valid_pairs = valid.reshape(pair_count, per_group, img_len)
    params = (
        lax.all_gather(ln1_gain, ("fsdp", "seq"), axis=0, tiled=True),
        lax.all_gather(ln1_bias, ("fsdp", "seq"), axis=0, tiled=True),
        lax.all_gather(qkv_weight, ("fsdp", "seq"), axis=0, tiled=True),
        lax.all_gather(qv_bias, ("fsdp", "seq"), axis=0, tiled=True),
        lax.all_gather(proj_weight, ("fsdp", "seq"), axis=0, tiled=True),
        lax.all_gather(proj_bias, ("fsdp", "seq"), axis=0, tiled=True),
        lax.all_gather(ln2_gain, ("fsdp", "seq"), axis=0, tiled=True),
        lax.all_gather(ln2_bias, ("fsdp", "seq"), axis=0, tiled=True),
        lax.all_gather(fc1_weight, ("fsdp", "seq"), axis=0, tiled=True),
        lax.all_gather(fc1_bias, ("fsdp", "seq"), axis=0, tiled=True),
        lax.all_gather(fc2_weight, ("fsdp", "seq"), axis=0, tiled=True),
        lax.all_gather(fc2_bias, ("fsdp", "seq"), axis=0, tiled=True),
    )
    (
        gain_one,
        shift_one,
        w_qkv,
        bias_qv,
        w_proj,
        bias_proj,
        gain_two,
        shift_two,
        w_up,
        bias_up,
        w_down,
        bias_down,
    ) = params
    inputs = tokens.astype(f32).reshape(rows, width)
    normed, unit_one, inv_one = layer_norm(inputs, gain_one.astype(f32), shift_one.astype(f32))
    normed_b = normed.astype(bf16)
    bias_qv = bias_qv.astype(f32)
    full_bias = jnp.concatenate([bias_qv[:width], jnp.zeros((width,), f32), bias_qv[width:]])
    qkv = (jnp.dot(normed_b, w_qkv, preferred_element_type=f32) + full_bias).astype(bf16)
    heads = lax.all_to_all(
        qkv.reshape(seq_count, part_len, 3, width), "seq", split_axis=3, concat_axis=1, tiled=True
    )
    pairs = heads.reshape(pair_count, per_group, img_len, 3, head_width)

    def attend(group):
        block, mask = group
        query = split_heads(block[:, :, 0], head_local)
        keyed = split_heads(block[:, :, 1], head_local)
        values = split_heads(block[:, :, 2], head_local)
        scores = masked_scores(query, keyed, mask, scale)
        top = jnp.max(scores, axis=-1, keepdims=True)
        expo = jnp.exp(scores - top)
        total = jnp.sum(expo, axis=-1, keepdims=True)
        probs = (expo / total).astype(bf16)
        mixed = jnp.einsum("ghqk,gkhd->gqhd", probs, values, preferred_element_type=f32)
        return (
            mixed.reshape(per_group, img_len, head_width).astype(bf16),
            (top + jnp.log(total))[..., 0],
        )

    attn_heads, log_totals = lax.map(attend, (pairs, valid_pairs))
    attn_heads = attn_heads.reshape(seq_count, seq_len, head_width)
    attn_local = lax.all_to_all(attn_heads, "seq", split_axis=1, concat_axis=2, tiled=True).reshape(
        rows, width
    )
    resid = inputs + jnp.dot(attn_local, w_proj, preferred_element_type=f32) + bias_proj.astype(f32)
    normed_two, unit_two, inv_two = layer_norm(resid, gain_two.astype(f32), shift_two.astype(f32))
    normed_two_b = normed_two.astype(bf16)
    hidden = jnp.dot(normed_two_b, w_up, preferred_element_type=f32) + bias_up.astype(f32)
    act, gelu_pull = jax.vjp(lambda value: jax.nn.gelu(value, approximate=False), hidden)
    act_b = act.astype(bf16)
    branch = jnp.dot(act_b, w_down, preferred_element_type=f32) + bias_down.astype(f32)
    layer_out = (own_valid * (resid + branch)).astype(bf16).reshape(seq_count, part_len, width)
    gain_one, w_qkv, w_proj, gain_two, w_up, w_down = (
        lax.all_gather(ln1_gain, ("fsdp", "seq"), axis=0, tiled=True),
        lax.all_gather(qkv_weight, ("fsdp", "seq"), axis=0, tiled=True),
        lax.all_gather(proj_weight, ("fsdp", "seq"), axis=0, tiled=True),
        lax.all_gather(ln2_gain, ("fsdp", "seq"), axis=0, tiled=True),
        lax.all_gather(fc1_weight, ("fsdp", "seq"), axis=0, tiled=True),
        lax.all_gather(fc2_weight, ("fsdp", "seq"), axis=0, tiled=True),
    )
    grad = own_valid * cotangent.astype(f32).reshape(rows, width)
    down_bias_grad = jnp.sum(grad, axis=0)
    grad_b = grad.astype(bf16)
    down_grad = jnp.dot(act_b.T, grad_b, preferred_element_type=f32)
    grad_act = jnp.dot(grad_b, w_down.T, preferred_element_type=f32)
    grad_hidden = gelu_pull(grad_act)[0]
    up_bias_grad = jnp.sum(grad_hidden, axis=0)
    grad_hidden_b = grad_hidden.astype(bf16)
    up_grad = jnp.dot(normed_two_b.T, grad_hidden_b, preferred_element_type=f32)
    grad_normed_two = jnp.dot(grad_hidden_b, w_up.T, preferred_element_type=f32)
    grad_resid_ln, gain_two_grad, shift_two_grad = norm_back(
        grad_normed_two, unit_two, inv_two, gain_two.astype(f32)
    )
    grad_resid = grad + grad_resid_ln
    proj_bias_grad = jnp.sum(grad_resid, axis=0)
    grad_resid_b = grad_resid.astype(bf16)
    proj_grad = jnp.dot(attn_local.T, grad_resid_b, preferred_element_type=f32)
    grad_attn = jnp.dot(grad_resid_b, w_proj.T, preferred_element_type=f32).astype(bf16)
    grad_heads = lax.all_to_all(
        grad_attn.reshape(seq_count, part_len, width),
        "seq",
        split_axis=2,
        concat_axis=1,
        tiled=True,
    )
    grad_pairs = grad_heads.reshape(pair_count, per_group, img_len, head_width)

    def attend_back(group):
        block, mask, lse, grad_mixed = group
        query = split_heads(block[:, :, 0], head_local)
        keyed = split_heads(block[:, :, 1], head_local)
        values = split_heads(block[:, :, 2], head_local)
        grad_out = split_heads(grad_mixed, head_local)
        scores = masked_scores(query, keyed, mask, scale)
        probs = jnp.exp(scores - lse[..., None])
        dprobs = jnp.einsum("gqhd,gkhd->ghqk", grad_out, values, preferred_element_type=f32)
        grad_values = jnp.einsum(
            "ghqk,gqhd->gkhd", probs.astype(bf16), grad_out, preferred_element_type=f32
        )
        rowdot = jnp.sum(dprobs * probs, axis=-1, keepdims=True)
        grad_scores = (probs * (dprobs - rowdot)).astype(bf16)
        grad_query = (
            jnp.einsum("ghqk,gkhd->gqhd", grad_scores, keyed, preferred_element_type=f32) * scale
        )
        grad_keyed = (
            jnp.einsum("ghqk,gqhd->gkhd", grad_scores, query, preferred_element_type=f32) * scale
        )
        stacked = jnp.stack(
            [
                grad_query.reshape(per_group, img_len, head_width),
                grad_keyed.reshape(per_group, img_len, head_width),
                grad_values.reshape(per_group, img_len, head_width),
            ],
            axis=2,
        )
        return stacked.astype(bf16)

    grad_qkv_heads = lax.map(attend_back, (pairs, valid_pairs, log_totals, grad_pairs))
    grad_qkv_heads = grad_qkv_heads.reshape(seq_count, seq_len, 3, head_width)
    grad_qkv = lax.all_to_all(
        grad_qkv_heads, "seq", split_axis=1, concat_axis=3, tiled=True
    ).reshape(rows, 3 * width)
    column_sums = jnp.sum(grad_qkv.astype(f32), axis=0)
    qv_grad = jnp.concatenate([column_sums[:width], column_sums[2 * width :]])
    qkv_grad = jnp.dot(normed_b.T, grad_qkv, preferred_element_type=f32)
    grad_normed = jnp.dot(grad_qkv, w_qkv.T, preferred_element_type=f32)
    grad_in_ln, gain_one_grad, shift_one_grad = norm_back(
        grad_normed, unit_one, inv_one, gain_one.astype(f32)
    )
    tokens_grad = (grad_resid + grad_in_ln).astype(bf16).reshape(seq_count, part_len, width)
    summed = (
        lax.psum_scatter(gain_one_grad, ("fsdp", "seq"), scatter_dimension=0, tiled=True),
        lax.psum_scatter(shift_one_grad, ("fsdp", "seq"), scatter_dimension=0, tiled=True),
        lax.psum_scatter(qkv_grad, ("fsdp", "seq"), scatter_dimension=0, tiled=True),
        lax.psum_scatter(qv_grad, ("fsdp", "seq"), scatter_dimension=0, tiled=True),
        lax.psum_scatter(proj_grad, ("fsdp", "seq"), scatter_dimension=0, tiled=True),
        lax.psum_scatter(proj_bias_grad, ("fsdp", "seq"), scatter_dimension=0, tiled=True),
        lax.psum_scatter(gain_two_grad, ("fsdp", "seq"), scatter_dimension=0, tiled=True),
        lax.psum_scatter(shift_two_grad, ("fsdp", "seq"), scatter_dimension=0, tiled=True),
        lax.psum_scatter(up_grad, ("fsdp", "seq"), scatter_dimension=0, tiled=True),
        lax.psum_scatter(up_bias_grad, ("fsdp", "seq"), scatter_dimension=0, tiled=True),
        lax.psum_scatter(down_grad, ("fsdp", "seq"), scatter_dimension=0, tiled=True),
        lax.psum_scatter(down_bias_grad, ("fsdp", "seq"), scatter_dimension=0, tiled=True),
    )
    return (
        layer_out,
        tokens_grad,
        summed[0],
        summed[1],
        summed[2],
        summed[3],
        summed[4],
        summed[5],
        summed[6],
        summed[7],
        summed[8],
        summed[9],
        summed[10],
        summed[11],
    )


def shards(
    tokens,
    keep_mask,
    ln1_gain,
    ln1_bias,
    qkv_weight,
    qv_bias,
    proj_weight,
    proj_bias,
    ln2_gain,
    ln2_bias,
    fc1_weight,
    fc1_bias,
    fc2_weight,
    fc2_bias,
    cotangent,
):
    n_fsdp, n_seq = lax.axis_size("fsdp"), lax.axis_size("seq")
    s = Sizes(n_fsdp // 4, n_seq, tokens.shape[1], tokens.shape[2], fc1_weight.shape[1])
    if not s.fits(tokens.shape[0]):
        return plain_shards(
            tokens,
            keep_mask,
            ln1_gain,
            ln1_bias,
            qkv_weight,
            qv_bias,
            proj_weight,
            proj_bias,
            ln2_gain,
            ln2_bias,
            fc1_weight,
            fc1_bias,
            fc2_weight,
            fc2_bias,
            cotangent,
        )
    framed, own = frames(s, keep_mask)
    small = pack_small(s, ln1_gain, ln1_bias, proj_bias, ln2_gain, ln2_bias, fc2_bias, qv_bias, fc1_bias)
    x = tokens.reshape(s.part, s.width)
    cot = cotangent.reshape(s.part, s.width)
    out, n1f, qkvf, attn, r1, n2, act, slope, p, wq, wp, w1, w2, vec = forward_call(
        s, x, framed, own, small, qkv_weight, proj_weight, fc1_weight, fc2_weight
    )
    flat = [w.reshape(-1, w.shape[-1]) for w in (wq, wp, w1, w2)]
    back, dwq, dwp, dw1, dw2, vecs = backward_call(s, x, own, cot, n1f, qkvf, attn, r1, n2, act, slope, p, *flat, vec)
    unit = s.rows
    piece = {name: vecs[0, start * unit : (start + times) * unit] for name, start, times in VECS}
    return (
        out.reshape(tokens.shape),
        back.reshape(tokens.shape),
        piece["ln1g"],
        piece["ln1b"],
        dwq,
        piece["qvb"],
        dwp,
        piece["projb"],
        piece["ln2g"],
        piece["ln2b"],
        dw1,
        piece["fc1b"],
        dw2,
        piece["fc2b"],
    )


def solution(mesh):
    rows = P(("fsdp", "seq"))
    weight = P(("fsdp", "seq"), None)
    data = P("fsdp", "seq", None)
    placed = (data, P("fsdp", None), rows, rows, weight, rows, weight, rows, rows, rows, weight, rows, weight, rows, data)
    return jax.shard_map(
        shards,
        mesh=mesh,
        in_specs=placed,
        out_specs=(data, data, rows, rows, weight, rows, weight, rows, rows, rows, weight, rows, weight, rows),
        check_vma=False,
    )
```
